768 devices in a mesh: gx: 12 (over z), gy: 4 (over x), gz: 16 (over y, core).
Axes of the slice: x: 4, y: 8, z: 12, core: 2. Of those that a mesh axis runs over, the one named last changes fastest.
Arguments:
- density: float32 [48, 16, 2048], P('gx', 'gy', 'gz'), may hold values from 0.5 to 2
- velocity: float32 [3, 48, 16, 2048], P(None, 'gx', 'gy', 'gz'), may hold values from -3 to 3
- pressure: float32 [48, 16, 2048], P('gx', 'gy', 'gz'), may hold values from 0.5 to 2
- fine_density: float32 [12, 4, 32, 8, 128], P('gx', 'gy', 'gz'), may hold values from -0.2 to 0.2
- fine_velocity: float32 [3, 12, 4, 32, 8, 128], P(None, 'gx', 'gy', 'gz'), may hold values from -3 to 3
- fine_pressure: float32 [12, 4, 32, 8, 128], P('gx', 'gy', 'gz'), may hold values from -0.2 to 0.2
- box_parent: int32 [12, 4, 32, 1], P('gx', 'gy'), may hold values from 0 to 15; in each aligned block of 2 rows (0 to 1, 2 to 3, ..., all dimensions but the last counted through in order) no two rows name the same one
- box_shift: int32 [12, 4, 32], P('gx', 'gy'), may hold values from 0 to 120
Outputs:
- coarse_state: float32 [5, 48, 16, 2048], P(None, 'gx', 'gy', 'gz')
- fine_state: float32 [5, 12, 4, 32, 8, 128], P(None, 'gx', 'gy', 'gz')
The draws below stay inside these ranges and needn't reach their ends.
Inputs may be any that keep to these rules, and one draw needn't show every extreme that they name: `box_parent`: among the 2 boxes of one owner (one aligned block), no parent is named more than 1 times, and in some blocks one parent is named exactly 1 times.
All inputs are finite; a program needn't handle non-finite values.
Results may differ from the reference program's by a relative error of at most 0.0003.
Values sent between devices are 32-bit elements; how exact they have to be, the bound alone decides.
No kernel may reach another device: no remote copies, remote signals or barrier semaphores. Data moves between devices by JAX's collectives and lax.ppermute only.
A program may use at most 32 MiB of HBM per device.

```python
import math
import jax
import jax.numpy as jnp
import numpy as np
from jax import lax

CX = 4
CY = 4
CZ = 128
FZ = 16
BOX_DEV = 2
FX = 8
FY = 8
CAP = 1
BOXES = 32
NX = 48
NY = 16
NZ = 2048
N_GX = 12
N_GY = 4
N_GZ = 16


def touch_ends(values, stream_key, smallest, high):
    shape = values.shape
    spot = [jax.random.randint(jax.random.fold_in(stream_key, axis), (), 0, shape[axis]) for axis in range(len(shape))]
    values = values.at[tuple(spot)].set(smallest)
    longest = shape.index(max(shape))
    spot[longest] = (spot[longest] + 1) % shape[longest]
    return values.at[tuple(spot)].set(high)


def level_of(key, shape, pieces, low, largest):
    factor_of = 1.0
    for axis_at, blocks in pieces:
        steps = jax.random.uniform(jax.random.fold_in(jax.random.fold_in(key, 6), axis_at), (blocks,), jnp.float32, low / len(pieces), largest / len(pieces))
        factor_of = factor_of * jnp.repeat(jnp.exp(steps), shape[axis_at] // blocks).reshape((-1,) + (1,) * (len(shape) - 1 - axis_at))
    return factor_of


def shared_out(rng, own, number, rows, number_of, top, bound, lean):
    sequence = jax.random.permutation(rng, number_of)
    crowded, ordinary = portions_of(number_of, rows * top, bound, lean, True), portions_of(number_of, rows * top, bound, lean, False)
    places = jnp.arange(number_of)

    def named(lengths, rotation):
        used = int((lengths > 0).sum())
        fixed = max(1, used // 4)
        passed = fixed + (places - fixed + rotation * (used - fixed)) % max(1, number_of - fixed)
        return jnp.zeros((number_of,), jnp.int32).at[sequence[jnp.where(places < fixed, places, passed)]].set(jnp.asarray(lengths, jnp.int32))

    lengths = jnp.where(number % 4 == 0, named(crowded, number // 4), named(ordinary, number - number // 4 - 1))
    mixed = jax.random.permutation(jax.random.fold_in(own, 3), number_of)
    source_of, taker = mixed[0:number_of // 2 * 2:2], mixed[1:number_of // 2 * 2:2]
    room = jnp.minimum(lengths[source_of] - 1, bound - lengths[taker]) // 2
    room = jnp.where((source_of == sequence[0]) | (taker == sequence[0]) | (lengths[taker] == 0), 0, jnp.maximum(room, 0))
    passed = jax.random.randint(jax.random.fold_in(own, 4), (number_of // 2,), 0, 1 << 20) % (room + 1)
    lengths = lengths.at[source_of].add(-passed).at[taker].add(passed)
    members = jnp.searchsorted(jnp.cumsum(lengths), jnp.arange(rows * top), side="right").astype(jnp.int32)
    table = members.reshape(top, rows).T
    table = table[jax.random.permutation(jax.random.fold_in(own, 1), rows)]
    rotation = jax.random.randint(jax.random.fold_in(own, 2), (rows, 1), 0, top)
    return jnp.take_along_axis(table, (jnp.arange(top)[None, :] + rotation) % top, axis=1)


def portions_of(number_of, total, limit, slope, full):
    portions = [(1 << 20) // math.isqrt(rank ** slope) + 1 for rank in range(1, number_of + 1)]
    largest = limit if full else min(limit, max(-(-total // number_of), total * portions[0] // sum(portions)))
    least = 1 if total - largest >= number_of - 1 else 0
    holding, surplus = [largest] + [least] * (number_of - 1), total - largest - least * (number_of - 1)
    while surplus > 0:
        free = [i for i in range(1, number_of) if holding[i] < largest] or [i for i in range(1, number_of) if holding[i] < limit]
        mass, remaining = sum([portions[i] for i in free]), surplus
        for i in free:
            extra = min(limit - holding[i], max(1, remaining * portions[i] // mass), surplus)
            holding[i] = holding[i] + extra
            surplus = surplus - extra
    return np.array(holding)


def centred(key, dims, spread, bound, pieces=(), held_as=jnp.bfloat16):
    loudness = level_of(key, dims, pieces, -0.22, 0.18) if pieces else 1.0
    drawn = jax.random.normal(key, dims, jnp.float32) * spread * loudness
    return jnp.minimum(jnp.maximum(drawn, -bound), bound).astype(held_as)


def setup_inputs(seed: int = 0) -> dict:
    key_of = jax.random.split(jax.random.key(seed), 9)
    density = jnp.clip(0.5 + 1.5 * jax.random.uniform(key_of[0], (NX, NY, NZ), jnp.float32) ** level_of(key_of[0], (NX, NY, NZ), ((0, 12), (1, 4), (2, 16)), -0.2, 0.2), 0.5, 2.0)
    velocity = centred(key_of[1], (3, NX, NY, NZ), 0.3, 3.0, ((1, 12), (2, 4), (3, 16)), jnp.float32)
    pressure = jnp.clip(0.5 + 1.5 * jax.random.uniform(key_of[2], (NX, NY, NZ), jnp.float32) ** level_of(key_of[2], (NX, NY, NZ), ((0, 12), (1, 4), (2, 16)), -0.2, 0.2), 0.5, 2.0)
    fine_density = jnp.clip(jax.random.uniform(key_of[3], (N_GX, N_GY, BOXES, FX, FY * FZ), jnp.float32, -0.2, 0.2) * level_of(key_of[3], (N_GX, N_GY, BOXES, FX, FY * FZ), ((0, 12), (1, 4), (2, 16)), -0.4, 0.0), -0.2, 0.2)
    fine_velocity = centred(key_of[4], (3, N_GX, N_GY, BOXES, FX, FY * FZ), 0.2, 3.0, ((1, 12), (2, 4), (3, 16)), jnp.float32)
    fine_pressure = jnp.clip(jax.random.uniform(key_of[5], (N_GX, N_GY, BOXES, FX, FY * FZ), jnp.float32, -0.2, 0.2) * level_of(key_of[5], (N_GX, N_GY, BOXES, FX, FY * FZ), ((0, 12), (1, 4), (2, 16)), -0.4, 0.0), -0.2, 0.2)
    box_parent_keys = jax.random.split(jax.random.fold_in(key_of[6], 1), N_GX * N_GY * BOXES // BOX_DEV)
    box_parent_turns = jax.random.permutation(jax.random.fold_in(key_of[6], 3), N_GX * N_GY * BOXES // BOX_DEV)
    box_parent = jax.vmap(lambda own, number: shared_out(jax.random.fold_in(key_of[6], 2), own, number, BOX_DEV, N_GZ, 1, CAP, 2))(box_parent_keys, box_parent_turns).reshape((N_GX, N_GY, BOXES, 1))
    box_shift = touch_ends(jax.random.randint(key_of[7], (N_GX, N_GY, BOXES), 0, CZ - FZ // 2 + 1), jax.random.fold_in(key_of[7], 1), 0, (CZ - FZ // 2 + 1) - 1).astype(jnp.int32)
    return dict(density=density, velocity=velocity, pressure=pressure, fine_density=fine_density, fine_velocity=fine_velocity, fine_pressure=fine_pressure, box_parent=box_parent, box_shift=box_shift)


GAMMA = 1.4
DT_COARSE = 0.05
DT_FINE = 0.025

def to_conserved(primitive):
    density = primitive[0]
    speed_x = primitive[1]
    speed_y = primitive[2]
    speed_z = primitive[3]
    energy = primitive[4] / (GAMMA - 1.0) + 0.5 * density * (speed_x * speed_x + speed_y * speed_y + speed_z * speed_z)
    return jnp.stack([density, density * speed_x, density * speed_y, density * speed_z, energy])

def to_primitive(conserved):
    density = conserved[0]
    speed_x = conserved[1] / density
    speed_y = conserved[2] / density
    speed_z = conserved[3] / density
    pressure = (GAMMA - 1.0) * (conserved[4] - 0.5 * (conserved[1] * speed_x + conserved[2] * speed_y + conserved[3] * speed_z))
    return [density, speed_x, speed_y, speed_z, pressure]

def minmod(first, second):
    return 0.5 * (jnp.sign(first) + jnp.sign(second)) * jnp.minimum(jnp.abs(first), jnp.abs(second))

def side_terms(state, normal):
    density, speed_x, speed_y, speed_z, pressure = state
    speeds = [speed_x, speed_y, speed_z]
    normal_speed = speeds[normal]
    energy = pressure / (GAMMA - 1.0) + 0.5 * density * (speed_x * speed_x + speed_y * speed_y + speed_z * speed_z)
    sound = jnp.sqrt(GAMMA * pressure / density)
    conserved = [density, density * speed_x, density * speed_y, density * speed_z, energy]
    fluxes = [item * normal_speed for item in conserved]
    fluxes[1 + normal] = fluxes[1 + normal] + pressure
    fluxes[4] = fluxes[4] + pressure * normal_speed
    return (speeds, normal_speed, energy, sound, conserved, fluxes)

def star_state(state, speeds, normal_speed, energy, wave, contact, normal):
    density = state[0]
    pressure = state[4]
    factor = density * (wave - normal_speed) / (wave - contact)
    parts = [factor]
    for index in range(3):
        parts.append(factor * (contact if index == normal else speeds[index]))
    parts.append(factor * (energy / density + (contact - normal_speed) * (contact + pressure / (density * (wave - normal_speed)))))
    return parts

def hllc_flux(left, right, normal):
    left_speeds, left_normal, left_energy, left_sound, left_state, left_flux = side_terms(left, normal)
    right_speeds, right_normal, right_energy, right_sound, right_state, right_flux = side_terms(right, normal)
    wave_left = jnp.minimum(left_normal - left_sound, right_normal - right_sound)
    wave_right = jnp.maximum(left_normal + left_sound, right_normal + right_sound)
    mass_left = left[0] * (wave_left - left_normal)
    mass_right = right[0] * (wave_right - right_normal)
    contact = (right[4] - left[4] + mass_left * left_normal - mass_right * right_normal) / (mass_left - mass_right)
    star_left = star_state(left, left_speeds, left_normal, left_energy, wave_left, contact, normal)
    star_right = star_state(right, right_speeds, right_normal, right_energy, wave_right, contact, normal)
    result = []
    for index in range(5):
        flux_starl = left_flux[index] + wave_left * (star_left[index] - left_state[index])
        flux_starr = right_flux[index] + wave_right * (star_right[index] - right_state[index])
        value = jnp.where(wave_left >= 0.0, left_flux[index], jnp.where(contact >= 0.0, flux_starl, jnp.where(wave_right >= 0.0, flux_starr, right_flux[index])))
        result.append(value)
    return result

def face_flux(fields, axis, spacing):
    length = fields[0].shape[axis] - 4
    left = []
    right = []
    for field in fields:
        jumps = lax.slice_in_dim(field, 1, length + 4, axis=axis) - lax.slice_in_dim(field, 0, length + 3, axis=axis)
        slopes = minmod(lax.slice_in_dim(jumps, 0, length + 2, axis=axis), lax.slice_in_dim(jumps, 1, length + 3, axis=axis))
        left.append(lax.slice_in_dim(field, 1, length + 2, axis=axis) + 0.5 * lax.slice_in_dim(slopes, 0, length + 1, axis=axis))
        right.append(lax.slice_in_dim(field, 2, length + 3, axis=axis) - 0.5 * lax.slice_in_dim(slopes, 1, length + 2, axis=axis))
    fluxes = hllc_flux(left, right, axis)
    return [(lax.slice_in_dim(flux, 1, length + 1, axis=axis) - lax.slice_in_dim(flux, 0, length, axis=axis)) / spacing for flux in fluxes]

def tendency(padded, spacing):
    fields = to_primitive(padded)
    extent = padded.shape[1:]
    result = None
    for axis in range(3):
        trimmed = []
        for field in fields:
            for other in range(3):
                if other != axis:
                    field = lax.slice_in_dim(field, 2, extent[other] - 2, axis=other)
            trimmed.append(field)
        change = face_flux(trimmed, axis, spacing)
        if result is None:
            result = [-part for part in change]
        else:
            result = [prior - part for prior, part in zip(result, change)]
    return jnp.stack(result)

def inject_fine(window):
    return jnp.repeat(jnp.repeat(jnp.repeat(window, 2, axis=1), 2, axis=2), 2, axis=3)

def fine_substep(state, ghosts):

    def rate(inner):
        return tendency(ghosts.at[:, 2:-2, 2:-2, 2:-2].set(inner), 0.5)
    section = state + DT_FINE * rate(state)
    return 0.5 * state + 0.5 * (section + DT_FINE * rate(section))

def fine_box(old_window, new_window, detail):
    padded = inject_fine(old_window)
    padded = padded.at[:, 2:-2, 2:-2, 2:-2].add(detail)
    first_ghosts = to_conserved(padded)
    state = first_ghosts[:, 2:-2, 2:-2, 2:-2]
    state = fine_substep(state, first_ghosts)
    second_ghosts = inject_fine(0.5 * (to_conserved(old_window) + new_window))
    return fine_substep(state, second_ghosts)

def coarsen_box(state):
    fields, width_x, width_y, width_z = state.shape
    blocks = state.reshape(fields, width_x // 2, 2, width_y // 2, 2, width_z // 2, 2)
    return lax.optimization_barrier(jnp.sum(blocks, axis=(2, 4, 6))) * 0.125

def periodic(field):
    return jnp.pad(field, ((0, 0), (2, 2), (2, 2), (2, 2)), mode='wrap')

def reference(density, velocity, pressure, fine_density, fine_velocity, fine_pressure, box_parent, box_shift):
    primitive = jnp.concatenate([density[None], velocity, pressure[None]])
    start = to_conserved(primitive)
    section = start + DT_COARSE * tendency(periodic(start), 1.0)
    updated = 0.5 * start + 0.5 * (section + DT_COARSE * tendency(periodic(section), 1.0))
    span = FZ // 2
    owners = N_GX * N_GY * N_GZ
    merged = FY * FZ

    def one_owner(owner):
        col_x = owner // (N_GY * N_GZ)
        col_y = owner // N_GZ % N_GY
        first = owner % N_GZ * BOX_DEV
        parents = lax.dynamic_slice(box_parent, (col_x, col_y, first, jnp.int32(0)), (1, 1, BOX_DEV, 1)).reshape(BOX_DEV)
        shifts = lax.dynamic_slice(box_shift, (col_x, col_y, first), (1, 1, BOX_DEV)).reshape(BOX_DEV)
        corner = (parents * CZ + shifts).astype(jnp.int32)
        cols = ((col_x * CX - 1 + jnp.arange(CX + 2, dtype=jnp.int32)) % NX).astype(jnp.int32)
        rows = ((col_y * CY - 1 + jnp.arange(CY + 2, dtype=jnp.int32)) % NY).astype(jnp.int32)
        old_column = jnp.take(jnp.take(primitive, cols, axis=1), rows, axis=2)
        new_column = jnp.take(jnp.take(updated, cols, axis=1), rows, axis=2)

        def window_of(column, base):
            heights = ((base - 1 + jnp.arange(span + 2, dtype=jnp.int32)) % NZ).astype(jnp.int32)
            return jnp.take(column, heights, axis=3)
        old_windows = jax.vmap(lambda base: window_of(old_column, base))(corner)
        new_windows = jax.vmap(lambda base: window_of(new_column, base))(corner)
        zero = jnp.int32(0)
        part_density = lax.dynamic_slice(fine_density, (col_x, col_y, first, zero, zero), (1, 1, BOX_DEV, FX, merged)).reshape(1, BOX_DEV, FX, FY, FZ)
        part_velocity = lax.dynamic_slice(fine_velocity, (zero, col_x, col_y, first, zero, zero), (3, 1, 1, BOX_DEV, FX, merged)).reshape(3, BOX_DEV, FX, FY, FZ)
        part_pressure = lax.dynamic_slice(fine_pressure, (col_x, col_y, first, zero, zero), (1, 1, BOX_DEV, FX, merged)).reshape(1, BOX_DEV, FX, FY, FZ)
        details = jnp.moveaxis(jnp.concatenate([part_density, part_velocity, part_pressure]), 1, 0)
        finals = jax.vmap(fine_box)(old_windows, new_windows, details)
        means = jax.vmap(coarsen_box)(finals)
        return (finals, means, corner)
    finals, means, corners = lax.map(one_owner, jnp.arange(owners, dtype=jnp.int32))
    fine_state = jnp.moveaxis(finals, 2, 0).reshape(5, N_GX, N_GY, N_GZ * BOX_DEV, FX, merged)
    owner_ids = jnp.arange(owners, dtype=jnp.int32)
    owner_x = owner_ids // (N_GY * N_GZ)
    owner_y = owner_ids // N_GZ % N_GY
    index_x = owner_x[:, None, None, None, None] * CX + jnp.arange(CX, dtype=jnp.int32)[None, None, :, None, None]
    index_y = owner_y[:, None, None, None, None] * CY + jnp.arange(CY, dtype=jnp.int32)[None, None, None, :, None]
    index_z = corners[:, :, None, None, None] + jnp.arange(span, dtype=jnp.int32)[None, None, None, None, :]
    shape_all = (owners, BOX_DEV, CX, CY, span)
    index_x = jnp.broadcast_to(index_x, shape_all).astype(jnp.int32)
    index_y = jnp.broadcast_to(index_y, shape_all).astype(jnp.int32)
    index_z = jnp.broadcast_to(index_z, shape_all).astype(jnp.int32)
    summed = jnp.zeros((5, NX, NY, NZ), jnp.float32).at[:, index_x, index_y, index_z].add(jnp.moveaxis(means, 2, 0))
    count = jnp.zeros((NX, NY, NZ), jnp.float32).at[index_x, index_y, index_z].add(1.0)
    coarse_state = jnp.where(count > 0.0, summed / jnp.maximum(count, 1.0), updated)
    return (coarse_state, fine_state)
```

```python
import jax
import jax.numpy as jnp
from jax import lax
from jax.experimental import pallas as pl
from jax.experimental.pallas import tpu as pltpu
from jax.sharding import PartitionSpec as P

F32 = jnp.float32
GROUP = 10
PER_ROW = 12
OLD = 20
TILES = 3


def iota(dim, shape=(8, 128)):
    return lax.broadcasted_iota(jnp.int32, shape, dim)


def roll(value, shift, axis):
    size = value.shape[axis]
    shift = shift % size
    return value if shift == 0 else pltpu.roll(value, shift, axis)


def inverse(value):
    guess = pl.reciprocal(value, approx=True)
    return guess * (2.0 - value * guess)


def root(value):
    return value * lax.rsqrt(jnp.maximum(value, 1e-30))


def conserved(prim):
    rho, u, v, w, p = prim
    return [rho, rho * u, rho * v, rho * w, 2.5 * p + 0.5 * rho * (u * u + v * v + w * w)]


def primitive(cons):
    inv = inverse(cons[0])
    u, v, w = cons[1] * inv, cons[2] * inv, cons[3] * inv
    p = 0.4 * (cons[4] - 0.5 * (cons[1] * u + cons[2] * v + cons[3] * w))
    return [cons[0], u, v, w, p]


def edges(before, here, after):
    down, up = here - before, after - here
    half = 0.5 * (
        jnp.maximum(jnp.minimum(down, up), 0.0) + jnp.minimum(jnp.maximum(down, up), 0.0)
    )
    return here + half, here - half


def hllc(left, right, normal):
    order = [0, 1 + normal] + [1 + d for d in range(3) if d != normal] + [4]
    rho_l, un_l, ut_l, us_l, p_l = [left[k] for k in order]
    rho_r, un_r, ut_r, us_r, p_r = [right[k] for k in order]
    a_l, a_r = p_l * inverse(rho_l), p_r * inverse(rho_r)
    c_l, c_r = root(1.4 * a_l), root(1.4 * a_r)
    s_l = jnp.minimum(un_l - c_l, un_r - c_r)
    s_r = jnp.maximum(un_l + c_l, un_r + c_r)
    m_l, m_r = rho_l * (s_l - un_l), rho_r * (s_r - un_r)
    star = (p_r - p_l + m_l * un_l - m_r * un_r) * inverse(m_l - m_r)
    side = (s_l >= 0.0) | (star >= 0.0)
    pick = lambda one, other: jnp.where(side, one, other)
    rho, un, ut, us, p = (
        pick(rho_l, rho_r),
        pick(un_l, un_r),
        pick(ut_l, ut_r),
        pick(us_l, us_r),
        pick(p_l, p_r),
    )
    a, m, s = pick(a_l, a_r), pick(m_l, m_r), pick(s_l, s_r)
    limited = pick(jnp.minimum(s_l, 0.0), jnp.maximum(s_r, 0.0))
    e = 2.5 * a + 0.5 * (un * un + ut * ut + us * us)
    energy = rho * e
    r = inverse(s - star)
    factor = m * r
    momentum = rho * un
    mass = momentum + limited * (factor - rho)
    force = momentum * un + p + limited * (factor * star - momentum)
    power = (energy + p) * un + limited * (
        factor * e + (star - un) * (factor * star + p * r) - energy
    )
    result = [None] * 5
    for k, part in zip(order, [mass, force, ut * mass, us * mass, power]):
        result[k] = part
    return result


def line_change(fields, axis, normal, wide=None):
    high, low = [], []
    for k in range(5):
        here = fields[k]
        if wide is None:
            after, before = roll(here, -1, axis), roll(here, 1, axis)
        else:
            after, before = roll(wide[k], -1, axis)[0:8], roll(wide[k], 1, axis)[0:8]
        one, other = edges(before, here, after)
        high.append(one)
        low.append(roll(other, -1, axis))
    flux = hllc(high, low, normal)
    return [part - roll(part, 1, axis) for part in flux]


def next_group(tiles, j):
    lane = iota(1, tiles[j][0].shape)
    other = tiles[j + 1] if j + 1 < len(tiles) and tiles[j + 1] is not None else tiles[j]
    return [jnp.where(lane < 96, roll(a, -32, 1), roll(b, -32, 1)) for a, b in zip(tiles[j], other)]


def prior_group(tiles, j):
    lane = iota(1, tiles[j][0].shape)
    other = tiles[j - 1] if j > 0 and tiles[j - 1] is not None else tiles[j]
    return [jnp.where(lane >= 32, roll(a, 32, 1), roll(b, 32, 1)) for a, b in zip(tiles[j], other)]


def group_changes(tiles, wanted):
    high, low, flux = [None] * len(tiles), [None] * len(tiles), [None] * len(tiles)
    for j in wanted:
        pairs = [
            edges(before, here, after)
            for before, here, after in zip(prior_group(tiles, j), tiles[j], next_group(tiles, j))
        ]
        high[j] = [pair[0] for pair in pairs]
        low[j] = [pair[1] for pair in pairs]
    for j in wanted:
        flux[j] = hllc(high[j], next_group(low, j), 0)
    return {
        j: [a - b for a, b in zip(flux[j], prior_group(flux, j))] for j in wanted
    }


def ends_kernel(rho_ref, vel_ref, p_ref, out_ref):
    lane = iota(1, (4, 128))
    for f in range(5):
        total = None
        for x in range(4):
            row = rho_ref[x] if f == 0 else (p_ref[x] if f == 4 else vel_ref[f - 1, x])
            part = lane - 32 * x
            first = roll(row, 32 * x + 8, 1)
            last = roll(row, 32 * x + 24, 1)
            piece = jnp.where(part < 16, first, last)
            total = piece if total is None else jnp.where(part < 0, total, piece)
        out_ref[f] = total


def block_kernel(ends_ref, before_ref, after_ref, rho_ref, vel_ref, p_ref, out_ref, up_ref, down_ref):
    lane = iota(1, (4, 128)) % 32
    for f in range(5):
        edge = jnp.where(
            lane < 8,
            roll(before_ref[f], -16, 1),
            jnp.where(lane >= 24, roll(after_ref[f], 16, 1), ends_ref[f]),
        )
        for copy in range(4):
            out_ref[copy, 20 + f] = edge
        up_ref[5 + f] = edge
        down_ref[5 + f] = edge
        for x in range(4):
            row = rho_ref[x] if f == 0 else (p_ref[x] if f == 4 else vel_ref[f - 1, x])
            for copy in range(4):
                out_ref[copy, 5 * x + f] = row
            if x == 3:
                up_ref[f] = row
            if x == 0:
                down_ref[f] = row


def coarse_kernel(
    place_ref, parent_ref, shift_ref, own_ref, prior_ref, next_ref, far_prior_ref, far_next_ref,
    new_ref, message_ref,
    prim_ref, edge_ref, section_ref, section_edge_ref, made_ref, made_edge_ref,
    old_pack_ref, body_ref, tips_ref,
):
    gy, gz = place_ref[0], place_ref[1]
    for k in range(4):
        source = lax.rem(gy + k, 4)
        for base, ref, tile in ((5, prior_ref, 5), (25, own_ref, 10), (45, next_ref, 15)):
            rows, tips = ref[source, 0:20], ref[source, 20:25]
            if k < 3:
                at = 2 + 4 * k
                prim_ref[base : base + 20, at : at + 4] = rows
                edge_ref[tile : tile + 5, at : at + 4] = tips
            else:
                prim_ref[base : base + 20, 14:16] = rows[:, 0:2]
                prim_ref[base : base + 20, 0:2] = rows[:, 2:4]
                edge_ref[tile : tile + 5, 14:16] = tips[:, 0:2]
                edge_ref[tile : tile + 5, 0:2] = tips[:, 2:4]
    prim_ref[0:5, 2:6] = far_prior_ref[0:5]
    edge_ref[0:5, 2:6] = far_prior_ref[5:10]
    prim_ref[65:70, 2:6] = far_next_ref[0:5]
    edge_ref[20:25, 2:6] = far_next_ref[5:10]

    def prim_row(x):
        return [prim_ref[5 * (x + 5) + f] for f in range(5)]

    def section_row(x, rows=16):
        return [section_ref[5 * (x + 3) + f, 0:rows] for f in range(5)]

    low = flux = high_prior = None
    for x in range(-4, 8):
        here = prim_row(x)
        pairs = [edges(b, h, a) for b, h, a in zip(prim_row(x - 1), here, prim_row(x + 1))]
        low = [pair[1] for pair in pairs]
        if high_prior is not None:
            flux_next = hllc(high_prior, low, 0)
            if flux is not None:
                middle = prim_row(x - 1)
                by_y = line_change(middle, 0, 1)
                by_z = line_change(middle, 1, 2)
                state = conserved(middle)
                section = [
                    state[f] - 0.05 * (flux_next[f] - flux[f] + by_y[f] + by_z[f]) for f in range(5)
                ]
                for f, value in enumerate(primitive(section)):
                    section_ref[5 * (x - 1 + 3) + f] = value
            flux = flux_next
        high_prior = [pair[0] for pair in pairs]
    tiles = [[edge_ref[5 * t + f] for f in range(5)] for t in range(5)]
    by_x = group_changes(tiles, (1, 2, 3))
    for t in (1, 2, 3):
        by_y = line_change(tiles[t], 0, 1)
        by_z = line_change(tiles[t], 1, 2)
        state = conserved(tiles[t])
        section = [state[f] - 0.05 * (by_x[t][f] + by_y[f] + by_z[f]) for f in range(5)]
        for f, value in enumerate(primitive(section)):
            section_edge_ref[5 * (t - 1) + f] = value

    def advance(old, here, changes):
        start, state = conserved(old), conserved(here)
        return [
            0.5 * start[f] + 0.5 * (state[f] - 0.05 * (changes[0][f] + changes[1][f] + changes[2][f]))
            for f in range(5)
        ]

    flux = high_prior = None
    for x in range(-2, 6):
        here = section_row(x, 8)
        pairs = [
            edges(b, h, a) for b, h, a in zip(section_row(x - 1, 8), here, section_row(x + 1, 8))
        ]
        low = [pair[1] for pair in pairs]
        if high_prior is not None:
            flux_next = hllc(high_prior, low, 0)
            if flux is not None:
                middle = section_row(x - 1, 8)
                by_y = line_change(middle, 0, 1, section_row(x - 1))
                by_z = line_change(middle, 1, 2)
                old = [part[0:8] for part in prim_row(x - 1)]
                by_x_row = [b - a for a, b in zip(flux, flux_next)]
                for f, value in enumerate(advance(old, middle, (by_x_row, by_y, by_z))):
                    made_ref[5 * x + f] = value
            flux = flux_next
        high_prior = [pair[0] for pair in pairs]
    wide = [[section_edge_ref[5 * t + f] for f in range(5)] for t in range(3)]
    tiles = [[part[0:8] for part in tile] for tile in wide]
    by_x = group_changes(tiles, (0, 1, 2))
    for t in range(3):
        by_y = line_change(tiles[t], 0, 1, wide[t])
        by_z = line_change(tiles[t], 1, 2)
        old = [edge_ref[5 * (t + 1) + f, 0:8] for f in range(5)]
        for f, value in enumerate(advance(old, tiles[t], (by_x[t], by_y, by_z))):
            made_edge_ref[5 * t + f] = value

    lane, sub = iota(1), iota(0)

    def spot(x):
        return (0, 3) if x < 0 else ((2, 0) if x > 3 else (1, x))

    for f in range(5):
        olds, news = {}, {}
        for x in range(-1, 5):
            tile, group = spot(x)
            main = prim_ref[5 * (x + 5) + f, 0:8]
            tips = edge_ref[5 * (tile + 1) + f, 0:8]
            under, over = roll(tips, -32 * group - 8, 1), roll(tips, 104 - 32 * group, 1)
            olds[x] = (main, jnp.where(lane == 127, under, main), jnp.where(lane == 0, over, main))
            main, tips = made_ref[5 * (x + 1) + f], made_edge_ref[5 * tile + f]
            under, over = roll(tips, -32 * group - 8, 1), roll(tips, 104 - 32 * group, 1)
            main = jnp.where(lane < 4, under, jnp.where(lane >= 124, over, main))
            news[x] = (main, jnp.where(lane == 127, under, main), jnp.where(lane == 0, over, main))
            if 0 <= x < 4:
                new_ref[f, x] = main[2:6]
        inner = (sub >= 2) & (sub < 6)
        for x in range(4):
            face = olds[-1 if x < 2 else 4][0]
            top, bottom = (-2, 4) if x % 2 == 0 else (-4, 2)
            for kind in range(3):
                old_pack_ref[kind, 4 * f + x] = jnp.where(
                    sub == 0,
                    roll(face, top, 0),
                    jnp.where(sub == 7, roll(face, bottom, 0), olds[x][kind]),
                )
        for half, (out, near, far) in enumerate(((-1, 0, 1), (4, 3, 2))):
            body_ref[2 * f + half] = jnp.where(
                inner,
                news[out][0],
                jnp.where(
                    sub == 0,
                    roll(news[far][0], -1, 0),
                    jnp.where(sub == 7, roll(news[far][0], 1, 0), news[near][0]),
                ),
            )
            for kind in range(3):
                tips_ref[kind, 2 * f + half] = jnp.where(
                    inner,
                    news[near][kind],
                    jnp.where(sub < 2, roll(news[far][kind], -2, 0), roll(news[far][kind], 2, 0)),
                )

    def send(owner, carry):
        hit = parent_ref[2 * owner] == gz
        other = parent_ref[2 * owner + 1] == gz
        shift = jnp.where(hit, shift_ref[2 * owner], shift_ref[2 * owner + 1])

        @pl.when(hit | other)
        def _():
            kind = jnp.where(shift == 0, 1, jnp.where(shift == 120, 2, 0))
            for tile in range(TILES):
                total = None
                for j in range(PER_ROW):
                    k = tile * PER_ROW + j
                    if k >= OLD + 10:
                        break
                    amount = lax.rem(GROUP * j + 129 - shift, 128)
                    if k < OLD:
                        piece = pltpu.roll(old_pack_ref[kind, k], amount, 1)
                    else:
                        piece = jnp.where(
                            (lane == GROUP * j) | (lane == GROUP * j + 9),
                            pltpu.roll(tips_ref[kind, k - OLD], amount, 1),
                            pltpu.roll(body_ref[k - OLD], amount, 1),
                        )
                    total = piece if total is None else jnp.where(lane < GROUP * j, total, piece)
                message_ref[owner, tile] = total

        return carry

    lax.fori_loop(0, 16, send, 0)


def fine_kernel(
    place_ref, parent_ref, got_ref, rho_ref, vel_ref, p_ref, out_ref, message_ref, mid_ref, tip_ref
):
    gz = place_ref[1]
    lane, sub = iota(1), iota(0)
    part = lane % 16
    yc, xc = lane // 32, sub // 2
    parents = [parent_ref[2 * gz + box] for box in range(2)]

    for box in range(2):
        for k in range(OLD + 10):
            j = k % PER_ROW
            tile = got_ref[parents[box], k // PER_ROW]
            at = GROUP * j + 1 + part // 2
            mid_ref[box, k] = jnp.take_along_axis(tile, at, axis=1)
            at = GROUP * j + jnp.where(part < 8, 0, 9)
            tip_ref[box, k] = jnp.take_along_axis(tile, at, axis=1)

    def row(ref, box, k, s):
        return jnp.broadcast_to(ref[box, k, s : s + 1, :], (8, 128))

    def by_y(items):
        return jnp.where(
            yc < 2,
            jnp.where(yc == 0, items[0], items[1]),
            jnp.where(yc == 2, items[2], items[3]),
        )

    def by_x(items):
        return jnp.where(
            xc < 2,
            jnp.where(xc == 0, items[0], items[1]),
            jnp.where(xc == 2, items[2], items[3]),
        )

    def inside(box, f):
        return by_x([by_y([row(mid_ref, box, 4 * f + x, 2 + y) for y in range(4)]) for x in range(4)])

    def old_ghosts(box, f):
        low = by_y([row(mid_ref, box, 4 * f + y // 2, 7 * (y % 2)) for y in range(4)])
        high = by_y([row(mid_ref, box, 4 * f + 2 + y // 2, 7 * (y % 2)) for y in range(4)])
        along_x = jnp.where(sub < 4, low, high)
        low = by_x([row(mid_ref, box, 4 * f + x, 1) for x in range(4)])
        high = by_x([row(mid_ref, box, 4 * f + x, 6) for x in range(4)])
        along_y = jnp.where(lane < 64, low, high)
        along_z = by_x(
            [by_y([row(tip_ref, box, 4 * f + x, 2 + y) for y in range(4)]) for x in range(4)]
        )
        return along_x, along_y, along_z

    def new_ghosts(box, f):
        k = OLD + 2 * f
        low = by_y([row(mid_ref, box, k, 2 + y) for y in range(4)])
        high = by_y([row(mid_ref, box, k + 1, 2 + y) for y in range(4)])
        along_x = jnp.where(sub < 4, low, high)
        spots = ((k, 1, 6), (k, 0, 7), (k + 1, 0, 7), (k + 1, 1, 6))
        low = by_x([row(mid_ref, box, at, one) for at, one, _ in spots])
        high = by_x([row(mid_ref, box, at, one) for at, _, one in spots])
        along_y = jnp.where(lane < 64, low, high)
        near, far = (2, 3, 4, 5), (0, 1, 6, 7)
        spots = ((k, near), (k, far), (k + 1, far), (k + 1, near))
        along_z = by_x([by_y([row(tip_ref, box, at, s) for s in rows]) for at, rows in spots])
        return along_x, along_y, along_z

    directions = (
        (0, 1, sub == 0, sub == 7, 4, sub >= 4),
        (1, 16, lane < 16, lane >= 112, 64, lane >= 64),
        (1, 1, part == 0, part == 15, 8, part >= 8),
    )

    def changes(fields, ghosts, bounds):
        total = None
        for normal, (axis, step, first, last, park, parked) in enumerate(directions):
            high, low, up = [[], []], [[], []], [[], []]
            for box in range(2):
                for f in range(5):
                    here, ghost = fields[box][f], ghosts[box][normal][f]
                    after = jnp.where(last, ghost, roll(here, -step, axis))
                    before = jnp.where(first, ghost, roll(here, step, axis))
                    one, other = edges(before, here, after)
                    high[box].append(one)
                    low[box].append(other)
                    up[box].append(jnp.where(last, ghost, roll(other, -step, axis)))
            right = [jnp.where(parked, roll(b, park, axis), a) for a, b in zip(low[0], low[1])]
            bottom = hllc(bounds[normal], right, normal)
            found = []
            for box in range(2):
                flux = hllc(high[box], up[box], normal)
                under = bottom if box == 0 else [roll(item, -park, axis) for item in bottom]
                found.append(
                    [a - jnp.where(first, b, roll(a, step, axis)) for a, b in zip(flux, under)]
                )
            total = (
                found
                if total is None
                else [[a + b for a, b in zip(t, g)] for t, g in zip(total, found)]
            )
        return total

    def lower_bounds(ghosts):
        return [
            [
                jnp.where(parked, roll(ghosts[1][normal][f], park, axis), ghosts[0][normal][f])
                for f in range(5)
            ]
            for normal, (axis, _, _, _, park, parked) in enumerate(directions)
        ]

    def substep(states, fields, ghosts):
        bounds = lower_bounds(ghosts)
        moved = changes(fields, ghosts, bounds)
        section = [[s - 0.05 * m for s, m in zip(states[b], moved[b])] for b in range(2)]
        moved = changes([primitive(item) for item in section], ghosts, bounds)
        return [
            [
                0.5 * s + 0.5 * (t - 0.05 * m)
                for s, t, m in zip(states[b], section[b], moved[b])
            ]
            for b in range(2)
        ]

    ghosts, fields = [], []
    for box in range(2):
        found = [old_ghosts(box, f) for f in range(5)]
        ghosts.append([[found[f][d] for f in range(5)] for d in range(3)])
        details = [rho_ref[box], vel_ref[0, box], vel_ref[1, box], vel_ref[2, box], p_ref[box]]
        fields.append([inside(box, f) + details[f] for f in range(5)])
    states = substep([conserved(item) for item in fields], fields, ghosts)
    later = []
    for box in range(2):
        found = [new_ghosts(box, f) for f in range(5)]
        later.append(
            [
                primitive(
                    [
                        0.5 * (a + b)
                        for a, b in zip(conserved(ghosts[box][d]), [found[f][d] for f in range(5)])
                    ]
                )
                for d in range(3)
            ]
        )
    states = substep(states, [primitive(item) for item in states], later)
    for box in range(2):
        packed = None
        for f in range(5):
            value = states[box][f]
            out_ref[f, box] = value
            value = value + roll(value, -1, 0)
            value = value + roll(value, -1, 1)
            value = (value + roll(value, -16, 1)) * 0.125
            inside_lane = lane % 32
            at = (inside_lane // 8) * 32 + (inside_lane % 8) * 2
            value = jnp.take_along_axis(value, at, axis=1)
            if f == 0:
                packed = value
            elif f < 4:
                packed = jnp.where(lane // 32 == f, value, packed)
            else:
                packed = jnp.where((sub % 2 == 1) & (lane < 32), roll(value, 1, 0), packed)
        message_ref[parents[box]] = packed


def final_kernel(place_ref, parent_ref, shift_ref, new_ref, got_ref, out_ref, sum_ref):
    gz = place_ref[1]
    lane = iota(1)

    def add(owner, carry):
        hit = parent_ref[2 * owner] == gz
        other = parent_ref[2 * owner + 1] == gz
        shift = jnp.where(hit, shift_ref[2 * owner], shift_ref[2 * owner + 1])

        def covered(carry):
            count, sums = carry
            inside = (lane >= shift) & (lane < shift + 8)
            value = got_ref[owner]
            parts = [
                item
                + jnp.where(inside, pltpu.roll(value, lax.rem(shift + 128 - 8 * k, 128), 1), 0.0)
                for k, item in enumerate(sums)
            ]
            return count + jnp.where(inside, 1.0, 0.0), parts

        return lax.cond(hit | other, covered, lambda same: same, carry)

    zero = jnp.zeros((8, 128), F32)
    count, sums = lax.fori_loop(0, 16, add, (zero, [zero] * 16))
    share = inverse(jnp.maximum(count, 1.0))
    for k in range(16):
        sum_ref[8 * k : 8 * k + 8] = sums[k] * share
    for f in range(5):
        for x in range(4):
            start = (0 if f == 4 else 32 * f) + 2 * x + (1 if f == 4 else 0)
            value = sum_ref[pl.ds(start, 4, stride=8)]
            out_ref[f, x] = jnp.where(count[0:4] > 0.0, value, new_ref[f, x])


def shape(*dims):
    return jax.ShapeDtypeStruct(dims, F32)


def call(kernel, outs, scalars, arrays, scratch=()):
    return pl.pallas_call(
        kernel,
        out_shape=outs,
        in_specs=[pl.BlockSpec(memory_space=pltpu.SMEM)] * scalars
        + [pl.BlockSpec(memory_space=pltpu.VMEM)] * arrays,
        out_specs=jax.tree.map(lambda _: pl.BlockSpec(memory_space=pltpu.VMEM), outs),
        scratch_shapes=[pltpu.VMEM(dims, F32) for dims in scratch],
        compiler_params=pltpu.CompilerParams(vmem_limit_bytes=32 * 1024 * 1024),
    )


def shifted(value, axis, step):
    size = lax.axis_size(axis)
    return lax.ppermute(value, axis, [(i, (i + step) % size) for i in range(size)])


def on_device(
    density, velocity, pressure, fine_density, fine_velocity, fine_pressure, box_parent, box_shift
):
    assert density.shape == (4, 4, 128) and fine_density.shape == (1, 1, 2, 8, 128)
    place = jnp.stack([lax.axis_index("gy"), lax.axis_index("gz")]).astype(jnp.int32)
    parents, shifts = box_parent.reshape(32), box_shift.reshape(32)
    ends = call(ends_kernel, shape(5, 4, 128), 0, 3)(density, velocity, pressure)
    before, after = shifted(ends, "gz", 1), shifted(ends, "gz", -1)
    block, for_up, for_down = call(
        block_kernel, (shape(4, 25, 4, 128), shape(10, 4, 128), shape(10, 4, 128)), 0, 6
    )(ends, before, after, density, velocity, pressure)
    far_prior, far_next = shifted(for_up, "gx", 2), shifted(for_down, "gx", -2)
    own = lax.all_to_all(block, "gy", 0, 0, tiled=True)
    prior, following = shifted(own, "gx", 1), shifted(own, "gx", -1)
    updated, message = call(
        coarse_kernel,
        (shape(5, 4, 4, 128), shape(16, TILES, 8, 128)),
        3,
        5,
        (
            (70, 16, 128),
            (25, 16, 128),
            (50, 16, 128),
            (15, 16, 128),
            (30, 8, 128),
            (15, 8, 128),
            (3, 20, 8, 128),
            (10, 8, 128),
            (3, 10, 8, 128),
        ),
    )(place, parents, shifts, own, prior, following, far_prior, far_next)
    got = lax.all_to_all(message, "gz", 0, 0, tiled=True)
    fine, means = call(
        fine_kernel,
        (shape(5, 2, 8, 128), shape(16, 8, 128)),
        2,
        4,
        ((2, 30, 8, 128), (2, 30, 8, 128)),
    )(
        place,
        parents,
        got,
        fine_density.reshape(2, 8, 128),
        fine_velocity.reshape(3, 2, 8, 128),
        fine_pressure.reshape(2, 8, 128),
    )
    incoming = lax.all_to_all(means, "gz", 0, 0, tiled=True)
    coarse = call(final_kernel, shape(5, 4, 4, 128), 3, 2, ((128, 128),))(
        place, parents, shifts, updated, incoming
    )
    return coarse, fine.reshape(5, 1, 1, 2, 8, 128)


def solution(mesh):
    in_specs = (
        P("gx", "gy", "gz"),
        P(None, "gx", "gy", "gz"),
        P("gx", "gy", "gz"),
        P("gx", "gy", "gz", None, None),
        P(None, "gx", "gy", "gz", None, None),
        P("gx", "gy", "gz", None, None),
        P("gx", "gy", None, None),
        P("gx", "gy", None),
    )
    out_specs = (P(None, "gx", "gy", "gz"), P(None, "gx", "gy", "gz", None, None))
    return jax.shard_map(
        on_device, mesh=mesh, in_specs=in_specs, out_specs=out_specs, check_vma=False
    )
```

```python
import jax
import jax.numpy as jnp
from jax import lax
from jax.experimental import pallas as pl
from jax.experimental.pallas import tpu as pltpu
from jax.sharding import PartitionSpec as P

F32 = jnp.float32
GROUP = 10
PER_ROW = 12
OLD = 20
TILES = 3
FIRST, SECOND = 2, 3
SENDS, ADDS = 8, 16


def iota(dim, shape=(8, 128)):
    return lax.broadcasted_iota(jnp.int32, shape, dim)


def roll(value, shift, axis):
    size = value.shape[axis]
    shift = shift % size
    return value if shift == 0 else pltpu.roll(value, shift, axis)


def inverse(value):
    guess = pl.reciprocal(value, approx=True)
    return guess * (2.0 - value * guess)


def root(value):
    return value * lax.rsqrt(jnp.maximum(value, 1e-30))


def conserved(prim):
    rho, u, v, w, p = prim
    return [rho, rho * u, rho * v, rho * w, 2.5 * p + 0.5 * rho * (u * u + v * v + w * w)]


def primitive(cons):
    inv = inverse(cons[0])
    u, v, w = cons[1] * inv, cons[2] * inv, cons[3] * inv
    p = 0.4 * (cons[4] - 0.5 * (cons[1] * u + cons[2] * v + cons[3] * w))
    return [cons[0], u, v, w, p]


def edges(before, here, after):
    down, up = here - before, after - here
    half = 0.5 * (
        jnp.maximum(jnp.minimum(down, up), 0.0) + jnp.minimum(jnp.maximum(down, up), 0.0)
    )
    return here + half, here - half


def hllc(left, right, normal):
    order = [0, 1 + normal] + [1 + d for d in range(3) if d != normal] + [4]
    rho_l, un_l, ut_l, us_l, p_l = [left[k] for k in order]
    rho_r, un_r, ut_r, us_r, p_r = [right[k] for k in order]
    a_l, a_r = p_l * inverse(rho_l), p_r * inverse(rho_r)
    c_l, c_r = root(1.4 * a_l), root(1.4 * a_r)
    s_l = jnp.minimum(un_l - c_l, un_r - c_r)
    s_r = jnp.maximum(un_l + c_l, un_r + c_r)
    m_l, m_r = rho_l * (s_l - un_l), rho_r * (s_r - un_r)
    star = (p_r - p_l + m_l * un_l - m_r * un_r) * inverse(m_l - m_r)
    side = (s_l >= 0.0) | (star >= 0.0)
    pick = lambda one, other: jnp.where(side, one, other)
    rho, un, ut, us, p = (
        pick(rho_l, rho_r),
        pick(un_l, un_r),
        pick(ut_l, ut_r),
        pick(us_l, us_r),
        pick(p_l, p_r),
    )
    a, m, s = pick(a_l, a_r), pick(m_l, m_r), pick(s_l, s_r)
    limited = pick(jnp.minimum(s_l, 0.0), jnp.maximum(s_r, 0.0))
    e = 2.5 * a + 0.5 * (un * un + ut * ut + us * us)
    energy = rho * e
    r = inverse(s - star)
    factor = m * r
    momentum = rho * un
    mass = momentum + limited * (factor - rho)
    force = momentum * un + p + limited * (factor * star - momentum)
    power = (energy + p) * un + limited * (
        factor * e + (star - un) * (factor * star + p * r) - energy
    )
    result = [None] * 5
    for k, part in zip(order, [mass, force, ut * mass, us * mass, power]):
        result[k] = part
    return result


def line_change(fields, axis, normal, wide=None):
    high, low = [], []
    for k in range(5):
        here = fields[k]
        if wide is None:
            after, before = roll(here, -1, axis), roll(here, 1, axis)
        else:
            after, before = roll(wide[k], -1, axis)[0:8], roll(wide[k], 1, axis)[0:8]
        one, other = edges(before, here, after)
        high.append(one)
        low.append(roll(other, -1, axis))
    flux = hllc(high, low, normal)
    return [part - roll(part, 1, axis) for part in flux]


def next_group(tiles, j):
    lane = iota(1, tiles[j][0].shape)
    other = tiles[j + 1] if j + 1 < len(tiles) and tiles[j + 1] is not None else tiles[j]
    return [jnp.where(lane < 96, roll(a, -32, 1), roll(b, -32, 1)) for a, b in zip(tiles[j], other)]


def prior_group(tiles, j):
    lane = iota(1, tiles[j][0].shape)
    other = tiles[j - 1] if j > 0 and tiles[j - 1] is not None else tiles[j]
    return [jnp.where(lane >= 32, roll(a, 32, 1), roll(b, 32, 1)) for a, b in zip(tiles[j], other)]


def group_changes(tiles, wanted):
    high, low, flux = [None] * len(tiles), [None] * len(tiles), [None] * len(tiles)
    for j in wanted:
        pairs = [
            edges(before, here, after)
            for before, here, after in zip(prior_group(tiles, j), tiles[j], next_group(tiles, j))
        ]
        high[j] = [pair[0] for pair in pairs]
        low[j] = [pair[1] for pair in pairs]
    for j in wanted:
        flux[j] = hllc(high[j], next_group(low, j), 0)
    return {
        j: [a - b for a, b in zip(flux[j], prior_group(flux, j))] for j in wanted
    }


def ends_kernel(
    rho_hbm, vel_hbm, p_hbm, parent_hbm, shift_hbm, out_ref, main_ref, parent_ref, shift_ref,
    rho_ref, vel_ref, p_ref, done,
):
    pairs = (
        (rho_hbm, rho_ref),
        (vel_hbm, vel_ref),
        (p_hbm, p_ref),
        (parent_hbm, parent_ref),
        (shift_hbm, shift_ref),
    )
    copies = [pltpu.make_async_copy(a, b, done.at[k]) for k, (a, b) in enumerate(pairs)]
    for copy in copies:
        copy.start()
    for copy in copies:
        copy.wait()
    lane = iota(1, (4, 128))
    for f in range(5):
        total = None
        for x in range(4):
            row = rho_ref[x] if f == 0 else (p_ref[x] if f == 4 else vel_ref[f - 1, x])
            main_ref[5 * x + f] = row
            part = lane - 32 * x
            first = roll(row, 32 * x + 8, 1)
            last = roll(row, 32 * x + 24, 1)
            piece = jnp.where(part < 16, first, last)
            total = piece if total is None else jnp.where(part < 0, total, piece)
        out_ref[f] = total


def block_kernel(ends_ref, before_ref, after_ref, main_ref, out_ref, up_ref, down_ref):
    lane = iota(1, (4, 128)) % 32
    for copy in range(4):
        out_ref[copy, 0:20] = main_ref[...]
    up_ref[0:5] = main_ref[15:20]
    down_ref[0:5] = main_ref[0:5]
    for f in range(5):
        edge = jnp.where(
            lane < 8,
            roll(before_ref[f], -16, 1),
            jnp.where(lane >= 24, roll(after_ref[f], 16, 1), ends_ref[f]),
        )
        for copy in range(4):
            out_ref[copy, 20 + f] = edge
        up_ref[5 + f] = edge
        down_ref[5 + f] = edge


def coarse_kernel(
    place_ref, parent_ref, shift_ref, own_ref, prior_ref, next_ref, far_prior_ref, far_next_ref,
    new_ref, message_ref,
    prim_ref, edge_ref, section_ref, section_edge_ref, made_ref, made_edge_ref,
    old_pack_ref, body_ref, tips_ref,
):
    gy, gz = place_ref[0], place_ref[1]
    for k in range(4):
        source = lax.rem(gy + k, 4)
        for base, ref, tile in ((5, prior_ref, 5), (25, own_ref, 10), (45, next_ref, 15)):
            rows, tips = ref[source, 0:20], ref[source, 20:25]
            if k < 3:
                at = 2 + 4 * k
                prim_ref[base : base + 20, at : at + 4] = rows
                edge_ref[tile : tile + 5, at : at + 4] = tips
            else:
                prim_ref[base : base + 20, 14:16] = rows[:, 0:2]
                prim_ref[base : base + 20, 0:2] = rows[:, 2:4]
                edge_ref[tile : tile + 5, 14:16] = tips[:, 0:2]
                edge_ref[tile : tile + 5, 0:2] = tips[:, 2:4]
    prim_ref[0:5, 2:6] = far_prior_ref[0:5]
    edge_ref[0:5, 2:6] = far_prior_ref[5:10]
    prim_ref[65:70, 2:6] = far_next_ref[0:5]
    edge_ref[20:25, 2:6] = far_next_ref[5:10]

    def prim_row(x):
        return [prim_ref[5 * (x + 5) + f] for f in range(5)]

    def section_row(x, rows=16):
        return [section_ref[5 * (x + 3) + f, 0:rows] for f in range(5)]

    def sweep(row, start, rows, at_once, emit):
        def pairs_of(x):
            found = [edges(b, h, a) for b, h, a in zip(row(x - 1), row(x), row(x + 1))]
            return [pair[0] for pair in found], [pair[1] for pair in found]

        def step(i, carry):
            high, flux = carry
            for k in range(at_once):
                x = start + i * at_once + k
                high_next, low = pairs_of(x + 1)
                flux_next = hllc(high, low, 0)
                emit(x, [after - before for before, after in zip(flux, flux_next)])
                high, flux = high_next, flux_next
            return high, flux

        high_before, _ = pairs_of(start - 1)
        high, low = pairs_of(start)
        lax.fori_loop(0, rows // at_once, step, (high, hllc(high_before, low, 0)))

    def section_of(x, by_x):
        middle = prim_row(x)
        by_y = line_change(middle, 0, 1)
        by_z = line_change(middle, 1, 2)
        state = conserved(middle)
        section = [state[f] - 0.05 * (by_x[f] + by_y[f] + by_z[f]) for f in range(5)]
        for f, value in enumerate(primitive(section)):
            section_ref[5 * (x + 3) + f] = value

    sweep(prim_row, -3, 10, FIRST, section_of)
    tiles = [[edge_ref[5 * t + f] for f in range(5)] for t in range(5)]
    by_x = group_changes(tiles, (1, 2, 3))
    for t in (1, 2, 3):
        by_y = line_change(tiles[t], 0, 1)
        by_z = line_change(tiles[t], 1, 2)
        state = conserved(tiles[t])
        section = [state[f] - 0.05 * (by_x[t][f] + by_y[f] + by_z[f]) for f in range(5)]
        for f, value in enumerate(primitive(section)):
            section_edge_ref[5 * (t - 1) + f] = value

    def advance(old, here, changes):
        start, state = conserved(old), conserved(here)
        return [
            0.5 * start[f] + 0.5 * (state[f] - 0.05 * (changes[0][f] + changes[1][f] + changes[2][f]))
            for f in range(5)
        ]

    def updated_of(x, by_x):
        middle = section_row(x, 8)
        by_y = line_change(middle, 0, 1, section_row(x))
        by_z = line_change(middle, 1, 2)
        old = [part[0:8] for part in prim_row(x)]
        for f, value in enumerate(advance(old, middle, (by_x, by_y, by_z))):
            made_ref[5 * (x + 1) + f] = value

    sweep(lambda x: section_row(x, 8), -1, 6, SECOND, updated_of)
    wide = [[section_edge_ref[5 * t + f] for f in range(5)] for t in range(3)]
    tiles = [[part[0:8] for part in tile] for tile in wide]
    by_x = group_changes(tiles, (0, 1, 2))
    for t in range(3):
        by_y = line_change(tiles[t], 0, 1, wide[t])
        by_z = line_change(tiles[t], 1, 2)
        old = [edge_ref[5 * (t + 1) + f, 0:8] for f in range(5)]
        for f, value in enumerate(advance(old, tiles[t], (by_x[t], by_y, by_z))):
            made_edge_ref[5 * t + f] = value

    lane, sub = iota(1), iota(0)

    def spot(x):
        return (0, 3) if x < 0 else ((2, 0) if x > 3 else (1, x))

    for f in range(5):
        olds, news = {}, {}
        for x in range(-1, 5):
            tile, group = spot(x)
            main = prim_ref[5 * (x + 5) + f, 0:8]
            tips = edge_ref[5 * (tile + 1) + f, 0:8]
            under, over = roll(tips, -32 * group - 8, 1), roll(tips, 104 - 32 * group, 1)
            olds[x] = (main, jnp.where(lane == 127, under, main), jnp.where(lane == 0, over, main))
            main, tips = made_ref[5 * (x + 1) + f], made_edge_ref[5 * tile + f]
            under, over = roll(tips, -32 * group - 8, 1), roll(tips, 104 - 32 * group, 1)
            main = jnp.where(lane < 4, under, jnp.where(lane >= 124, over, main))
            news[x] = (main, jnp.where(lane == 127, under, main), jnp.where(lane == 0, over, main))
            if 0 <= x < 4:
                new_ref[f, x] = main[2:6]
        inner = (sub >= 2) & (sub < 6)
        for x in range(4):
            face = olds[-1 if x < 2 else 4][0]
            top, bottom = (-2, 4) if x % 2 == 0 else (-4, 2)
            for kind in range(3):
                old_pack_ref[kind, 4 * f + x] = jnp.where(
                    sub == 0,
                    roll(face, top, 0),
                    jnp.where(sub == 7, roll(face, bottom, 0), olds[x][kind]),
                )
        for half, (out, near, far) in enumerate(((-1, 0, 1), (4, 3, 2))):
            body_ref[2 * f + half] = jnp.where(
                inner,
                news[out][0],
                jnp.where(
                    sub == 0,
                    roll(news[far][0], -1, 0),
                    jnp.where(sub == 7, roll(news[far][0], 1, 0), news[near][0]),
                ),
            )
            for kind in range(3):
                tips_ref[kind, 2 * f + half] = jnp.where(
                    inner,
                    news[near][kind],
                    jnp.where(sub < 2, roll(news[far][kind], -2, 0), roll(news[far][kind], 2, 0)),
                )

    def send(turn, carry):
        for k_owner in range(SENDS):
            owner = SENDS * turn + k_owner
            hit = parent_ref[2 * owner] == gz
            shift = jnp.where(hit, shift_ref[2 * owner], shift_ref[2 * owner + 1])
            kind = jnp.where(shift == 0, 1, jnp.where(shift == 120, 2, 0))
            for tile in range(TILES):
                total = None
                for j in range(PER_ROW):
                    k = tile * PER_ROW + j
                    if k >= OLD + 10:
                        break
                    amount = lax.rem(GROUP * j + 129 - shift, 128)
                    if k < OLD:
                        piece = pltpu.roll(old_pack_ref[kind, k], amount, 1)
                    else:
                        piece = jnp.where(
                            (lane == GROUP * j) | (lane == GROUP * j + 9),
                            pltpu.roll(tips_ref[kind, k - OLD], amount, 1),
                            pltpu.roll(body_ref[k - OLD], amount, 1),
                        )
                    total = piece if total is None else jnp.where(lane < GROUP * j, total, piece)
                message_ref[owner, tile] = total
        return carry

    lax.fori_loop(0, 16 // SENDS, send, 0)


def fine_kernel(
    place_ref, parent_ref, got_ref, rho_ref, vel_ref, p_ref, out_ref, message_ref,
    mid_ref, tip_ref, ghost_ref, bound_ref,
):
    gz = place_ref[1]
    lane, sub = iota(1), iota(0)
    part = lane % 16
    yc, xc = lane // 32, sub // 2
    parents = [parent_ref[2 * gz + box] for box in range(2)]

    for box in range(2):
        for k in range(OLD + 10):
            j = k % PER_ROW
            tile = got_ref[parents[box], k // PER_ROW]
            at = GROUP * j + 1 + part // 2
            mid_ref[box, 8 * k : 8 * k + 8] = jnp.take_along_axis(tile, at, axis=1)
            at = GROUP * j + jnp.where(part < 8, 0, 9)
            tip_ref[box, 8 * k : 8 * k + 8] = jnp.take_along_axis(tile, at, axis=1)

    def every(ref, box, k, row, step=1):
        return ref[box, pl.ds(8 * k + row, 8, stride=8 * step)]

    def by_y(items):
        return jnp.where(
            yc < 2,
            jnp.where(yc == 0, items[0], items[1]),
            jnp.where(yc == 2, items[2], items[3]),
        )

    def spread(value, rows):
        return jnp.take_along_axis(value, rows, axis=0)

    side, low_y = (sub >= 4).astype(jnp.int32), lane < 64
    outer_x = (xc == 0) | (xc == 3)
    half_x = (xc >= 2).astype(jnp.int32)

    def old_parts(box):
        inside, along_x, along_y, along_z = [], [], [], []
        for f in range(5):
            if f % 2 == 0:
                middle = by_y([every(mid_ref, box, 4 * f, 2 + y) for y in range(4)])
                sides = jnp.where(low_y, every(mid_ref, box, 4 * f, 1), every(mid_ref, box, 4 * f, 6))
                tips = by_y([every(tip_ref, box, 4 * f, 2 + y) for y in range(4)])
            if f % 4 == 0:
                faces = by_y(
                    [every(mid_ref, box, 4 * f + y // 2, 7 * (y % 2), 2) for y in range(4)]
                )
            at = 4 * (f % 2) + xc
            inside.append(spread(middle, at))
            along_y.append(spread(sides, at))
            along_z.append(spread(tips, at))
            along_x.append(spread(faces, 2 * (f % 4) + side))
        return inside, [along_x, along_y, along_z]

    def new_parts(box):
        along_x, along_y, along_z = [], [], []
        for f in range(5):
            if f % 4 == 0:
                k = OLD + 2 * f
                faces = by_y([every(mid_ref, box, k, 2 + y) for y in range(4)])
                sides_near = jnp.where(low_y, every(mid_ref, box, k, 1), every(mid_ref, box, k, 6))
                sides_far = jnp.where(low_y, every(mid_ref, box, k, 0), every(mid_ref, box, k, 7))
                tips_near = by_y([every(tip_ref, box, k, 2 + y) for y in range(4)])
                tips_far = by_y([every(tip_ref, box, k, row) for row in (0, 1, 6, 7)])
            at = 2 * (f % 4) + half_x
            along_x.append(spread(faces, 2 * (f % 4) + side))
            along_y.append(jnp.where(outer_x, spread(sides_near, at), spread(sides_far, at)))
            along_z.append(jnp.where(outer_x, spread(tips_near, at), spread(tips_far, at)))
        return [along_x, along_y, along_z]

    directions = (
        (0, 1, sub == 0, sub == 7, 4, sub >= 4),
        (1, 16, lane < 16, lane >= 112, 64, lane >= 64),
        (1, 1, part == 0, part == 15, 8, part >= 8),
    )

    def changes(fields, step_index):
        total = None
        for normal, (axis, step, first, last, park, parked) in enumerate(directions):
            high, low, up = [[], []], [[], []], [[], []]
            for box in range(2):
                for f in range(5):
                    here, ghost = fields[box][f], ghost_ref[step_index, box, normal, f]
                    after = jnp.where(last, ghost, roll(here, -step, axis))
                    before = jnp.where(first, ghost, roll(here, step, axis))
                    one, other = edges(before, here, after)
                    high[box].append(one)
                    low[box].append(other)
                    up[box].append(jnp.where(last, ghost, roll(other, -step, axis)))
            right = [jnp.where(parked, roll(b, park, axis), a) for a, b in zip(low[0], low[1])]
            bottom = hllc([bound_ref[step_index, normal, f] for f in range(5)], right, normal)
            found = []
            for box in range(2):
                flux = hllc(high[box], up[box], normal)
                under = bottom if box == 0 else [roll(item, -park, axis) for item in bottom]
                found.append(
                    [a - jnp.where(first, b, roll(a, step, axis)) for a, b in zip(flux, under)]
                )
            total = (
                found
                if total is None
                else [[a + b for a, b in zip(t, g)] for t, g in zip(total, found)]
            )
        return total

    def keep(step_index, ghosts):
        for normal, (axis, _, _, _, park, parked) in enumerate(directions):
            for f in range(5):
                for box in range(2):
                    ghost_ref[step_index, box, normal, f] = ghosts[box][normal][f]
                bound_ref[step_index, normal, f] = jnp.where(
                    parked, roll(ghosts[1][normal][f], park, axis), ghosts[0][normal][f]
                )

    ghosts, states, later = [], [], []
    for box in range(2):
        inside, found = old_parts(box)
        ghosts.append(found)
        details = [rho_ref[box], vel_ref[0, box], vel_ref[1, box], vel_ref[2, box], p_ref[box]]
        states.append(conserved([a + b for a, b in zip(inside, details)]))
        later.append(
            [
                primitive([0.5 * (a + b) for a, b in zip(conserved(old), new)])
                for old, new in zip(found, new_parts(box))
            ]
        )
    keep(0, ghosts)
    keep(1, later)

    def stage(i, carry):
        start, state = carry
        again = lax.rem(i, 2) == 1
        weight = jnp.where(again, 0.5, 1.0).astype(F32)
        start = jax.tree.map(lambda a, b: jnp.where(again, a, b), start, state)
        moved = changes([primitive(item) for item in state], i // 2)
        state = jax.tree.map(
            lambda s, t, m: (1.0 - weight) * s + weight * (t - 0.05 * m), start, state, moved
        )
        return start, state

    _, states = lax.fori_loop(0, 4, stage, (states, states), unroll=4)
    for box in range(2):
        packed = None
        for f in range(5):
            value = states[box][f]
            out_ref[f, box] = value
            value = value + roll(value, -1, 0)
            value = value + roll(value, -1, 1)
            value = (value + roll(value, -16, 1)) * 0.125
            inside_lane = lane % 32
            at = (inside_lane // 8) * 32 + (inside_lane % 8) * 2
            value = jnp.take_along_axis(value, at, axis=1)
            if f == 0:
                packed = value
            elif f < 4:
                packed = jnp.where(lane // 32 == f, value, packed)
            else:
                packed = jnp.where((sub % 2 == 1) & (lane < 32), roll(value, 1, 0), packed)
        message_ref[parents[box]] = packed


def final_kernel(place_ref, parent_ref, shift_ref, new_ref, got_ref, out_ref, sum_ref):
    gz = place_ref[1]
    lane = iota(1)

    def add(turn, carry):
        count, sums = carry
        for k_owner in range(ADDS):
            owner = ADDS * turn + k_owner
            hit = parent_ref[2 * owner] == gz
            other = parent_ref[2 * owner + 1] == gz
            shift = jnp.where(hit, shift_ref[2 * owner], shift_ref[2 * owner + 1])
            shift = jnp.where(hit | other, shift, 256)
            inside = (lane >= shift) & (lane < shift + 8)
            value = got_ref[owner]
            count = count + jnp.where(inside, 1.0, 0.0)
            sums = [
                item
                + jnp.where(inside, pltpu.roll(value, lax.rem(shift + 128 - 8 * k, 128), 1), 0.0)
                for k, item in enumerate(sums)
            ]
        return count, sums

    zero = jnp.zeros((8, 128), F32)
    count, sums = lax.fori_loop(0, 16 // ADDS, add, (zero, [zero] * 16))
    share = inverse(jnp.maximum(count, 1.0))
    for k in range(16):
        sum_ref[8 * k : 8 * k + 8] = sums[k] * share
    for f in range(5):
        for x in range(4):
            start = (0 if f == 4 else 32 * f) + 2 * x + (1 if f == 4 else 0)
            value = sum_ref[pl.ds(start, 4, stride=8)]
            out_ref[f, x] = jnp.where(count[0:4] > 0.0, value, new_ref[f, x])


FINE_SCRATCH = ((2, 352, 128), (2, 352, 128), (2, 2, 3, 5, 8, 128), (2, 3, 5, 8, 128))


def shape(*dims):
    return jax.ShapeDtypeStruct(dims, F32)


def call(kernel, outs, scalars, arrays, scratch=()):
    return pl.pallas_call(
        kernel,
        out_shape=outs,
        in_specs=[pl.BlockSpec(memory_space=pltpu.SMEM)] * scalars
        + [pl.BlockSpec(memory_space=pltpu.VMEM)] * arrays,
        out_specs=jax.tree.map(lambda _: pl.BlockSpec(memory_space=pltpu.VMEM), outs),
        scratch_shapes=[pltpu.VMEM(dims, F32) for dims in scratch],
        compiler_params=pltpu.CompilerParams(vmem_limit_bytes=32 * 1024 * 1024),
    )


def shifted(value, axis, step):
    size = lax.axis_size(axis)
    return lax.ppermute(value, axis, [(i, (i + step) % size) for i in range(size)])


def on_device(
    density, velocity, pressure, fine_density, fine_velocity, fine_pressure, box_parent, box_shift
):
    assert density.shape == (4, 4, 128) and fine_density.shape == (1, 1, 2, 8, 128)
    place = jnp.stack([lax.axis_index("gy"), lax.axis_index("gz")]).astype(jnp.int32)
    table = jax.ShapeDtypeStruct((32,), jnp.int32)
    ends, main, parents, shifts = pl.pallas_call(
        ends_kernel,
        out_shape=(shape(5, 4, 128), shape(20, 4, 128), table, table),
        in_specs=[pl.BlockSpec(memory_space=pltpu.HBM)] * 5,
        out_specs=(pl.BlockSpec(memory_space=pltpu.VMEM),) * 4,
        scratch_shapes=[
            pltpu.VMEM((4, 4, 128), F32),
            pltpu.VMEM((3, 4, 4, 128), F32),
            pltpu.VMEM((4, 4, 128), F32),
            pltpu.SemaphoreType.DMA((5,)),
        ],
        compiler_params=pltpu.CompilerParams(vmem_limit_bytes=56 * 1024 * 1024),
    )(density, velocity, pressure, box_parent.reshape(32), box_shift.reshape(32))
    before, after = shifted(ends, "gz", 1), shifted(ends, "gz", -1)
    block, for_up, for_down = call(
        block_kernel, (shape(4, 25, 4, 128), shape(10, 4, 128), shape(10, 4, 128)), 0, 4
    )(ends, before, after, main)
    far_prior, far_next = shifted(for_up, "gx", 2), shifted(for_down, "gx", -2)
    own = lax.all_to_all(block, "gy", 0, 0, tiled=True)
    prior, following = shifted(own, "gx", 1), shifted(own, "gx", -1)
    updated, message = call(
        coarse_kernel,
        (shape(5, 4, 4, 128), shape(16, TILES, 8, 128)),
        3,
        5,
        (
            (70, 16, 128),
            (25, 16, 128),
            (50, 16, 128),
            (15, 16, 128),
            (30, 8, 128),
            (15, 8, 128),
            (3, 20, 8, 128),
            (10, 8, 128),
            (3, 10, 8, 128),
        ),
    )(place, parents, shifts, own, prior, following, far_prior, far_next)
    got = lax.all_to_all(message, "gz", 0, 0, tiled=True)
    fine, means = call(
        fine_kernel,
        (shape(5, 2, 8, 128), shape(16, 8, 128)),
        2,
        4,
        FINE_SCRATCH,
    )(
        place,
        parents,
        got,
        fine_density.reshape(2, 8, 128),
        fine_velocity.reshape(3, 2, 8, 128),
        fine_pressure.reshape(2, 8, 128),
    )
    incoming = lax.all_to_all(means, "gz", 0, 0, tiled=True)
    coarse = call(final_kernel, shape(5, 4, 4, 128), 3, 2, ((128, 128),))(
        place, parents, shifts, updated, incoming
    )
    return coarse, fine.reshape(5, 1, 1, 2, 8, 128)


def solution(mesh):
    in_specs = (
        P("gx", "gy", "gz"),
        P(None, "gx", "gy", "gz"),
        P("gx", "gy", "gz"),
        P("gx", "gy", "gz", None, None),
        P(None, "gx", "gy", "gz", None, None),
        P("gx", "gy", "gz", None, None),
        P("gx", "gy", None, None),
        P("gx", "gy", None),
    )
    out_specs = (P(None, "gx", "gy", "gz"), P(None, "gx", "gy", "gz", None, None))
    return jax.shard_map(
        on_device, mesh=mesh, in_specs=in_specs, out_specs=out_specs, check_vma=False
    )
```

```python
import jax
import jax.numpy as jnp
from jax import lax
from jax.experimental import pallas as pl
from jax.experimental.pallas import tpu as pltpu
from jax.sharding import PartitionSpec as P

F32 = jnp.float32
GROUP = 10
PER_ROW = 12
OLD = 20
TILES = 3
FIRST, SECOND = 2, 3
SENDS, ADDS = 8, 16


def iota(dim, shape=(8, 128)):
    return lax.broadcasted_iota(jnp.int32, shape, dim)


class Table:
    def __init__(self, ref, base):
        self.ref, self.base = ref, base

    def __getitem__(self, k):
        return self.ref[self.base + k]


def roll(value, shift, axis):
    size = value.shape[axis]
    shift = shift % size
    return value if shift == 0 else pltpu.roll(value, shift, axis)


def inverse(value):
    guess = pl.reciprocal(value, approx=True)
    return guess * (2.0 - value * guess)


def root(value):
    return value * lax.rsqrt(jnp.maximum(value, 1e-30))


def conserved(prim):
    rho, u, v, w, p = prim
    return [rho, rho * u, rho * v, rho * w, 2.5 * p + 0.5 * rho * (u * u + v * v + w * w)]


def primitive(cons):
    inv = inverse(cons[0])
    u, v, w = cons[1] * inv, cons[2] * inv, cons[3] * inv
    p = 0.4 * (cons[4] - 0.5 * (cons[1] * u + cons[2] * v + cons[3] * w))
    return [cons[0], u, v, w, p]


def edges(before, here, after):
    down, up = here - before, after - here
    half = 0.5 * (
        jnp.maximum(jnp.minimum(down, up), 0.0) + jnp.minimum(jnp.maximum(down, up), 0.0)
    )
    return here + half, here - half


def hllc(left, right, normal):
    order = [0, 1 + normal] + [1 + d for d in range(3) if d != normal] + [4]
    rho_l, un_l, ut_l, us_l, p_l = [left[k] for k in order]
    rho_r, un_r, ut_r, us_r, p_r = [right[k] for k in order]
    a_l, a_r = p_l * inverse(rho_l), p_r * inverse(rho_r)
    c_l, c_r = root(1.4 * a_l), root(1.4 * a_r)
    s_l = jnp.minimum(un_l - c_l, un_r - c_r)
    s_r = jnp.maximum(un_l + c_l, un_r + c_r)
    m_l, m_r = rho_l * (s_l - un_l), rho_r * (s_r - un_r)
    star = (p_r - p_l + m_l * un_l - m_r * un_r) * inverse(m_l - m_r)
    side = (s_l >= 0.0) | (star >= 0.0)
    pick = lambda one, other: jnp.where(side, one, other)
    rho, un, ut, us, p = (
        pick(rho_l, rho_r),
        pick(un_l, un_r),
        pick(ut_l, ut_r),
        pick(us_l, us_r),
        pick(p_l, p_r),
    )
    a, m, s = pick(a_l, a_r), pick(m_l, m_r), pick(s_l, s_r)
    limited = pick(jnp.minimum(s_l, 0.0), jnp.maximum(s_r, 0.0))
    e = 2.5 * a + 0.5 * (un * un + ut * ut + us * us)
    energy = rho * e
    r = inverse(s - star)
    factor = m * r
    momentum = rho * un
    mass = momentum + limited * (factor - rho)
    force = momentum * un + p + limited * (factor * star - momentum)
    power = (energy + p) * un + limited * (
        factor * e + (star - un) * (factor * star + p * r) - energy
    )
    result = [None] * 5
    for k, part in zip(order, [mass, force, ut * mass, us * mass, power]):
        result[k] = part
    return result


def line_change(fields, axis, normal, wide=None):
    high, low = [], []
    for k in range(5):
        here = fields[k]
        if wide is None:
            after, before = roll(here, -1, axis), roll(here, 1, axis)
        else:
            after, before = roll(wide[k], -1, axis)[0:8], roll(wide[k], 1, axis)[0:8]
        one, other = edges(before, here, after)
        high.append(one)
        low.append(roll(other, -1, axis))
    flux = hllc(high, low, normal)
    return [part - roll(part, 1, axis) for part in flux]


def next_group(tiles, j):
    lane = iota(1, tiles[j][0].shape)
    other = tiles[j + 1] if j + 1 < len(tiles) and tiles[j + 1] is not None else tiles[j]
    return [jnp.where(lane < 96, roll(a, -32, 1), roll(b, -32, 1)) for a, b in zip(tiles[j], other)]


def prior_group(tiles, j):
    lane = iota(1, tiles[j][0].shape)
    other = tiles[j - 1] if j > 0 and tiles[j - 1] is not None else tiles[j]
    return [jnp.where(lane >= 32, roll(a, 32, 1), roll(b, 32, 1)) for a, b in zip(tiles[j], other)]


def group_changes(tiles, wanted):
    high, low, flux = [None] * len(tiles), [None] * len(tiles), [None] * len(tiles)
    for j in wanted:
        pairs = [
            edges(before, here, after)
            for before, here, after in zip(prior_group(tiles, j), tiles[j], next_group(tiles, j))
        ]
        high[j] = [pair[0] for pair in pairs]
        low[j] = [pair[1] for pair in pairs]
    for j in wanted:
        flux[j] = hllc(high[j], next_group(low, j), 0)
    return {
        j: [a - b for a, b in zip(flux[j], prior_group(flux, j))] for j in wanted
    }


def ends_kernel(prim_ref, out_ref, up_ref, down_ref):
    lane = iota(1, (4, 128))
    for f in range(5):
        total = None
        for x in range(4):
            row = prim_ref[f, x]
            part = lane - 32 * x
            first = roll(row, 32 * x + 8, 1)
            last = roll(row, 32 * x + 24, 1)
            piece = jnp.where(part < 16, first, last)
            total = piece if total is None else jnp.where(part < 0, total, piece)
        out_ref[f] = total
        for ref, x in ((up_ref, 3), (down_ref, 0)):
            ref[f] = prim_ref[f, x]
            ref[5 + f] = total


def block_kernel(ends_ref, before_ref, after_ref, prim_ref, _, __, out_ref):
    lane = iota(1, (4, 128)) % 32
    for f in range(5):
        edge = jnp.where(
            lane < 8,
            roll(before_ref[f], -16, 1),
            jnp.where(lane >= 24, roll(after_ref[f], 16, 1), ends_ref[f]),
        )
        for copy in range(4):
            out_ref[copy, 20 + f] = edge
            for x in range(4):
                out_ref[copy, 5 * x + f] = prim_ref[f, x]


def near_kernel(place_ref, own_ref, up_ref, down_ref):
    gy = place_ref[0]
    over, under = lax.rem(gy + 1, 4), lax.rem(gy + 3, 4)
    for ref, xs in ((up_ref, (3, 2, 1, 0)), (down_ref, (0, 1, 2, 3))):

        def take(block, distance):
            start = 5 * xs[distance - 1] if distance else 20
            return own_ref[block, start : start + 5]

        for k, distance in ((0, 1), (9, 0)):
            for j, block in enumerate((gy, over, under)):
                ref[5 * (k + j) : 5 * (k + j) + 5] = take(block, distance)
        for k, distance in ((3, 3), (5, 2), (6, 4)):
            ref[5 * k : 5 * k + 5] = take(gy, distance)
        ref[20:25, 0:2] = take(under, 3)[:, 2:4]
        ref[20:25, 2:4] = take(over, 3)[:, 0:2]
        ref[35:40, 0:3] = take(under, 2)[:, 1:4]
        ref[35:40, 3:4] = take(under, 4)[:, 3:4]
        ref[40:45, 0:3] = take(over, 2)[:, 0:3]
        ref[40:45, 3:4] = take(over, 4)[:, 0:1]


def coarse_kernel(
    place_ref, own_ref, prior_ref, next_ref, far_prior_ref, far_next_ref,
    new_ref, message_ref,
    prim_ref, edge_ref, section_ref, section_edge_ref, made_ref, made_edge_ref,
    old_pack_ref, body_ref, tips_ref,
):
    gy, gz = place_ref[0], place_ref[1]
    parent_ref, shift_ref = Table(place_ref, 2), Table(place_ref, 34)
    for k in range(4):
        source = lax.rem(gy + k, 4)
        rows, tips = own_ref[source, 0:20], own_ref[source, 20:25]
        for ref, base, count, value in ((prim_ref, 25, 20, rows), (edge_ref, 10, 5, tips)):
            if k < 3:
                ref[base : base + count, 2 + 4 * k : 6 + 4 * k] = value
            else:
                ref[base : base + count, 14:16] = value[:, 0:2]
                ref[base : base + count, 0:2] = value[:, 2:4]
    for got_ref, tile, bases in (
        (prior_ref, 5, (20, 15, 10, 5)),
        (next_ref, 15, (45, 50, 55, 60)),
    ):
        got = [got_ref[5 * k : 5 * k + 5] for k in range(12)]
        for ref, base, first in ((prim_ref, bases[0], 0), (edge_ref, tile, 9)):
            ref[base : base + 5, 2:6] = got[first]
            ref[base : base + 5, 6:10] = got[first + 1]
            ref[base : base + 5, 14:16] = got[first + 2][:, 0:2]
            ref[base : base + 5, 0:2] = got[first + 2][:, 2:4]
        for base, first in ((bases[2], 3), (bases[1], 5), (bases[3], 6)):
            prim_ref[base : base + 5, 2:6] = got[first]
        prim_ref[bases[2] : bases[2] + 5, 0:2] = got[4][:, 0:2]
        prim_ref[bases[2] : bases[2] + 5, 6:8] = got[4][:, 2:4]
        prim_ref[bases[1] : bases[1] + 5, 15:16] = got[7][:, 0:1]
        prim_ref[bases[1] : bases[1] + 5, 0:2] = got[7][:, 1:3]
        prim_ref[bases[1] : bases[1] + 5, 6:9] = got[8][:, 0:3]
        prim_ref[bases[3] : bases[3] + 5, 1:2] = got[7][:, 3:4]
        prim_ref[bases[3] : bases[3] + 5, 6:7] = got[8][:, 3:4]
    prim_ref[0:5, 2:6] = far_prior_ref[0:5]
    edge_ref[0:5, 2:6] = far_prior_ref[5:10]
    prim_ref[65:70, 2:6] = far_next_ref[0:5]
    edge_ref[20:25, 2:6] = far_next_ref[5:10]

    def prim_row(x):
        return [prim_ref[5 * (x + 5) + f] for f in range(5)]

    def section_row(x, rows=16):
        return [section_ref[5 * (x + 3) + f, 0:rows] for f in range(5)]

    def sweep(row, start, rows, at_once, emit):
        def pairs_of(x):
            found = [edges(b, h, a) for b, h, a in zip(row(x - 1), row(x), row(x + 1))]
            return [pair[0] for pair in found], [pair[1] for pair in found]

        def step(i, carry):
            high, flux = carry
            for k in range(at_once):
                x = start + i * at_once + k
                high_next, low = pairs_of(x + 1)
                flux_next = hllc(high, low, 0)
                emit(x, [after - before for before, after in zip(flux, flux_next)])
                high, flux = high_next, flux_next
            return high, flux

        high_before, _ = pairs_of(start - 1)
        high, low = pairs_of(start)
        lax.fori_loop(0, rows // at_once, step, (high, hllc(high_before, low, 0)))

    def section_of(x, by_x):
        middle = prim_row(x)
        by_y = line_change(middle, 0, 1)
        by_z = line_change(middle, 1, 2)
        state = conserved(middle)
        section = [state[f] - 0.05 * (by_x[f] + by_y[f] + by_z[f]) for f in range(5)]
        for f, value in enumerate(primitive(section)):
            section_ref[5 * (x + 3) + f] = value

    sweep(prim_row, -3, 10, FIRST, section_of)
    tiles = [[edge_ref[5 * t + f] for f in range(5)] for t in range(5)]
    by_x = group_changes(tiles, (1, 2, 3))
    for t in (1, 2, 3):
        by_y = line_change(tiles[t], 0, 1)
        by_z = line_change(tiles[t], 1, 2)
        state = conserved(tiles[t])
        section = [state[f] - 0.05 * (by_x[t][f] + by_y[f] + by_z[f]) for f in range(5)]
        for f, value in enumerate(primitive(section)):
            section_edge_ref[5 * (t - 1) + f] = value

    def advance(old, here, changes):
        start, state = conserved(old), conserved(here)
        return [
            0.5 * start[f] + 0.5 * (state[f] - 0.05 * (changes[0][f] + changes[1][f] + changes[2][f]))
            for f in range(5)
        ]

    def updated_of(x, by_x):
        middle = section_row(x, 8)
        by_y = line_change(middle, 0, 1, section_row(x))
        by_z = line_change(middle, 1, 2)
        old = [part[0:8] for part in prim_row(x)]
        for f, value in enumerate(advance(old, middle, (by_x, by_y, by_z))):
            made_ref[5 * (x + 1) + f] = value

    sweep(lambda x: section_row(x, 8), -1, 6, SECOND, updated_of)
    wide = [[section_edge_ref[5 * t + f] for f in range(5)] for t in range(3)]
    tiles = [[part[0:8] for part in tile] for tile in wide]
    by_x = group_changes(tiles, (0, 1, 2))
    for t in range(3):
        by_y = line_change(tiles[t], 0, 1, wide[t])
        by_z = line_change(tiles[t], 1, 2)
        old = [edge_ref[5 * (t + 1) + f, 0:8] for f in range(5)]
        for f, value in enumerate(advance(old, tiles[t], (by_x[t], by_y, by_z))):
            made_edge_ref[5 * t + f] = value

    lane, sub = iota(1), iota(0)

    def spot(x):
        return (0, 3) if x < 0 else ((2, 0) if x > 3 else (1, x))

    for f in range(5):
        olds, news = {}, {}
        for x in range(-1, 5):
            tile, group = spot(x)
            main = prim_ref[5 * (x + 5) + f, 0:8]
            tips = edge_ref[5 * (tile + 1) + f, 0:8]
            under, over = roll(tips, -32 * group - 8, 1), roll(tips, 104 - 32 * group, 1)
            olds[x] = (main, jnp.where(lane == 127, under, main), jnp.where(lane == 0, over, main))
            main, tips = made_ref[5 * (x + 1) + f], made_edge_ref[5 * tile + f]
            under, over = roll(tips, -32 * group - 8, 1), roll(tips, 104 - 32 * group, 1)
            main = jnp.where(lane < 4, under, jnp.where(lane >= 124, over, main))
            news[x] = (main, jnp.where(lane == 127, under, main), jnp.where(lane == 0, over, main))
            if 0 <= x < 4:
                new_ref[f, x] = main[2:6]
        inner = (sub >= 2) & (sub < 6)
        for x in range(4):
            face = olds[-1 if x < 2 else 4][0]
            top, bottom = (-2, 4) if x % 2 == 0 else (-4, 2)
            for kind in range(3):
                old_pack_ref[kind, 4 * f + x] = jnp.where(
                    sub == 0,
                    roll(face, top, 0),
                    jnp.where(sub == 7, roll(face, bottom, 0), olds[x][kind]),
                )
        for half, (out, near, far) in enumerate(((-1, 0, 1), (4, 3, 2))):
            body_ref[2 * f + half] = jnp.where(
                inner,
                news[out][0],
                jnp.where(
                    sub == 0,
                    roll(news[far][0], -1, 0),
                    jnp.where(sub == 7, roll(news[far][0], 1, 0), news[near][0]),
                ),
            )
            for kind in range(3):
                tips_ref[kind, 2 * f + half] = jnp.where(
                    inner,
                    news[near][kind],
                    jnp.where(sub < 2, roll(news[far][kind], -2, 0), roll(news[far][kind], 2, 0)),
                )

    def send(turn, carry):
        for k_owner in range(SENDS):
            owner = SENDS * turn + k_owner
            hit = parent_ref[2 * owner] == gz
            shift = jnp.where(hit, shift_ref[2 * owner], shift_ref[2 * owner + 1])
            kind = jnp.where(shift == 0, 1, jnp.where(shift == 120, 2, 0))
            for tile in range(TILES):
                total = None
                for j in range(PER_ROW):
                    k = tile * PER_ROW + j
                    if k >= OLD + 10:
                        break
                    amount = lax.rem(GROUP * j + 129 - shift, 128)
                    if k < OLD:
                        piece = pltpu.roll(old_pack_ref[kind, k], amount, 1)
                    else:
                        piece = jnp.where(
                            (lane == GROUP * j) | (lane == GROUP * j + 9),
                            pltpu.roll(tips_ref[kind, k - OLD], amount, 1),
                            pltpu.roll(body_ref[k - OLD], amount, 1),
                        )
                    total = piece if total is None else jnp.where(lane < GROUP * j, total, piece)
                if tile < TILES - 1:
                    message_ref[owner, 2 * tile] = total[0:4]
                    message_ref[owner, 2 * tile + 1] = total[4:8]
                else:
                    message_ref[owner, 2 * tile] = jnp.where(
                        iota(1, (4, 128)) < 60, total[0:4], roll(total, 60, 1)[4:8]
                    )
        return carry

    lax.fori_loop(0, 16 // SENDS, send, 0)


def fine_kernel(
    place_ref, got_ref, rho_ref, vel_ref, p_ref, out_ref, message_ref,
    mid_ref, tip_ref, ghost_ref, bound_ref,
):
    gz = place_ref[1]
    parent_ref = Table(place_ref, 2)
    lane, sub = iota(1), iota(0)
    part = lane % 16
    yc, xc = lane // 32, sub // 2
    parents = [parent_ref[2 * gz + box] for box in range(2)]

    for box in range(2):
        tiles = [
            jnp.concatenate([got_ref[parents[box], 2 * t], got_ref[parents[box], 2 * t + 1]])
            for t in range(TILES - 1)
        ]
        short = got_ref[parents[box], 2 * TILES - 2]
        tiles.append(jnp.concatenate([short, roll(short, -60, 1)]))
        for k in range(OLD + 10):
            j = k % PER_ROW
            tile = tiles[k // PER_ROW]
            at = GROUP * j + 1 + part // 2
            mid_ref[box, 8 * k : 8 * k + 8] = jnp.take_along_axis(tile, at, axis=1)
            at = GROUP * j + jnp.where(part < 8, 0, 9)
            tip_ref[box, 8 * k : 8 * k + 8] = jnp.take_along_axis(tile, at, axis=1)

    def every(ref, box, k, row, step=1):
        return ref[box, pl.ds(8 * k + row, 8, stride=8 * step)]

    def by_y(items):
        return jnp.where(
            yc < 2,
            jnp.where(yc == 0, items[0], items[1]),
            jnp.where(yc == 2, items[2], items[3]),
        )

    def spread(value, rows):
        return jnp.take_along_axis(value, rows, axis=0)

    side, low_y = (sub >= 4).astype(jnp.int32), lane < 64
    outer_x = (xc == 0) | (xc == 3)
    half_x = (xc >= 2).astype(jnp.int32)

    def old_parts(box):
        inside, along_x, along_y, along_z = [], [], [], []
        for f in range(5):
            if f % 2 == 0:
                middle = by_y([every(mid_ref, box, 4 * f, 2 + y) for y in range(4)])
                sides = jnp.where(low_y, every(mid_ref, box, 4 * f, 1), every(mid_ref, box, 4 * f, 6))
                tips = by_y([every(tip_ref, box, 4 * f, 2 + y) for y in range(4)])
            if f % 4 == 0:
                faces = by_y(
                    [every(mid_ref, box, 4 * f + y // 2, 7 * (y % 2), 2) for y in range(4)]
                )
            at = 4 * (f % 2) + xc
            inside.append(spread(middle, at))
            along_y.append(spread(sides, at))
            along_z.append(spread(tips, at))
            along_x.append(spread(faces, 2 * (f % 4) + side))
        return inside, [along_x, along_y, along_z]

    def new_parts(box):
        along_x, along_y, along_z = [], [], []
        for f in range(5):
            if f % 4 == 0:
                k = OLD + 2 * f
                faces = by_y([every(mid_ref, box, k, 2 + y) for y in range(4)])
                sides_near = jnp.where(low_y, every(mid_ref, box, k, 1), every(mid_ref, box, k, 6))
                sides_far = jnp.where(low_y, every(mid_ref, box, k, 0), every(mid_ref, box, k, 7))
                tips_near = by_y([every(tip_ref, box, k, 2 + y) for y in range(4)])
                tips_far = by_y([every(tip_ref, box, k, row) for row in (0, 1, 6, 7)])
            at = 2 * (f % 4) + half_x
            along_x.append(spread(faces, 2 * (f % 4) + side))
            along_y.append(jnp.where(outer_x, spread(sides_near, at), spread(sides_far, at)))
            along_z.append(jnp.where(outer_x, spread(tips_near, at), spread(tips_far, at)))
        return [along_x, along_y, along_z]

    directions = (
        (0, 1, sub == 0, sub == 7, 4, sub >= 4),
        (1, 16, lane < 16, lane >= 112, 64, lane >= 64),
        (1, 1, part == 0, part == 15, 8, part >= 8),
    )

    def changes(fields, step_index):
        total = None
        for normal, (axis, step, first, last, park, parked) in enumerate(directions):
            high, low, up = [[], []], [[], []], [[], []]
            for box in range(2):
                for f in range(5):
                    here, ghost = fields[box][f], ghost_ref[step_index, box, normal, f]
                    after = jnp.where(last, ghost, roll(here, -step, axis))
                    before = jnp.where(first, ghost, roll(here, step, axis))
                    one, other = edges(before, here, after)
                    high[box].append(one)
                    low[box].append(other)
                    up[box].append(jnp.where(last, ghost, roll(other, -step, axis)))
            right = [jnp.where(parked, roll(b, park, axis), a) for a, b in zip(low[0], low[1])]
            bottom = hllc([bound_ref[step_index, normal, f] for f in range(5)], right, normal)
            found = []
            for box in range(2):
                flux = hllc(high[box], up[box], normal)
                under = bottom if box == 0 else [roll(item, -park, axis) for item in bottom]
                found.append(
                    [a - jnp.where(first, b, roll(a, step, axis)) for a, b in zip(flux, under)]
                )
            total = (
                found
                if total is None
                else [[a + b for a, b in zip(t, g)] for t, g in zip(total, found)]
            )
        return total

    def keep(step_index, ghosts):
        for normal, (axis, _, _, _, park, parked) in enumerate(directions):
            for f in range(5):
                for box in range(2):
                    ghost_ref[step_index, box, normal, f] = ghosts[box][normal][f]
                bound_ref[step_index, normal, f] = jnp.where(
                    parked, roll(ghosts[1][normal][f], park, axis), ghosts[0][normal][f]
                )

    ghosts, states, later = [], [], []
    for box in range(2):
        inside, found = old_parts(box)
        ghosts.append(found)
        details = [rho_ref[box], vel_ref[0, box], vel_ref[1, box], vel_ref[2, box], p_ref[box]]
        states.append(conserved([a + b for a, b in zip(inside, details)]))
        later.append(
            [
                primitive([0.5 * (a + b) for a, b in zip(conserved(old), new)])
                for old, new in zip(found, new_parts(box))
            ]
        )
    keep(0, ghosts)
    keep(1, later)

    def stage(i, carry):
        start, state = carry
        again = lax.rem(i, 2) == 1
        weight = jnp.where(again, 0.5, 1.0).astype(F32)
        start = jax.tree.map(lambda a, b: jnp.where(again, a, b), start, state)
        moved = changes([primitive(item) for item in state], i // 2)
        state = jax.tree.map(
            lambda s, t, m: (1.0 - weight) * s + weight * (t - 0.05 * m), start, state, moved
        )
        return start, state

    _, states = lax.fori_loop(0, 4, stage, (states, states), unroll=4)
    for box in range(2):
        packed = None
        for f in range(5):
            value = states[box][f]
            out_ref[f, box] = value
            value = value + roll(value, -1, 0)
            value = value + roll(value, -1, 1)
            value = (value + roll(value, -16, 1)) * 0.125
            inside_lane = lane % 32
            at = (inside_lane // 8) * 32 + (inside_lane % 8) * 2
            value = jnp.take_along_axis(value, at, axis=1)
            if f == 0:
                packed = value
            elif f < 4:
                packed = jnp.where(lane // 32 == f, value, packed)
            else:
                packed = jnp.where((sub % 2 == 1) & (lane < 32), roll(value, 1, 0), packed)
        message_ref[parents[box]] = packed


def final_kernel(place_ref, new_ref, got_ref, out_ref, sum_ref):
    gz = place_ref[1]
    parent_ref, shift_ref = Table(place_ref, 2), Table(place_ref, 34)
    lane = iota(1)

    def add(turn, carry):
        count, sums = carry
        for k_owner in range(ADDS):
            owner = ADDS * turn + k_owner
            hit = parent_ref[2 * owner] == gz
            other = parent_ref[2 * owner + 1] == gz
            shift = jnp.where(hit, shift_ref[2 * owner], shift_ref[2 * owner + 1])
            shift = jnp.where(hit | other, shift, 256)
            inside = (lane >= shift) & (lane < shift + 8)
            value = got_ref[owner]
            count = count + jnp.where(inside, 1.0, 0.0)
            sums = [
                item
                + jnp.where(inside, pltpu.roll(value, lax.rem(shift + 128 - 8 * k, 128), 1), 0.0)
                for k, item in enumerate(sums)
            ]
        return count, sums

    zero = jnp.zeros((8, 128), F32)
    count, sums = lax.fori_loop(0, 16 // ADDS, add, (zero, [zero] * 16))
    share = inverse(jnp.maximum(count, 1.0))
    for k in range(16):
        sum_ref[8 * k : 8 * k + 8] = sums[k] * share
    for f in range(5):
        for x in range(4):
            start = (0 if f == 4 else 32 * f) + 2 * x + (1 if f == 4 else 0)
            value = sum_ref[pl.ds(start, 4, stride=8)]
            out_ref[f, x] = jnp.where(count[0:4] > 0.0, value, new_ref[f, x])


FINE_SCRATCH = ((2, 352, 128), (2, 352, 128), (2, 2, 3, 5, 8, 128), (2, 3, 5, 8, 128))


def shape(*dims):
    return jax.ShapeDtypeStruct(dims, F32)


def call(kernel, outs, scalars, arrays, scratch=()):
    return pl.pallas_call(
        kernel,
        out_shape=outs,
        in_specs=[pl.BlockSpec(memory_space=pltpu.SMEM)] * scalars
        + [pl.BlockSpec(memory_space=pltpu.VMEM)] * arrays,
        out_specs=jax.tree.map(lambda _: pl.BlockSpec(memory_space=pltpu.VMEM), outs),
        scratch_shapes=[pltpu.VMEM(dims, F32) for dims in scratch],
        compiler_params=pltpu.CompilerParams(vmem_limit_bytes=32 * 1024 * 1024),
    )


def shifted(value, axis, step):
    size = lax.axis_size(axis)
    return lax.ppermute(value, axis, [(i, (i + step) % size) for i in range(size)])


def on_device(
    density, velocity, pressure, fine_density, fine_velocity, fine_pressure, box_parent, box_shift
):
    assert density.shape == (4, 4, 128) and fine_density.shape == (1, 1, 2, 8, 128)
    place = jnp.stack([lax.axis_index("gy"), lax.axis_index("gz")]).astype(jnp.int32)
    place = jnp.concatenate([place, box_parent.reshape(32), box_shift.reshape(32)])
    prim = jnp.concatenate([density[None], velocity, pressure[None]])
    ends, for_up, for_down = call(
        ends_kernel, (shape(5, 4, 128), shape(10, 4, 128), shape(10, 4, 128)), 0, 1
    )(prim)
    far_prior, far_next = shifted(for_up, "gx", 2), shifted(for_down, "gx", -2)
    before, after = shifted(ends, "gz", 1), shifted(ends, "gz", -1)
    block = call(block_kernel, shape(4, 25, 4, 128), 0, 6)(
        ends, before, after, prim, far_prior, far_next
    )
    own = lax.all_to_all(block, "gy", 0, 0, tiled=True)
    for_up, for_down = call(near_kernel, (shape(60, 4, 128), shape(60, 4, 128)), 1, 1)(place, own)
    prior, following = shifted(for_up, "gx", 1), shifted(for_down, "gx", -1)
    updated, message = call(
        coarse_kernel,
        (shape(5, 4, 4, 128), shape(16, 2 * TILES - 1, 4, 128)),
        1,
        5,
        (
            (70, 16, 128),
            (25, 16, 128),
            (50, 16, 128),
            (15, 16, 128),
            (30, 8, 128),
            (15, 8, 128),
            (3, 20, 8, 128),
            (10, 8, 128),
            (3, 10, 8, 128),
        ),
    )(place, own, prior, following, far_prior, far_next)
    got = lax.all_to_all(message, "gz", 0, 0, tiled=True)
    fine, means = call(
        fine_kernel,
        (shape(5, 2, 8, 128), shape(16, 8, 128)),
        1,
        4,
        FINE_SCRATCH,
    )(
        place,
        got,
        fine_density.reshape(2, 8, 128),
        fine_velocity.reshape(3, 2, 8, 128),
        fine_pressure.reshape(2, 8, 128),
    )
    incoming = lax.all_to_all(means, "gz", 0, 0, tiled=True)
    coarse = call(final_kernel, shape(5, 4, 4, 128), 1, 2, ((128, 128),))(place, updated, incoming)
    return coarse, fine.reshape(5, 1, 1, 2, 8, 128)


def solution(mesh):
    in_specs = (
        P("gx", "gy", "gz"),
        P(None, "gx", "gy", "gz"),
        P("gx", "gy", "gz"),
        P("gx", "gy", "gz", None, None),
        P(None, "gx", "gy", "gz", None, None),
        P("gx", "gy", "gz", None, None),
        P("gx", "gy", None, None),
        P("gx", "gy", None),
    )
    out_specs = (P(None, "gx", "gy", "gz"), P(None, "gx", "gy", "gz", None, None))
    return jax.shard_map(
        on_device, mesh=mesh, in_specs=in_specs, out_specs=out_specs, check_vma=False
    )
```

```python
import jax
import jax.numpy as jnp
from jax import lax
from jax.experimental import pallas as pl
from jax.experimental.pallas import tpu as pltpu
from jax.sharding import PartitionSpec as P

F32 = jnp.float32
GROUP = 10
PER_ROW = 12
OLD = 20
TILES = 3
FIRST, SECOND = 2, 3
SENDS, ADDS = 8, 16


def iota(dim, shape=(8, 128)):
    return lax.broadcasted_iota(jnp.int32, shape, dim)


class Table:
    def __init__(self, ref, base):
        self.ref, self.base = ref, base

    def __getitem__(self, k):
        return self.ref[self.base + k]


def roll(value, shift, axis):
    size = value.shape[axis]
    shift = shift % size
    return value if shift == 0 else pltpu.roll(value, shift, axis)


def inverse(value):
    guess = pl.reciprocal(value, approx=True)
    return guess * (2.0 - value * guess)


def root(value):
    return value * lax.rsqrt(jnp.maximum(value, 1e-30))


def conserved(prim):
    rho, u, v, w, p = prim
    return [rho, rho * u, rho * v, rho * w, 2.5 * p + 0.5 * rho * (u * u + v * v + w * w)]


def primitive(cons):
    inv = inverse(cons[0])
    u, v, w = cons[1] * inv, cons[2] * inv, cons[3] * inv
    p = 0.4 * (cons[4] - 0.5 * (cons[1] * u + cons[2] * v + cons[3] * w))
    return [cons[0], u, v, w, p]


def edges(before, here, after):
    down, up = here - before, after - here
    half = 0.5 * (
        jnp.maximum(jnp.minimum(down, up), 0.0) + jnp.minimum(jnp.maximum(down, up), 0.0)
    )
    return here + half, here - half


def hllc(left, right, normal):
    order = [0, 1 + normal] + [1 + d for d in range(3) if d != normal] + [4]
    rho_l, un_l, ut_l, us_l, p_l = [left[k] for k in order]
    rho_r, un_r, ut_r, us_r, p_r = [right[k] for k in order]
    a_l, a_r = p_l * inverse(rho_l), p_r * inverse(rho_r)
    c_l, c_r = root(1.4 * a_l), root(1.4 * a_r)
    s_l = jnp.minimum(un_l - c_l, un_r - c_r)
    s_r = jnp.maximum(un_l + c_l, un_r + c_r)
    m_l, m_r = rho_l * (s_l - un_l), rho_r * (s_r - un_r)
    star = (p_r - p_l + m_l * un_l - m_r * un_r) * inverse(m_l - m_r)
    side = (s_l >= 0.0) | (star >= 0.0)
    pick = lambda one, other: jnp.where(side, one, other)
    rho, un, ut, us, p = (
        pick(rho_l, rho_r),
        pick(un_l, un_r),
        pick(ut_l, ut_r),
        pick(us_l, us_r),
        pick(p_l, p_r),
    )
    a, m, s = pick(a_l, a_r), pick(m_l, m_r), pick(s_l, s_r)
    limited = pick(jnp.minimum(s_l, 0.0), jnp.maximum(s_r, 0.0))
    e = 2.5 * a + 0.5 * (un * un + ut * ut + us * us)
    energy = rho * e
    r = inverse(s - star)
    factor = m * r
    momentum = rho * un
    mass = momentum + limited * (factor - rho)
    force = momentum * un + p + limited * (factor * star - momentum)
    power = (energy + p) * un + limited * (
        factor * e + (star - un) * (factor * star + p * r) - energy
    )
    result = [None] * 5
    for k, part in zip(order, [mass, force, ut * mass, us * mass, power]):
        result[k] = part
    return result


def line_change(fields, axis, normal, wide=None):
    high, low = [], []
    for k in range(5):
        here = fields[k]
        if wide is None:
            after, before = roll(here, -1, axis), roll(here, 1, axis)
        else:
            after, before = roll(wide[k], -1, axis)[0:8], roll(wide[k], 1, axis)[0:8]
        one, other = edges(before, here, after)
        high.append(one)
        low.append(roll(other, -1, axis))
    flux = hllc(high, low, normal)
    return [part - roll(part, 1, axis) for part in flux]


def next_group(tiles, j):
    lane = iota(1, tiles[j][0].shape)
    other = tiles[j + 1] if j + 1 < len(tiles) and tiles[j + 1] is not None else tiles[j]
    return [jnp.where(lane < 96, roll(a, -32, 1), roll(b, -32, 1)) for a, b in zip(tiles[j], other)]


def prior_group(tiles, j):
    lane = iota(1, tiles[j][0].shape)
    other = tiles[j - 1] if j > 0 and tiles[j - 1] is not None else tiles[j]
    return [jnp.where(lane >= 32, roll(a, 32, 1), roll(b, 32, 1)) for a, b in zip(tiles[j], other)]


def group_changes(tiles, wanted):
    high, low, flux = [None] * len(tiles), [None] * len(tiles), [None] * len(tiles)
    for j in wanted:
        pairs = [
            edges(before, here, after)
            for before, here, after in zip(prior_group(tiles, j), tiles[j], next_group(tiles, j))
        ]
        high[j] = [pair[0] for pair in pairs]
        low[j] = [pair[1] for pair in pairs]
    for j in wanted:
        flux[j] = hllc(high[j], next_group(low, j), 0)
    return {
        j: [a - b for a, b in zip(flux[j], prior_group(flux, j))] for j in wanted
    }


def ends_kernel(prim_ref, out_ref):
    lane = iota(1, (4, 128))
    for f in range(5):
        total = None
        for x in range(4):
            row = prim_ref[f, x]
            part = lane - 32 * x
            first = roll(row, 32 * x + 8, 1)
            last = roll(row, 32 * x + 24, 1)
            piece = jnp.where(part < 16, first, last)
            total = piece if total is None else jnp.where(part < 0, total, piece)
        out_ref[f] = total


def block_kernel(_, ends_ref, before_ref, after_ref, prim_ref, out_ref, up_ref, down_ref):
    lane = iota(1, (4, 128)) % 32
    for f in range(5):
        edge = jnp.where(
            lane < 8,
            roll(before_ref[f], -16, 1),
            jnp.where(lane >= 24, roll(after_ref[f], 16, 1), ends_ref[f]),
        )
        for copy in range(4):
            out_ref[copy, 20 + f] = edge
            for x in range(4):
                out_ref[copy, 5 * x + f] = prim_ref[f, x]
        for ref, x in ((up_ref, 3), (down_ref, 0)):
            ref[f] = prim_ref[f, x]
            ref[5 + f] = edge


def near_kernel(place_ref, own_ref, _, __, up_ref, down_ref):
    gy = place_ref[0]
    over, under = lax.rem(gy + 1, 4), lax.rem(gy + 3, 4)
    for ref, xs in ((up_ref, (3, 2, 1, 0)), (down_ref, (0, 1, 2, 3))):

        def take(block, distance):
            start = 5 * xs[distance - 1] if distance else 20
            return own_ref[block, start : start + 5]

        for k, distance in ((0, 1), (9, 0)):
            for j, block in enumerate((gy, over, under)):
                ref[5 * (k + j) : 5 * (k + j) + 5] = take(block, distance)
        for k, distance in ((3, 3), (5, 2), (6, 4)):
            ref[5 * k : 5 * k + 5] = take(gy, distance)
        ref[20:25, 0:2] = take(under, 3)[:, 2:4]
        ref[20:25, 2:4] = take(over, 3)[:, 0:2]
        ref[35:40, 0:3] = take(under, 2)[:, 1:4]
        ref[35:40, 3:4] = take(under, 4)[:, 3:4]
        ref[40:45, 0:3] = take(over, 2)[:, 0:3]
        ref[40:45, 3:4] = take(over, 4)[:, 0:1]


def coarse_kernel(
    place_ref, own_ref, prior_ref, next_ref, far_prior_ref, far_next_ref,
    new_ref, message_ref,
    prim_ref, edge_ref, section_ref, section_edge_ref, made_ref, made_edge_ref,
    old_pack_ref, body_ref, tips_ref,
):
    gy, gz = place_ref[0], place_ref[1]
    parent_ref, shift_ref = Table(place_ref, 2), Table(place_ref, 34)
    for k in range(4):
        source = lax.rem(gy + k, 4)
        rows, tips = own_ref[source, 0:20], own_ref[source, 20:25]
        for ref, base, count, value in ((prim_ref, 25, 20, rows), (edge_ref, 10, 5, tips)):
            if k < 3:
                ref[base : base + count, 2 + 4 * k : 6 + 4 * k] = value
            else:
                ref[base : base + count, 14:16] = value[:, 0:2]
                ref[base : base + count, 0:2] = value[:, 2:4]
    for got_ref, tile, bases in (
        (prior_ref, 5, (20, 15, 10, 5)),
        (next_ref, 15, (45, 50, 55, 60)),
    ):
        got = [got_ref[5 * k : 5 * k + 5] for k in range(12)]
        for ref, base, first in ((prim_ref, bases[0], 0), (edge_ref, tile, 9)):
            ref[base : base + 5, 2:6] = got[first]
            ref[base : base + 5, 6:10] = got[first + 1]
            ref[base : base + 5, 14:16] = got[first + 2][:, 0:2]
            ref[base : base + 5, 0:2] = got[first + 2][:, 2:4]
        for base, first in ((bases[2], 3), (bases[1], 5), (bases[3], 6)):
            prim_ref[base : base + 5, 2:6] = got[first]
        prim_ref[bases[2] : bases[2] + 5, 0:2] = got[4][:, 0:2]
        prim_ref[bases[2] : bases[2] + 5, 6:8] = got[4][:, 2:4]
        prim_ref[bases[1] : bases[1] + 5, 15:16] = got[7][:, 0:1]
        prim_ref[bases[1] : bases[1] + 5, 0:2] = got[7][:, 1:3]
        prim_ref[bases[1] : bases[1] + 5, 6:9] = got[8][:, 0:3]
        prim_ref[bases[3] : bases[3] + 5, 1:2] = got[7][:, 3:4]
        prim_ref[bases[3] : bases[3] + 5, 6:7] = got[8][:, 3:4]
    prim_ref[0:5, 2:6] = far_prior_ref[0:5]
    edge_ref[0:5, 2:6] = far_prior_ref[5:10]
    prim_ref[65:70, 2:6] = far_next_ref[0:5]
    edge_ref[20:25, 2:6] = far_next_ref[5:10]

    def prim_row(x):
        return [prim_ref[5 * (x + 5) + f] for f in range(5)]

    def section_row(x, rows=16):
        return [section_ref[5 * (x + 3) + f, 0:rows] for f in range(5)]

    def sweep(row, start, rows, at_once, emit):
        def pairs_of(x):
            found = [edges(b, h, a) for b, h, a in zip(row(x - 1), row(x), row(x + 1))]
            return [pair[0] for pair in found], [pair[1] for pair in found]

        def step(i, carry):
            high, flux = carry
            for k in range(at_once):
                x = start + i * at_once + k
                high_next, low = pairs_of(x + 1)
                flux_next = hllc(high, low, 0)
                emit(x, [after - before for before, after in zip(flux, flux_next)])
                high, flux = high_next, flux_next
            return high, flux

        high_before, _ = pairs_of(start - 1)
        high, low = pairs_of(start)
        lax.fori_loop(0, rows // at_once, step, (high, hllc(high_before, low, 0)))

    def section_of(x, by_x):
        middle = prim_row(x)
        by_y = line_change(middle, 0, 1)
        by_z = line_change(middle, 1, 2)
        state = conserved(middle)
        section = [state[f] - 0.05 * (by_x[f] + by_y[f] + by_z[f]) for f in range(5)]
        for f, value in enumerate(primitive(section)):
            section_ref[5 * (x + 3) + f] = value

    sweep(prim_row, -3, 10, FIRST, section_of)
    tiles = [[edge_ref[5 * t + f] for f in range(5)] for t in range(5)]
    by_x = group_changes(tiles, (1, 2, 3))
    for t in (1, 2, 3):
        by_y = line_change(tiles[t], 0, 1)
        by_z = line_change(tiles[t], 1, 2)
        state = conserved(tiles[t])
        section = [state[f] - 0.05 * (by_x[t][f] + by_y[f] + by_z[f]) for f in range(5)]
        for f, value in enumerate(primitive(section)):
            section_edge_ref[5 * (t - 1) + f] = value

    def advance(old, here, changes):
        start, state = conserved(old), conserved(here)
        return [
            0.5 * start[f] + 0.5 * (state[f] - 0.05 * (changes[0][f] + changes[1][f] + changes[2][f]))
            for f in range(5)
        ]

    def updated_of(x, by_x):
        middle = section_row(x, 8)
        by_y = line_change(middle, 0, 1, section_row(x))
        by_z = line_change(middle, 1, 2)
        old = [part[0:8] for part in prim_row(x)]
        for f, value in enumerate(advance(old, middle, (by_x, by_y, by_z))):
            made_ref[5 * (x + 1) + f] = value

    sweep(lambda x: section_row(x, 8), -1, 6, SECOND, updated_of)
    wide = [[section_edge_ref[5 * t + f] for f in range(5)] for t in range(3)]
    tiles = [[part[0:8] for part in tile] for tile in wide]
    by_x = group_changes(tiles, (0, 1, 2))
    for t in range(3):
        by_y = line_change(tiles[t], 0, 1, wide[t])
        by_z = line_change(tiles[t], 1, 2)
        old = [edge_ref[5 * (t + 1) + f, 0:8] for f in range(5)]
        for f, value in enumerate(advance(old, tiles[t], (by_x[t], by_y, by_z))):
            made_edge_ref[5 * t + f] = value

    lane, sub = iota(1), iota(0)

    def spot(x):
        return (0, 3) if x < 0 else ((2, 0) if x > 3 else (1, x))

    for f in range(5):
        olds, news = {}, {}
        for x in range(-1, 5):
            tile, group = spot(x)
            main = prim_ref[5 * (x + 5) + f, 0:8]
            tips = edge_ref[5 * (tile + 1) + f, 0:8]
            under, over = roll(tips, -32 * group - 8, 1), roll(tips, 104 - 32 * group, 1)
            olds[x] = (main, jnp.where(lane == 127, under, main), jnp.where(lane == 0, over, main))
            main, tips = made_ref[5 * (x + 1) + f], made_edge_ref[5 * tile + f]
            under, over = roll(tips, -32 * group - 8, 1), roll(tips, 104 - 32 * group, 1)
            main = jnp.where(lane < 4, under, jnp.where(lane >= 124, over, main))
            news[x] = (main, jnp.where(lane == 127, under, main), jnp.where(lane == 0, over, main))
            if 0 <= x < 4:
                new_ref[f, x] = main[2:6]
        inner = (sub >= 2) & (sub < 6)
        for x in range(4):
            face = olds[-1 if x < 2 else 4][0]
            top, bottom = (-2, 4) if x % 2 == 0 else (-4, 2)
            for kind in range(3):
                old_pack_ref[kind, 4 * f + x] = jnp.where(
                    sub == 0,
                    roll(face, top, 0),
                    jnp.where(sub == 7, roll(face, bottom, 0), olds[x][kind]),
                )
        for half, (out, near, far) in enumerate(((-1, 0, 1), (4, 3, 2))):
            body_ref[2 * f + half] = jnp.where(
                inner,
                news[out][0],
                jnp.where(
                    sub == 0,
                    roll(news[far][0], -1, 0),
                    jnp.where(sub == 7, roll(news[far][0], 1, 0), news[near][0]),
                ),
            )
            for kind in range(3):
                tips_ref[kind, 2 * f + half] = jnp.where(
                    inner,
                    news[near][kind],
                    jnp.where(sub < 2, roll(news[far][kind], -2, 0), roll(news[far][kind], 2, 0)),
                )

    def send(turn, carry):
        for k_owner in range(SENDS):
            owner = SENDS * turn + k_owner
            hit = parent_ref[2 * owner] == gz
            shift = jnp.where(hit, shift_ref[2 * owner], shift_ref[2 * owner + 1])
            kind = jnp.where(shift == 0, 1, jnp.where(shift == 120, 2, 0))
            for tile in range(TILES):
                total = None
                for j in range(PER_ROW):
                    k = tile * PER_ROW + j
                    if k >= OLD + 10:
                        break
                    amount = lax.rem(GROUP * j + 129 - shift, 128)
                    if k < OLD:
                        piece = pltpu.roll(old_pack_ref[kind, k], amount, 1)
                    else:
                        piece = jnp.where(
                            (lane == GROUP * j) | (lane == GROUP * j + 9),
                            pltpu.roll(tips_ref[kind, k - OLD], amount, 1),
                            pltpu.roll(body_ref[k - OLD], amount, 1),
                        )
                    total = piece if total is None else jnp.where(lane < GROUP * j, total, piece)
                if tile < TILES - 1:
                    message_ref[owner, 2 * tile] = total[0:4]
                    message_ref[owner, 2 * tile + 1] = total[4:8]
                else:
                    message_ref[owner, 2 * tile] = jnp.where(
                        iota(1, (4, 128)) < 60, total[0:4], roll(total, 60, 1)[4:8]
                    )
        return carry

    lax.fori_loop(0, 16 // SENDS, send, 0)


def fine_kernel(
    place_ref, got_ref, rho_ref, vel_ref, p_ref, out_ref, message_ref,
    mid_ref, tip_ref, ghost_ref, bound_ref,
):
    gz = place_ref[1]
    parent_ref = Table(place_ref, 2)
    lane, sub = iota(1), iota(0)
    part = lane % 16
    yc, xc = lane // 32, sub // 2
    parents = [parent_ref[2 * gz + box] for box in range(2)]

    for box in range(2):
        tiles = [
            jnp.concatenate([got_ref[parents[box], 2 * t], got_ref[parents[box], 2 * t + 1]])
            for t in range(TILES - 1)
        ]
        short = got_ref[parents[box], 2 * TILES - 2]
        tiles.append(jnp.concatenate([short, roll(short, -60, 1)]))
        for k in range(OLD + 10):
            j = k % PER_ROW
            tile = tiles[k // PER_ROW]
            at = GROUP * j + 1 + part // 2
            mid_ref[box, 8 * k : 8 * k + 8] = jnp.take_along_axis(tile, at, axis=1)
            at = GROUP * j + jnp.where(part < 8, 0, 9)
            tip_ref[box, 8 * k : 8 * k + 8] = jnp.take_along_axis(tile, at, axis=1)

    def every(ref, box, k, row, step=1):
        return ref[box, pl.ds(8 * k + row, 8, stride=8 * step)]

    def by_y(items):
        return jnp.where(
            yc < 2,
            jnp.where(yc == 0, items[0], items[1]),
            jnp.where(yc == 2, items[2], items[3]),
        )

    def spread(value, rows):
        return jnp.take_along_axis(value, rows, axis=0)

    side, low_y = (sub >= 4).astype(jnp.int32), lane < 64
    outer_x = (xc == 0) | (xc == 3)
    half_x = (xc >= 2).astype(jnp.int32)

    def old_parts(box):
        inside, along_x, along_y, along_z = [], [], [], []
        for f in range(5):
            if f % 2 == 0:
                middle = by_y([every(mid_ref, box, 4 * f, 2 + y) for y in range(4)])
                sides = jnp.where(low_y, every(mid_ref, box, 4 * f, 1), every(mid_ref, box, 4 * f, 6))
                tips = by_y([every(tip_ref, box, 4 * f, 2 + y) for y in range(4)])
            if f % 4 == 0:
                faces = by_y(
                    [every(mid_ref, box, 4 * f + y // 2, 7 * (y % 2), 2) for y in range(4)]
                )
            at = 4 * (f % 2) + xc
            inside.append(spread(middle, at))
            along_y.append(spread(sides, at))
            along_z.append(spread(tips, at))
            along_x.append(spread(faces, 2 * (f % 4) + side))
        return inside, [along_x, along_y, along_z]

    def new_parts(box):
        along_x, along_y, along_z = [], [], []
        for f in range(5):
            if f % 4 == 0:
                k = OLD + 2 * f
                faces = by_y([every(mid_ref, box, k, 2 + y) for y in range(4)])
                sides_near = jnp.where(low_y, every(mid_ref, box, k, 1), every(mid_ref, box, k, 6))
                sides_far = jnp.where(low_y, every(mid_ref, box, k, 0), every(mid_ref, box, k, 7))
                tips_near = by_y([every(tip_ref, box, k, 2 + y) for y in range(4)])
                tips_far = by_y([every(tip_ref, box, k, row) for row in (0, 1, 6, 7)])
            at = 2 * (f % 4) + half_x
            along_x.append(spread(faces, 2 * (f % 4) + side))
            along_y.append(jnp.where(outer_x, spread(sides_near, at), spread(sides_far, at)))
            along_z.append(jnp.where(outer_x, spread(tips_near, at), spread(tips_far, at)))
        return [along_x, along_y, along_z]

    directions = (
        (0, 1, sub == 0, sub == 7, 4, sub >= 4),
        (1, 16, lane < 16, lane >= 112, 64, lane >= 64),
        (1, 1, part == 0, part == 15, 8, part >= 8),
    )

    def changes(fields, step_index):
        total = None
        for normal, (axis, step, first, last, park, parked) in enumerate(directions):
            high, low, up = [[], []], [[], []], [[], []]
            for box in range(2):
                for f in range(5):
                    here, ghost = fields[box][f], ghost_ref[step_index, box, normal, f]
                    after = jnp.where(last, ghost, roll(here, -step, axis))
                    before = jnp.where(first, ghost, roll(here, step, axis))
                    one, other = edges(before, here, after)
                    high[box].append(one)
                    low[box].append(other)
                    up[box].append(jnp.where(last, ghost, roll(other, -step, axis)))
            right = [jnp.where(parked, roll(b, park, axis), a) for a, b in zip(low[0], low[1])]
            bottom = hllc([bound_ref[step_index, normal, f] for f in range(5)], right, normal)
            found = []
            for box in range(2):
                flux = hllc(high[box], up[box], normal)
                under = bottom if box == 0 else [roll(item, -park, axis) for item in bottom]
                found.append(
                    [a - jnp.where(first, b, roll(a, step, axis)) for a, b in zip(flux, under)]
                )
            total = (
                found
                if total is None
                else [[a + b for a, b in zip(t, g)] for t, g in zip(total, found)]
            )
        return total

    def keep(step_index, ghosts):
        for normal, (axis, _, _, _, park, parked) in enumerate(directions):
            for f in range(5):
                for box in range(2):
                    ghost_ref[step_index, box, normal, f] = ghosts[box][normal][f]
                bound_ref[step_index, normal, f] = jnp.where(
                    parked, roll(ghosts[1][normal][f], park, axis), ghosts[0][normal][f]
                )

    ghosts, states, later = [], [], []
    for box in range(2):
        inside, found = old_parts(box)
        ghosts.append(found)
        details = [rho_ref[box], vel_ref[0, box], vel_ref[1, box], vel_ref[2, box], p_ref[box]]
        states.append(conserved([a + b for a, b in zip(inside, details)]))
        later.append(
            [
                primitive([0.5 * (a + b) for a, b in zip(conserved(old), new)])
                for old, new in zip(found, new_parts(box))
            ]
        )
    keep(0, ghosts)
    keep(1, later)

    def stage(i, carry):
        start, state = carry
        again = lax.rem(i, 2) == 1
        weight = jnp.where(again, 0.5, 1.0).astype(F32)
        start = jax.tree.map(lambda a, b: jnp.where(again, a, b), start, state)
        moved = changes([primitive(item) for item in state], i // 2)
        state = jax.tree.map(
            lambda s, t, m: (1.0 - weight) * s + weight * (t - 0.05 * m), start, state, moved
        )
        return start, state

    _, states = lax.fori_loop(0, 4, stage, (states, states), unroll=4)
    for box in range(2):
        packed = None
        for f in range(5):
            value = states[box][f]
            out_ref[f, box] = value
            value = value + roll(value, -1, 0)
            value = value + roll(value, -1, 1)
            value = (value + roll(value, -16, 1)) * 0.125
            inside_lane = lane % 32
            at = (inside_lane // 8) * 32 + (inside_lane % 8) * 2
            value = jnp.take_along_axis(value, at, axis=1)
            if f == 0:
                packed = value
            elif f < 4:
                packed = jnp.where(lane // 32 == f, value, packed)
            else:
                packed = jnp.where((sub % 2 == 1) & (lane < 32), roll(value, 1, 0), packed)
        message_ref[parents[box]] = packed


def final_kernel(place_ref, new_ref, got_ref, out_ref, sum_ref):
    gz = place_ref[1]
    parent_ref, shift_ref = Table(place_ref, 2), Table(place_ref, 34)
    lane = iota(1)

    def add(turn, carry):
        count, sums = carry
        for k_owner in range(ADDS):
            owner = ADDS * turn + k_owner
            hit = parent_ref[2 * owner] == gz
            other = parent_ref[2 * owner + 1] == gz
            shift = jnp.where(hit, shift_ref[2 * owner], shift_ref[2 * owner + 1])
            shift = jnp.where(hit | other, shift, 256)
            inside = (lane >= shift) & (lane < shift + 8)
            value = got_ref[owner]
            count = count + jnp.where(inside, 1.0, 0.0)
            sums = [
                item
                + jnp.where(inside, pltpu.roll(value, lax.rem(shift + 128 - 8 * k, 128), 1), 0.0)
                for k, item in enumerate(sums)
            ]
        return count, sums

    zero = jnp.zeros((8, 128), F32)
    count, sums = lax.fori_loop(0, 16 // ADDS, add, (zero, [zero] * 16))
    share = inverse(jnp.maximum(count, 1.0))
    for k in range(16):
        sum_ref[8 * k : 8 * k + 8] = sums[k] * share
    for f in range(5):
        for x in range(4):
            start = (0 if f == 4 else 32 * f) + 2 * x + (1 if f == 4 else 0)
            value = sum_ref[pl.ds(start, 4, stride=8)]
            out_ref[f, x] = jnp.where(count[0:4] > 0.0, value, new_ref[f, x])


FINE_SCRATCH = ((2, 352, 128), (2, 352, 128), (2, 2, 3, 5, 8, 128), (2, 3, 5, 8, 128))


def shape(*dims):
    return jax.ShapeDtypeStruct(dims, F32)


def call(kernel, outs, scalars, arrays, scratch=()):
    return pl.pallas_call(
        kernel,
        out_shape=outs,
        in_specs=[pl.BlockSpec(memory_space=pltpu.SMEM)] * scalars
        + [pl.BlockSpec(memory_space=pltpu.VMEM)] * arrays,
        out_specs=jax.tree.map(lambda _: pl.BlockSpec(memory_space=pltpu.VMEM), outs),
        scratch_shapes=[pltpu.VMEM(dims, F32) for dims in scratch],
        compiler_params=pltpu.CompilerParams(vmem_limit_bytes=32 * 1024 * 1024),
    )


def shifted(value, axis, step):
    size = lax.axis_size(axis)
    return lax.ppermute(value, axis, [(i, (i + step) % size) for i in range(size)])


def on_device(
    density, velocity, pressure, fine_density, fine_velocity, fine_pressure, box_parent, box_shift
):
    assert density.shape == (4, 4, 128) and fine_density.shape == (1, 1, 2, 8, 128)
    place = jnp.stack([lax.axis_index("gy"), lax.axis_index("gz")]).astype(jnp.int32)
    place = jnp.concatenate([place, box_parent.reshape(32), box_shift.reshape(32)])
    prim = jnp.concatenate([density[None], velocity, pressure[None]])
    ends = call(ends_kernel, shape(5, 4, 128), 0, 1)(prim)
    before, after = shifted(ends, "gz", 1), shifted(ends, "gz", -1)
    block, for_up, for_down = call(
        block_kernel, (shape(4, 25, 4, 128), shape(10, 4, 128), shape(10, 4, 128)), 1, 4
    )(place, ends, before, after, prim)
    own = lax.all_to_all(block, "gy", 0, 0, tiled=True)
    far_prior, far_next = shifted(for_up, "gx", 2), shifted(for_down, "gx", -2)
    for_up, for_down = call(near_kernel, (shape(60, 4, 128), shape(60, 4, 128)), 1, 3)(
        place, own, far_prior, far_next
    )
    prior, following = shifted(for_up, "gx", 1), shifted(for_down, "gx", -1)
    updated, message = call(
        coarse_kernel,
        (shape(5, 4, 4, 128), shape(16, 2 * TILES - 1, 4, 128)),
        1,
        5,
        (
            (70, 16, 128),
            (25, 16, 128),
            (50, 16, 128),
            (15, 16, 128),
            (30, 8, 128),
            (15, 8, 128),
            (3, 20, 8, 128),
            (10, 8, 128),
            (3, 10, 8, 128),
        ),
    )(place, own, prior, following, far_prior, far_next)
    got = lax.all_to_all(message, "gz", 0, 0, tiled=True)
    fine, means = call(
        fine_kernel,
        (shape(5, 2, 8, 128), shape(16, 8, 128)),
        1,
        4,
        FINE_SCRATCH,
    )(
        place,
        got,
        fine_density.reshape(2, 8, 128),
        fine_velocity.reshape(3, 2, 8, 128),
        fine_pressure.reshape(2, 8, 128),
    )
    incoming = lax.all_to_all(means, "gz", 0, 0, tiled=True)
    coarse = call(final_kernel, shape(5, 4, 4, 128), 1, 2, ((128, 128),))(place, updated, incoming)
    return coarse, fine.reshape(5, 1, 1, 2, 8, 128)


def solution(mesh):
    in_specs = (
        P("gx", "gy", "gz"),
        P(None, "gx", "gy", "gz"),
        P("gx", "gy", "gz"),
        P("gx", "gy", "gz", None, None),
        P(None, "gx", "gy", "gz", None, None),
        P("gx", "gy", "gz", None, None),
        P("gx", "gy", None, None),
        P("gx", "gy", None),
    )
    out_specs = (P(None, "gx", "gy", "gz"), P(None, "gx", "gy", "gz", None, None))
    return jax.shard_map(
        on_device, mesh=mesh, in_specs=in_specs, out_specs=out_specs, check_vma=False
    )
```

```python
import jax
import jax.numpy as jnp
from jax import lax
from jax.experimental import pallas as pl
from jax.experimental.pallas import tpu as pltpu
from jax.sharding import PartitionSpec as P

F32 = jnp.float32
GROUP = 10
PER_ROW = 12
OLD = 20
TILES = 3
FIRST, SECOND = 2, 3
SENDS, ADDS = 8, 16


def iota(dim, shape=(8, 128)):
    return lax.broadcasted_iota(jnp.int32, shape, dim)


class Table:
    def __init__(self, ref, base):
        self.ref, self.base = ref, base

    def __getitem__(self, k):
        return self.ref[self.base + k]


def roll(value, shift, axis):
    size = value.shape[axis]
    shift = shift % size
    return value if shift == 0 else pltpu.roll(value, shift, axis)


def inverse(value):
    guess = pl.reciprocal(value, approx=True)
    return guess * (2.0 - value * guess)


def root(value):
    return value * lax.rsqrt(jnp.maximum(value, 1e-30))


def conserved(prim):
    rho, u, v, w, p = prim
    return [rho, rho * u, rho * v, rho * w, 2.5 * p + 0.5 * rho * (u * u + v * v + w * w)]


def primitive(cons):
    inv = inverse(cons[0])
    u, v, w = cons[1] * inv, cons[2] * inv, cons[3] * inv
    p = 0.4 * (cons[4] - 0.5 * (cons[1] * u + cons[2] * v + cons[3] * w))
    return [cons[0], u, v, w, p]


def edges(before, here, after):
    down, up = here - before, after - here
    half = 0.5 * (
        jnp.maximum(jnp.minimum(down, up), 0.0) + jnp.minimum(jnp.maximum(down, up), 0.0)
    )
    return here + half, here - half


def hllc(left, right, normal):
    order = [0, 1 + normal] + [1 + d for d in range(3) if d != normal] + [4]
    rho_l, un_l, ut_l, us_l, p_l = [left[k] for k in order]
    rho_r, un_r, ut_r, us_r, p_r = [right[k] for k in order]
    a_l, a_r = p_l * inverse(rho_l), p_r * inverse(rho_r)
    c_l, c_r = root(1.4 * a_l), root(1.4 * a_r)
    s_l = jnp.minimum(un_l - c_l, un_r - c_r)
    s_r = jnp.maximum(un_l + c_l, un_r + c_r)
    m_l, m_r = rho_l * (s_l - un_l), rho_r * (s_r - un_r)
    star = (p_r - p_l + m_l * un_l - m_r * un_r) * inverse(m_l - m_r)
    side = (s_l >= 0.0) | (star >= 0.0)
    pick = lambda one, other: jnp.where(side, one, other)
    rho, un, ut, us, p = (
        pick(rho_l, rho_r),
        pick(un_l, un_r),
        pick(ut_l, ut_r),
        pick(us_l, us_r),
        pick(p_l, p_r),
    )
    a, m, s = pick(a_l, a_r), pick(m_l, m_r), pick(s_l, s_r)
    limited = pick(jnp.minimum(s_l, 0.0), jnp.maximum(s_r, 0.0))
    e = 2.5 * a + 0.5 * (un * un + ut * ut + us * us)
    energy = rho * e
    r = inverse(s - star)
    factor = m * r
    momentum = rho * un
    mass = momentum + limited * (factor - rho)
    force = momentum * un + p + limited * (factor * star - momentum)
    power = (energy + p) * un + limited * (
        factor * e + (star - un) * (factor * star + p * r) - energy
    )
    result = [None] * 5
    for k, part in zip(order, [mass, force, ut * mass, us * mass, power]):
        result[k] = part
    return result


def line_change(fields, axis, normal, wide=None):
    high, low = [], []
    for k in range(5):
        here = fields[k]
        if wide is None:
            after, before = roll(here, -1, axis), roll(here, 1, axis)
        else:
            after, before = roll(wide[k], -1, axis)[0:8], roll(wide[k], 1, axis)[0:8]
        one, other = edges(before, here, after)
        high.append(one)
        low.append(roll(other, -1, axis))
    flux = hllc(high, low, normal)
    return [part - roll(part, 1, axis) for part in flux]


def next_group(tiles, j):
    lane = iota(1, tiles[j][0].shape)
    other = tiles[j + 1] if j + 1 < len(tiles) and tiles[j + 1] is not None else tiles[j]
    return [jnp.where(lane < 96, roll(a, -32, 1), roll(b, -32, 1)) for a, b in zip(tiles[j], other)]


def prior_group(tiles, j):
    lane = iota(1, tiles[j][0].shape)
    other = tiles[j - 1] if j > 0 and tiles[j - 1] is not None else tiles[j]
    return [jnp.where(lane >= 32, roll(a, 32, 1), roll(b, 32, 1)) for a, b in zip(tiles[j], other)]


def group_changes(tiles, wanted):
    high, low, flux = [None] * len(tiles), [None] * len(tiles), [None] * len(tiles)
    for j in wanted:
        pairs = [
            edges(before, here, after)
            for before, here, after in zip(prior_group(tiles, j), tiles[j], next_group(tiles, j))
        ]
        high[j] = [pair[0] for pair in pairs]
        low[j] = [pair[1] for pair in pairs]
    for j in wanted:
        flux[j] = hllc(high[j], next_group(low, j), 0)
    return {
        j: [a - b for a, b in zip(flux[j], prior_group(flux, j))] for j in wanted
    }


def ends_kernel(prim_ref, out_ref, up_ref):
    lane = iota(1, (4, 128))
    for f in range(5):
        total = None
        for x in range(4):
            row = prim_ref[f, x]
            part = lane - 32 * x
            first = roll(row, 32 * x + 8, 1)
            last = roll(row, 32 * x + 24, 1)
            piece = jnp.where(part < 16, first, last)
            total = piece if total is None else jnp.where(part < 0, total, piece)
        out_ref[f] = total
        up_ref[f] = prim_ref[f, 3]
        up_ref[5 + f] = total


def block_kernel(_, ends_ref, before_ref, after_ref, prim_ref, __, out_ref, down_ref):
    lane = iota(1, (4, 128)) % 32
    for f in range(5):
        edge = jnp.where(
            lane < 8,
            roll(before_ref[f], -16, 1),
            jnp.where(lane >= 24, roll(after_ref[f], 16, 1), ends_ref[f]),
        )
        for copy in range(4):
            out_ref[copy, 20 + f] = edge
            for x in range(4):
                out_ref[copy, 5 * x + f] = prim_ref[f, x]
        down_ref[f] = prim_ref[f, 0]
        down_ref[5 + f] = edge


def near_kernel(place_ref, own_ref, _, up_ref, down_ref):
    gy = place_ref[0]
    over, under = lax.rem(gy + 1, 4), lax.rem(gy + 3, 4)
    for ref, xs in ((up_ref, (3, 2, 1, 0)), (down_ref, (0, 1, 2, 3))):

        def take(block, distance):
            start = 5 * xs[distance - 1] if distance else 20
            return own_ref[block, start : start + 5]

        for k, distance in ((0, 1), (9, 0)):
            for j, block in enumerate((gy, over, under)):
                ref[5 * (k + j) : 5 * (k + j) + 5] = take(block, distance)
        for k, distance in ((3, 3), (5, 2), (6, 4)):
            ref[5 * k : 5 * k + 5] = take(gy, distance)
        ref[20:25, 0:2] = take(under, 3)[:, 2:4]
        ref[20:25, 2:4] = take(over, 3)[:, 0:2]
        ref[35:40, 0:3] = take(under, 2)[:, 1:4]
        ref[35:40, 3:4] = take(under, 4)[:, 3:4]
        ref[40:45, 0:3] = take(over, 2)[:, 0:3]
        ref[40:45, 3:4] = take(over, 4)[:, 0:1]


def coarse_kernel(
    place_ref, own_ref, prior_ref, next_ref, far_prior_ref, far_next_ref,
    new_ref, message_ref,
    prim_ref, edge_ref, section_ref, section_edge_ref, made_ref, made_edge_ref,
    old_pack_ref, body_ref, tips_ref,
):
    gy, gz = place_ref[0], place_ref[1]
    parent_ref, shift_ref = Table(place_ref, 2), Table(place_ref, 34)
    for k in range(4):
        source = lax.rem(gy + k, 4)
        rows, tips = own_ref[source, 0:20], own_ref[source, 20:25]
        for ref, base, count, value in ((prim_ref, 25, 20, rows), (edge_ref, 10, 5, tips)):
            if k < 3:
                ref[base : base + count, 2 + 4 * k : 6 + 4 * k] = value
            else:
                ref[base : base + count, 14:16] = value[:, 0:2]
                ref[base : base + count, 0:2] = value[:, 2:4]
    for got_ref, tile, bases in (
        (prior_ref, 5, (20, 15, 10, 5)),
        (next_ref, 15, (45, 50, 55, 60)),
    ):
        got = [got_ref[5 * k : 5 * k + 5] for k in range(12)]
        for ref, base, first in ((prim_ref, bases[0], 0), (edge_ref, tile, 9)):
            ref[base : base + 5, 2:6] = got[first]
            ref[base : base + 5, 6:10] = got[first + 1]
            ref[base : base + 5, 14:16] = got[first + 2][:, 0:2]
            ref[base : base + 5, 0:2] = got[first + 2][:, 2:4]
        for base, first in ((bases[2], 3), (bases[1], 5), (bases[3], 6)):
            prim_ref[base : base + 5, 2:6] = got[first]
        prim_ref[bases[2] : bases[2] + 5, 0:2] = got[4][:, 0:2]
        prim_ref[bases[2] : bases[2] + 5, 6:8] = got[4][:, 2:4]
        prim_ref[bases[1] : bases[1] + 5, 15:16] = got[7][:, 0:1]
        prim_ref[bases[1] : bases[1] + 5, 0:2] = got[7][:, 1:3]
        prim_ref[bases[1] : bases[1] + 5, 6:9] = got[8][:, 0:3]
        prim_ref[bases[3] : bases[3] + 5, 1:2] = got[7][:, 3:4]
        prim_ref[bases[3] : bases[3] + 5, 6:7] = got[8][:, 3:4]
    prim_ref[0:5, 2:6] = far_prior_ref[0:5]
    edge_ref[0:5, 2:6] = far_prior_ref[5:10]
    prim_ref[65:70, 2:6] = far_next_ref[0:5]
    edge_ref[20:25, 2:6] = far_next_ref[5:10]

    def prim_row(x):
        return [prim_ref[5 * (x + 5) + f] for f in range(5)]

    def section_row(x, rows=16):
        return [section_ref[5 * (x + 3) + f, 0:rows] for f in range(5)]

    def sweep(row, start, rows, at_once, emit):
        def pairs_of(x):
            found = [edges(b, h, a) for b, h, a in zip(row(x - 1), row(x), row(x + 1))]
            return [pair[0] for pair in found], [pair[1] for pair in found]

        def step(i, carry):
            high, flux = carry
            for k in range(at_once):
                x = start + i * at_once + k
                high_next, low = pairs_of(x + 1)
                flux_next = hllc(high, low, 0)
                emit(x, [after - before for before, after in zip(flux, flux_next)])
                high, flux = high_next, flux_next
            return high, flux

        high_before, _ = pairs_of(start - 1)
        high, low = pairs_of(start)
        lax.fori_loop(0, rows // at_once, step, (high, hllc(high_before, low, 0)))

    def section_of(x, by_x):
        middle = prim_row(x)
        by_y = line_change(middle, 0, 1)
        by_z = line_change(middle, 1, 2)
        state = conserved(middle)
        section = [state[f] - 0.05 * (by_x[f] + by_y[f] + by_z[f]) for f in range(5)]
        for f, value in enumerate(primitive(section)):
            section_ref[5 * (x + 3) + f] = value

    sweep(prim_row, -3, 10, FIRST, section_of)
    tiles = [[edge_ref[5 * t + f] for f in range(5)] for t in range(5)]
    by_x = group_changes(tiles, (1, 2, 3))
    for t in (1, 2, 3):
        by_y = line_change(tiles[t], 0, 1)
        by_z = line_change(tiles[t], 1, 2)
        state = conserved(tiles[t])
        section = [state[f] - 0.05 * (by_x[t][f] + by_y[f] + by_z[f]) for f in range(5)]
        for f, value in enumerate(primitive(section)):
            section_edge_ref[5 * (t - 1) + f] = value

    def advance(old, here, changes):
        start, state = conserved(old), conserved(here)
        return [
            0.5 * start[f] + 0.5 * (state[f] - 0.05 * (changes[0][f] + changes[1][f] + changes[2][f]))
            for f in range(5)
        ]

    def updated_of(x, by_x):
        middle = section_row(x, 8)
        by_y = line_change(middle, 0, 1, section_row(x))
        by_z = line_change(middle, 1, 2)
        old = [part[0:8] for part in prim_row(x)]
        for f, value in enumerate(advance(old, middle, (by_x, by_y, by_z))):
            made_ref[5 * (x + 1) + f] = value

    sweep(lambda x: section_row(x, 8), -1, 6, SECOND, updated_of)
    wide = [[section_edge_ref[5 * t + f] for f in range(5)] for t in range(3)]
    tiles = [[part[0:8] for part in tile] for tile in wide]
    by_x = group_changes(tiles, (0, 1, 2))
    for t in range(3):
        by_y = line_change(tiles[t], 0, 1, wide[t])
        by_z = line_change(tiles[t], 1, 2)
        old = [edge_ref[5 * (t + 1) + f, 0:8] for f in range(5)]
        for f, value in enumerate(advance(old, tiles[t], (by_x[t], by_y, by_z))):
            made_edge_ref[5 * t + f] = value

    lane, sub = iota(1), iota(0)

    def spot(x):
        return (0, 3) if x < 0 else ((2, 0) if x > 3 else (1, x))

    for f in range(5):
        olds, news = {}, {}
        for x in range(-1, 5):
            tile, group = spot(x)
            main = prim_ref[5 * (x + 5) + f, 0:8]
            tips = edge_ref[5 * (tile + 1) + f, 0:8]
            under, over = roll(tips, -32 * group - 8, 1), roll(tips, 104 - 32 * group, 1)
            olds[x] = (main, jnp.where(lane == 127, under, main), jnp.where(lane == 0, over, main))
            main, tips = made_ref[5 * (x + 1) + f], made_edge_ref[5 * tile + f]
            under, over = roll(tips, -32 * group - 8, 1), roll(tips, 104 - 32 * group, 1)
            main = jnp.where(lane < 4, under, jnp.where(lane >= 124, over, main))
            news[x] = (main, jnp.where(lane == 127, under, main), jnp.where(lane == 0, over, main))
            if 0 <= x < 4:
                new_ref[f, x] = main[2:6]
        inner = (sub >= 2) & (sub < 6)
        for x in range(4):
            face = olds[-1 if x < 2 else 4][0]
            top, bottom = (-2, 4) if x % 2 == 0 else (-4, 2)
            for kind in range(3):
                old_pack_ref[kind, 4 * f + x] = jnp.where(
                    sub == 0,
                    roll(face, top, 0),
                    jnp.where(sub == 7, roll(face, bottom, 0), olds[x][kind]),
                )
        for half, (out, near, far) in enumerate(((-1, 0, 1), (4, 3, 2))):
            body_ref[2 * f + half] = jnp.where(
                inner,
                news[out][0],
                jnp.where(
                    sub == 0,
                    roll(news[far][0], -1, 0),
                    jnp.where(sub == 7, roll(news[far][0], 1, 0), news[near][0]),
                ),
            )
            for kind in range(3):
                tips_ref[kind, 2 * f + half] = jnp.where(
                    inner,
                    news[near][kind],
                    jnp.where(sub < 2, roll(news[far][kind], -2, 0), roll(news[far][kind], 2, 0)),
                )

    def send(turn, carry):
        for k_owner in range(SENDS):
            owner = SENDS * turn + k_owner
            hit = parent_ref[2 * owner] == gz
            shift = jnp.where(hit, shift_ref[2 * owner], shift_ref[2 * owner + 1])
            kind = jnp.where(shift == 0, 1, jnp.where(shift == 120, 2, 0))
            for tile in range(TILES):
                total = None
                for j in range(PER_ROW):
                    k = tile * PER_ROW + j
                    if k >= OLD + 10:
                        break
                    amount = lax.rem(GROUP * j + 129 - shift, 128)
                    if k < OLD:
                        piece = pltpu.roll(old_pack_ref[kind, k], amount, 1)
                    else:
                        piece = jnp.where(
                            (lane == GROUP * j) | (lane == GROUP * j + 9),
                            pltpu.roll(tips_ref[kind, k - OLD], amount, 1),
                            pltpu.roll(body_ref[k - OLD], amount, 1),
                        )
                    total = piece if total is None else jnp.where(lane < GROUP * j, total, piece)
                if tile < TILES - 1:
                    message_ref[owner, 2 * tile] = total[0:4]
                    message_ref[owner, 2 * tile + 1] = total[4:8]
                else:
                    message_ref[owner, 2 * tile] = jnp.where(
                        iota(1, (4, 128)) < 60, total[0:4], roll(total, 60, 1)[4:8]
                    )
        return carry

    lax.fori_loop(0, 16 // SENDS, send, 0)


def fine_kernel(
    place_ref, got_ref, rho_ref, vel_ref, p_ref, out_ref, message_ref,
    mid_ref, tip_ref, ghost_ref, bound_ref,
):
    gz = place_ref[1]
    parent_ref = Table(place_ref, 2)
    lane, sub = iota(1), iota(0)
    part = lane % 16
    yc, xc = lane // 32, sub // 2
    parents = [parent_ref[2 * gz + box] for box in range(2)]

    for box in range(2):
        tiles = [
            jnp.concatenate([got_ref[parents[box], 2 * t], got_ref[parents[box], 2 * t + 1]])
            for t in range(TILES - 1)
        ]
        short = got_ref[parents[box], 2 * TILES - 2]
        tiles.append(jnp.concatenate([short, roll(short, -60, 1)]))
        for k in range(OLD + 10):
            j = k % PER_ROW
            tile = tiles[k // PER_ROW]
            at = GROUP * j + 1 + part // 2
            mid_ref[box, 8 * k : 8 * k + 8] = jnp.take_along_axis(tile, at, axis=1)
            at = GROUP * j + jnp.where(part < 8, 0, 9)
            tip_ref[box, 8 * k : 8 * k + 8] = jnp.take_along_axis(tile, at, axis=1)

    def every(ref, box, k, row, step=1):
        return ref[box, pl.ds(8 * k + row, 8, stride=8 * step)]

    def by_y(items):
        return jnp.where(
            yc < 2,
            jnp.where(yc == 0, items[0], items[1]),
            jnp.where(yc == 2, items[2], items[3]),
        )

    def spread(value, rows):
        return jnp.take_along_axis(value, rows, axis=0)

    side, low_y = (sub >= 4).astype(jnp.int32), lane < 64
    outer_x = (xc == 0) | (xc == 3)
    half_x = (xc >= 2).astype(jnp.int32)

    def old_parts(box):
        inside, along_x, along_y, along_z = [], [], [], []
        for f in range(5):
            if f % 2 == 0:
                middle = by_y([every(mid_ref, box, 4 * f, 2 + y) for y in range(4)])
                sides = jnp.where(low_y, every(mid_ref, box, 4 * f, 1), every(mid_ref, box, 4 * f, 6))
                tips = by_y([every(tip_ref, box, 4 * f, 2 + y) for y in range(4)])
            if f % 4 == 0:
                faces = by_y(
                    [every(mid_ref, box, 4 * f + y // 2, 7 * (y % 2), 2) for y in range(4)]
                )
            at = 4 * (f % 2) + xc
            inside.append(spread(middle, at))
            along_y.append(spread(sides, at))
            along_z.append(spread(tips, at))
            along_x.append(spread(faces, 2 * (f % 4) + side))
        return inside, [along_x, along_y, along_z]

    def new_parts(box):
        along_x, along_y, along_z = [], [], []
        for f in range(5):
            if f % 4 == 0:
                k = OLD + 2 * f
                faces = by_y([every(mid_ref, box, k, 2 + y) for y in range(4)])
                sides_near = jnp.where(low_y, every(mid_ref, box, k, 1), every(mid_ref, box, k, 6))
                sides_far = jnp.where(low_y, every(mid_ref, box, k, 0), every(mid_ref, box, k, 7))
                tips_near = by_y([every(tip_ref, box, k, 2 + y) for y in range(4)])
                tips_far = by_y([every(tip_ref, box, k, row) for row in (0, 1, 6, 7)])
            at = 2 * (f % 4) + half_x
            along_x.append(spread(faces, 2 * (f % 4) + side))
            along_y.append(jnp.where(outer_x, spread(sides_near, at), spread(sides_far, at)))
            along_z.append(jnp.where(outer_x, spread(tips_near, at), spread(tips_far, at)))
        return [along_x, along_y, along_z]

    directions = (
        (0, 1, sub == 0, sub == 7, 4, sub >= 4),
        (1, 16, lane < 16, lane >= 112, 64, lane >= 64),
        (1, 1, part == 0, part == 15, 8, part >= 8),
    )

    def changes(fields, step_index):
        total = None
        for normal, (axis, step, first, last, park, parked) in enumerate(directions):
            high, low, up = [[], []], [[], []], [[], []]
            for box in range(2):
                for f in range(5):
                    here, ghost = fields[box][f], ghost_ref[step_index, box, normal, f]
                    after = jnp.where(last, ghost, roll(here, -step, axis))
                    before = jnp.where(first, ghost, roll(here, step, axis))
                    one, other = edges(before, here, after)
                    high[box].append(one)
                    low[box].append(other)
                    up[box].append(jnp.where(last, ghost, roll(other, -step, axis)))
            right = [jnp.where(parked, roll(b, park, axis), a) for a, b in zip(low[0], low[1])]
            bottom = hllc([bound_ref[step_index, normal, f] for f in range(5)], right, normal)
            found = []
            for box in range(2):
                flux = hllc(high[box], up[box], normal)
                under = bottom if box == 0 else [roll(item, -park, axis) for item in bottom]
                found.append(
                    [a - jnp.where(first, b, roll(a, step, axis)) for a, b in zip(flux, under)]
                )
            total = (
                found
                if total is None
                else [[a + b for a, b in zip(t, g)] for t, g in zip(total, found)]
            )
        return total

    def keep(step_index, ghosts):
        for normal, (axis, _, _, _, park, parked) in enumerate(directions):
            for f in range(5):
                for box in range(2):
                    ghost_ref[step_index, box, normal, f] = ghosts[box][normal][f]
                bound_ref[step_index, normal, f] = jnp.where(
                    parked, roll(ghosts[1][normal][f], park, axis), ghosts[0][normal][f]
                )

    ghosts, states, later = [], [], []
    for box in range(2):
        inside, found = old_parts(box)
        ghosts.append(found)
        details = [rho_ref[box], vel_ref[0, box], vel_ref[1, box], vel_ref[2, box], p_ref[box]]
        states.append(conserved([a + b for a, b in zip(inside, details)]))
        later.append(
            [
                primitive([0.5 * (a + b) for a, b in zip(conserved(old), new)])
                for old, new in zip(found, new_parts(box))
            ]
        )
    keep(0, ghosts)
    keep(1, later)

    def stage(i, carry):
        start, state = carry
        again = lax.rem(i, 2) == 1
        weight = jnp.where(again, 0.5, 1.0).astype(F32)
        start = jax.tree.map(lambda a, b: jnp.where(again, a, b), start, state)
        moved = changes([primitive(item) for item in state], i // 2)
        state = jax.tree.map(
            lambda s, t, m: (1.0 - weight) * s + weight * (t - 0.05 * m), start, state, moved
        )
        return start, state

    _, states = lax.fori_loop(0, 4, stage, (states, states), unroll=4)
    for box in range(2):
        packed = None
        for f in range(5):
            value = states[box][f]
            out_ref[f, box] = value
            value = value + roll(value, -1, 0)
            value = value + roll(value, -1, 1)
            value = (value + roll(value, -16, 1)) * 0.125
            inside_lane = lane % 32
            at = (inside_lane // 8) * 32 + (inside_lane % 8) * 2
            value = jnp.take_along_axis(value, at, axis=1)
            if f == 0:
                packed = value
            elif f < 4:
                packed = jnp.where(lane // 32 == f, value, packed)
            else:
                packed = jnp.where((sub % 2 == 1) & (lane < 32), roll(value, 1, 0), packed)
        message_ref[parents[box]] = packed


def final_kernel(place_ref, new_ref, got_ref, out_ref, sum_ref):
    gz = place_ref[1]
    parent_ref, shift_ref = Table(place_ref, 2), Table(place_ref, 34)
    lane = iota(1)

    def add(turn, carry):
        count, sums = carry
        for k_owner in range(ADDS):
            owner = ADDS * turn + k_owner
            hit = parent_ref[2 * owner] == gz
            other = parent_ref[2 * owner + 1] == gz
            shift = jnp.where(hit, shift_ref[2 * owner], shift_ref[2 * owner + 1])
            shift = jnp.where(hit | other, shift, 256)
            inside = (lane >= shift) & (lane < shift + 8)
            value = got_ref[owner]
            count = count + jnp.where(inside, 1.0, 0.0)
            sums = [
                item
                + jnp.where(inside, pltpu.roll(value, lax.rem(shift + 128 - 8 * k, 128), 1), 0.0)
                for k, item in enumerate(sums)
            ]
        return count, sums

    zero = jnp.zeros((8, 128), F32)
    count, sums = lax.fori_loop(0, 16 // ADDS, add, (zero, [zero] * 16))
    share = inverse(jnp.maximum(count, 1.0))
    for k in range(16):
        sum_ref[8 * k : 8 * k + 8] = sums[k] * share
    for f in range(5):
        for x in range(4):
            start = (0 if f == 4 else 32 * f) + 2 * x + (1 if f == 4 else 0)
            value = sum_ref[pl.ds(start, 4, stride=8)]
            out_ref[f, x] = jnp.where(count[0:4] > 0.0, value, new_ref[f, x])


FINE_SCRATCH = ((2, 352, 128), (2, 352, 128), (2, 2, 3, 5, 8, 128), (2, 3, 5, 8, 128))


def shape(*dims):
    return jax.ShapeDtypeStruct(dims, F32)


def call(kernel, outs, scalars, arrays, scratch=()):
    return pl.pallas_call(
        kernel,
        out_shape=outs,
        in_specs=[pl.BlockSpec(memory_space=pltpu.SMEM)] * scalars
        + [pl.BlockSpec(memory_space=pltpu.VMEM)] * arrays,
        out_specs=jax.tree.map(lambda _: pl.BlockSpec(memory_space=pltpu.VMEM), outs),
        scratch_shapes=[pltpu.VMEM(dims, F32) for dims in scratch],
        compiler_params=pltpu.CompilerParams(vmem_limit_bytes=32 * 1024 * 1024),
    )


def shifted(value, axis, step):
    size = lax.axis_size(axis)
    return lax.ppermute(value, axis, [(i, (i + step) % size) for i in range(size)])


def on_device(
    density, velocity, pressure, fine_density, fine_velocity, fine_pressure, box_parent, box_shift
):
    assert density.shape == (4, 4, 128) and fine_density.shape == (1, 1, 2, 8, 128)
    place = jnp.stack([lax.axis_index("gy"), lax.axis_index("gz")]).astype(jnp.int32)
    place = jnp.concatenate([place, box_parent.reshape(32), box_shift.reshape(32)])
    prim = jnp.concatenate([density[None], velocity, pressure[None]])
    ends, for_up = call(ends_kernel, (shape(5, 4, 128), shape(10, 4, 128)), 0, 1)(prim)
    before, after = shifted(ends, "gz", 1), shifted(ends, "gz", -1)
    far_prior = shifted(for_up, "gx", 2)
    block, for_down = call(block_kernel, (shape(4, 25, 4, 128), shape(10, 4, 128)), 1, 5)(
        place, ends, before, after, prim, far_prior
    )
    own = lax.all_to_all(block, "gy", 0, 0, tiled=True)
    far_next = shifted(for_down, "gx", -2)
    for_up, for_down = call(near_kernel, (shape(60, 4, 128), shape(60, 4, 128)), 1, 2)(
        place, own, far_next
    )
    prior, following = shifted(for_up, "gx", 1), shifted(for_down, "gx", -1)
    updated, message = call(
        coarse_kernel,
        (shape(5, 4, 4, 128), shape(16, 2 * TILES - 1, 4, 128)),
        1,
        5,
        (
            (70, 16, 128),
            (25, 16, 128),
            (50, 16, 128),
            (15, 16, 128),
            (30, 8, 128),
            (15, 8, 128),
            (3, 20, 8, 128),
            (10, 8, 128),
            (3, 10, 8, 128),
        ),
    )(place, own, prior, following, far_prior, far_next)
    got = lax.all_to_all(message, "gz", 0, 0, tiled=True)
    fine, means = call(
        fine_kernel,
        (shape(5, 2, 8, 128), shape(16, 8, 128)),
        1,
        4,
        FINE_SCRATCH,
    )(
        place,
        got,
        fine_density.reshape(2, 8, 128),
        fine_velocity.reshape(3, 2, 8, 128),
        fine_pressure.reshape(2, 8, 128),
    )
    incoming = lax.all_to_all(means, "gz", 0, 0, tiled=True)
    coarse = call(final_kernel, shape(5, 4, 4, 128), 1, 2, ((128, 128),))(place, updated, incoming)
    return coarse, fine.reshape(5, 1, 1, 2, 8, 128)


def solution(mesh):
    in_specs = (
        P("gx", "gy", "gz"),
        P(None, "gx", "gy", "gz"),
        P("gx", "gy", "gz"),
        P("gx", "gy", "gz", None, None),
        P(None, "gx", "gy", "gz", None, None),
        P("gx", "gy", "gz", None, None),
        P("gx", "gy", None, None),
        P("gx", "gy", None),
    )
    out_specs = (P(None, "gx", "gy", "gz"), P(None, "gx", "gy", "gz", None, None))
    return jax.shard_map(
        on_device, mesh=mesh, in_specs=in_specs, out_specs=out_specs, check_vma=False
    )
```

```python
import jax
import jax.numpy as jnp
from jax import lax
from jax.experimental import pallas as pl
from jax.experimental.pallas import tpu as pltpu
from jax.sharding import PartitionSpec as P

F32 = jnp.float32
GROUP = 10
PER_ROW = 12
OLD = 20
TILES = 3
FIRST, SECOND = 2, 3
SENDS, ADDS = 8, 16


def iota(dim, shape=(8, 128)):
    return lax.broadcasted_iota(jnp.int32, shape, dim)


class Table:
    def __init__(self, ref, base):
        self.ref, self.base = ref, base

    def __getitem__(self, k):
        return self.ref[self.base + k]


def roll(value, shift, axis):
    size = value.shape[axis]
    shift = shift % size
    return value if shift == 0 else pltpu.roll(value, shift, axis)


def inverse(value):
    guess = pl.reciprocal(value, approx=True)
    return guess * (2.0 - value * guess)


def root(value):
    return value * lax.rsqrt(jnp.maximum(value, 1e-30))


def conserved(prim):
    rho, u, v, w, p = prim
    return [rho, rho * u, rho * v, rho * w, 2.5 * p + 0.5 * rho * (u * u + v * v + w * w)]


def primitive(cons):
    inv = inverse(cons[0])
    u, v, w = cons[1] * inv, cons[2] * inv, cons[3] * inv
    p = 0.4 * (cons[4] - 0.5 * (cons[1] * u + cons[2] * v + cons[3] * w))
    return [cons[0], u, v, w, p]


def edges(before, here, after):
    down, up = here - before, after - here
    half = 0.5 * (
        jnp.maximum(jnp.minimum(down, up), 0.0) + jnp.minimum(jnp.maximum(down, up), 0.0)
    )
    return here + half, here - half


def hllc(left, right, normal):
    order = [0, 1 + normal] + [1 + d for d in range(3) if d != normal] + [4]
    rho_l, un_l, ut_l, us_l, p_l = [left[k] for k in order]
    rho_r, un_r, ut_r, us_r, p_r = [right[k] for k in order]
    a_l, a_r = p_l * inverse(rho_l), p_r * inverse(rho_r)
    c_l, c_r = root(1.4 * a_l), root(1.4 * a_r)
    s_l = jnp.minimum(un_l - c_l, un_r - c_r)
    s_r = jnp.maximum(un_l + c_l, un_r + c_r)
    m_l, m_r = rho_l * (s_l - un_l), rho_r * (s_r - un_r)
    star = (p_r - p_l + m_l * un_l - m_r * un_r) * inverse(m_l - m_r)
    side = (s_l >= 0.0) | (star >= 0.0)
    pick = lambda one, other: jnp.where(side, one, other)
    rho, un, ut, us, p = (
        pick(rho_l, rho_r),
        pick(un_l, un_r),
        pick(ut_l, ut_r),
        pick(us_l, us_r),
        pick(p_l, p_r),
    )
    a, m, s = pick(a_l, a_r), pick(m_l, m_r), pick(s_l, s_r)
    limited = pick(jnp.minimum(s_l, 0.0), jnp.maximum(s_r, 0.0))
    e = 2.5 * a + 0.5 * (un * un + ut * ut + us * us)
    energy = rho * e
    r = inverse(s - star)
    factor = m * r
    momentum = rho * un
    mass = momentum + limited * (factor - rho)
    force = momentum * un + p + limited * (factor * star - momentum)
    power = (energy + p) * un + limited * (
        factor * e + (star - un) * (factor * star + p * r) - energy
    )
    result = [None] * 5
    for k, part in zip(order, [mass, force, ut * mass, us * mass, power]):
        result[k] = part
    return result


def line_change(fields, axis, normal, wide=None):
    high, low = [], []
    for k in range(5):
        here = fields[k]
        if wide is None:
            after, before = roll(here, -1, axis), roll(here, 1, axis)
        else:
            after, before = roll(wide[k], -1, axis)[0:8], roll(wide[k], 1, axis)[0:8]
        one, other = edges(before, here, after)
        high.append(one)
        low.append(roll(other, -1, axis))
    flux = hllc(high, low, normal)
    return [part - roll(part, 1, axis) for part in flux]


def next_group(tiles, j):
    lane = iota(1, tiles[j][0].shape)
    other = tiles[j + 1] if j + 1 < len(tiles) and tiles[j + 1] is not None else tiles[j]
    return [jnp.where(lane < 96, roll(a, -32, 1), roll(b, -32, 1)) for a, b in zip(tiles[j], other)]


def prior_group(tiles, j):
    lane = iota(1, tiles[j][0].shape)
    other = tiles[j - 1] if j > 0 and tiles[j - 1] is not None else tiles[j]
    return [jnp.where(lane >= 32, roll(a, 32, 1), roll(b, 32, 1)) for a, b in zip(tiles[j], other)]


def group_changes(tiles, wanted):
    high, low, flux = [None] * len(tiles), [None] * len(tiles), [None] * len(tiles)
    for j in wanted:
        pairs = [
            edges(before, here, after)
            for before, here, after in zip(prior_group(tiles, j), tiles[j], next_group(tiles, j))
        ]
        high[j] = [pair[0] for pair in pairs]
        low[j] = [pair[1] for pair in pairs]
    for j in wanted:
        flux[j] = hllc(high[j], next_group(low, j), 0)
    return {
        j: [a - b for a, b in zip(flux[j], prior_group(flux, j))] for j in wanted
    }


def ends_kernel(prim_ref, out_ref):
    lane = iota(1, (4, 128))
    for f in range(5):
        total = None
        for x in range(4):
            row = prim_ref[f, x]
            part = lane - 32 * x
            first = roll(row, 32 * x + 8, 1)
            last = roll(row, 32 * x + 24, 1)
            piece = jnp.where(part < 16, first, last)
            total = piece if total is None else jnp.where(part < 0, total, piece)
        out_ref[f] = total


def block_kernel(_, ends_ref, before_ref, after_ref, prim_ref, out_ref, up_ref, down_ref):
    lane = iota(1, (4, 128)) % 32
    for f in range(5):
        edge = jnp.where(
            lane < 8,
            roll(before_ref[f], -16, 1),
            jnp.where(lane >= 24, roll(after_ref[f], 16, 1), ends_ref[f]),
        )
        for copy in range(4):
            out_ref[copy, 20 + f] = edge
            for x in range(4):
                out_ref[copy, 5 * x + f] = prim_ref[f, x]
        for ref, x in ((up_ref, 3), (down_ref, 0)):
            ref[f] = prim_ref[f, x]
            ref[5 + f] = edge


def near_kernel(place_ref, own_ref, _, __, up_ref, down_ref):
    gy = place_ref[0]
    over, under = lax.rem(gy + 1, 4), lax.rem(gy + 3, 4)
    for ref, xs in ((up_ref, (3, 2, 1, 0)), (down_ref, (0, 1, 2, 3))):

        def take(block, distance):
            start = 5 * xs[distance - 1] if distance else 20
            return own_ref[block, start : start + 5]

        for k, distance in ((0, 1), (9, 0)):
            for j, block in enumerate((gy, over, under)):
                ref[5 * (k + j) : 5 * (k + j) + 5] = take(block, distance)
        for k, distance in ((3, 3), (5, 2), (6, 4)):
            ref[5 * k : 5 * k + 5] = take(gy, distance)
        ref[20:25, 0:2] = take(under, 3)[:, 2:4]
        ref[20:25, 2:4] = take(over, 3)[:, 0:2]
        ref[35:40, 0:3] = take(under, 2)[:, 1:4]
        ref[35:40, 3:4] = take(under, 4)[:, 3:4]
        ref[40:45, 0:3] = take(over, 2)[:, 0:3]
        ref[40:45, 3:4] = take(over, 4)[:, 0:1]


def coarse_kernel(
    place_ref, own_ref, prior_ref, next_ref, far_prior_ref, far_next_ref,
    new_ref, message_ref,
    prim_ref, edge_ref, section_ref, section_edge_ref, made_ref, made_edge_ref,
    old_pack_ref, body_ref, tips_ref,
):
    gy, gz = place_ref[0], place_ref[1]
    parent_ref, shift_ref = Table(place_ref, 2), Table(place_ref, 34)
    for k in range(4):
        source = lax.rem(gy + k, 4)
        rows, tips = own_ref[source, 0:20], own_ref[source, 20:25]
        for ref, base, count, value in ((prim_ref, 25, 20, rows), (edge_ref, 10, 5, tips)):
            if k < 3:
                ref[base : base + count, 2 + 4 * k : 6 + 4 * k] = value
            else:
                ref[base : base + count, 14:16] = value[:, 0:2]
                ref[base : base + count, 0:2] = value[:, 2:4]
    for got_ref, tile, bases in (
        (prior_ref, 5, (20, 15, 10, 5)),
        (next_ref, 15, (45, 50, 55, 60)),
    ):
        got = [got_ref[5 * k : 5 * k + 5] for k in range(12)]
        for ref, base, first in ((prim_ref, bases[0], 0), (edge_ref, tile, 9)):
            ref[base : base + 5, 2:6] = got[first]
            ref[base : base + 5, 6:10] = got[first + 1]
            ref[base : base + 5, 14:16] = got[first + 2][:, 0:2]
            ref[base : base + 5, 0:2] = got[first + 2][:, 2:4]
        for base, first in ((bases[2], 3), (bases[1], 5), (bases[3], 6)):
            prim_ref[base : base + 5, 2:6] = got[first]
        prim_ref[bases[2] : bases[2] + 5, 0:2] = got[4][:, 0:2]
        prim_ref[bases[2] : bases[2] + 5, 6:8] = got[4][:, 2:4]
        prim_ref[bases[1] : bases[1] + 5, 15:16] = got[7][:, 0:1]
        prim_ref[bases[1] : bases[1] + 5, 0:2] = got[7][:, 1:3]
        prim_ref[bases[1] : bases[1] + 5, 6:9] = got[8][:, 0:3]
        prim_ref[bases[3] : bases[3] + 5, 1:2] = got[7][:, 3:4]
        prim_ref[bases[3] : bases[3] + 5, 6:7] = got[8][:, 3:4]
    prim_ref[0:5, 2:6] = far_prior_ref[0:5]
    edge_ref[0:5, 2:6] = far_prior_ref[5:10]
    prim_ref[65:70, 2:6] = far_next_ref[0:5]
    edge_ref[20:25, 2:6] = far_next_ref[5:10]

    def prim_row(x):
        return [prim_ref[5 * (x + 5) + f] for f in range(5)]

    def section_row(x, rows=16):
        return [section_ref[5 * (x + 3) + f, 0:rows] for f in range(5)]

    def sweep(row, start, rows, at_once, emit):
        def pairs_of(x):
            found = [edges(b, h, a) for b, h, a in zip(row(x - 1), row(x), row(x + 1))]
            return [pair[0] for pair in found], [pair[1] for pair in found]

        def step(i, carry):
            high, flux = carry
            for k in range(at_once):
                x = start + i * at_once + k
                high_next, low = pairs_of(x + 1)
                flux_next = hllc(high, low, 0)
                emit(x, [after - before for before, after in zip(flux, flux_next)])
                high, flux = high_next, flux_next
            return high, flux

        high_before, _ = pairs_of(start - 1)
        high, low = pairs_of(start)
        lax.fori_loop(0, rows // at_once, step, (high, hllc(high_before, low, 0)))

    def section_of(x, by_x):
        middle = prim_row(x)
        by_y = line_change(middle, 0, 1)
        by_z = line_change(middle, 1, 2)
        state = conserved(middle)
        section = [state[f] - 0.05 * (by_x[f] + by_y[f] + by_z[f]) for f in range(5)]
        for f, value in enumerate(primitive(section)):
            section_ref[5 * (x + 3) + f] = value

    sweep(prim_row, -3, 10, FIRST, section_of)
    tiles = [[edge_ref[5 * t + f] for f in range(5)] for t in range(5)]
    by_x = group_changes(tiles, (1, 2, 3))
    for t in (1, 2, 3):
        by_y = line_change(tiles[t], 0, 1)
        by_z = line_change(tiles[t], 1, 2)
        state = conserved(tiles[t])
        section = [state[f] - 0.05 * (by_x[t][f] + by_y[f] + by_z[f]) for f in range(5)]
        for f, value in enumerate(primitive(section)):
            section_edge_ref[5 * (t - 1) + f] = value

    def advance(old, here, changes):
        start, state = conserved(old), conserved(here)
        return [
            0.5 * start[f] + 0.5 * (state[f] - 0.05 * (changes[0][f] + changes[1][f] + changes[2][f]))
            for f in range(5)
        ]

    def updated_of(x, by_x):
        middle = section_row(x, 8)
        by_y = line_change(middle, 0, 1, section_row(x))
        by_z = line_change(middle, 1, 2)
        old = [part[0:8] for part in prim_row(x)]
        for f, value in enumerate(advance(old, middle, (by_x, by_y, by_z))):
            made_ref[5 * (x + 1) + f] = value

    sweep(lambda x: section_row(x, 8), -1, 6, SECOND, updated_of)
    wide = [[section_edge_ref[5 * t + f] for f in range(5)] for t in range(3)]
    tiles = [[part[0:8] for part in tile] for tile in wide]
    by_x = group_changes(tiles, (0, 1, 2))
    for t in range(3):
        by_y = line_change(tiles[t], 0, 1, wide[t])
        by_z = line_change(tiles[t], 1, 2)
        old = [edge_ref[5 * (t + 1) + f, 0:8] for f in range(5)]
        for f, value in enumerate(advance(old, tiles[t], (by_x[t], by_y, by_z))):
            made_edge_ref[5 * t + f] = value

    lane, sub = iota(1), iota(0)

    def spot(x):
        return (0, 3) if x < 0 else ((2, 0) if x > 3 else (1, x))

    for f in range(5):
        olds, news = {}, {}
        for x in range(-1, 5):
            tile, group = spot(x)
            main = prim_ref[5 * (x + 5) + f, 0:8]
            tips = edge_ref[5 * (tile + 1) + f, 0:8]
            under, over = roll(tips, -32 * group - 8, 1), roll(tips, 104 - 32 * group, 1)
            olds[x] = (main, jnp.where(lane == 127, under, main), jnp.where(lane == 0, over, main))
            main, tips = made_ref[5 * (x + 1) + f], made_edge_ref[5 * tile + f]
            under, over = roll(tips, -32 * group - 8, 1), roll(tips, 104 - 32 * group, 1)
            main = jnp.where(lane < 4, under, jnp.where(lane >= 124, over, main))
            news[x] = (main, jnp.where(lane == 127, under, main), jnp.where(lane == 0, over, main))
            if 0 <= x < 4:
                new_ref[f, x] = main[2:6]
        inner = (sub >= 2) & (sub < 6)
        for x in range(4):
            face = olds[-1 if x < 2 else 4][0]
            top, bottom = (-2, 4) if x % 2 == 0 else (-4, 2)
            for kind in range(3):
                old_pack_ref[kind, 4 * f + x] = roll(jnp.where(
                    sub == 0,
                    roll(face, top, 0),
                    jnp.where(sub == 7, roll(face, bottom, 0), olds[x][kind]),
                ), GROUP * ((4 * f + x) % PER_ROW), 1)
        for half, (out, near, far) in enumerate(((-1, 0, 1), (4, 3, 2))):
            body_ref[2 * f + half] = roll(jnp.where(
                inner,
                news[out][0],
                jnp.where(
                    sub == 0,
                    roll(news[far][0], -1, 0),
                    jnp.where(sub == 7, roll(news[far][0], 1, 0), news[near][0]),
                ),
            ), GROUP * ((OLD + 2 * f + half) % PER_ROW), 1)
            for kind in range(3):
                tips_ref[kind, 2 * f + half] = roll(jnp.where(
                    inner,
                    news[near][kind],
                    jnp.where(sub < 2, roll(news[far][kind], -2, 0), roll(news[far][kind], 2, 0)),
                ), GROUP * ((OLD + 2 * f + half) % PER_ROW), 1)

    def send(turn, carry):
        for k_owner in range(SENDS):
            owner = SENDS * turn + k_owner
            hit = parent_ref[2 * owner] == gz
            shift = jnp.where(hit, shift_ref[2 * owner], shift_ref[2 * owner + 1])
            kind = jnp.where(shift == 0, 1, jnp.where(shift == 120, 2, 0))
            place = (lane + (129 - shift)) & 127
            group = (place * 205) >> 11
            within = place - GROUP * group
            ends = (within == 0) | (within == GROUP - 1)
            for tile in range(TILES):
                total = None
                for j in range(PER_ROW):
                    k = tile * PER_ROW + j
                    if k >= OLD + 10:
                        break
                    if k < OLD:
                        piece = old_pack_ref[kind, k]
                    else:
                        piece = jnp.where(ends, tips_ref[kind, k - OLD], body_ref[k - OLD])
                    total = piece if total is None else jnp.where(group == j, piece, total)
                total = pltpu.roll(total, lax.rem(129 - shift, 128), 1)
                if tile < TILES - 1:
                    message_ref[owner, 2 * tile] = total[0:4]
                    message_ref[owner, 2 * tile + 1] = total[4:8]
                else:
                    message_ref[owner, 2 * tile] = jnp.where(
                        iota(1, (4, 128)) < 60, total[0:4], roll(total, 60, 1)[4:8]
                    )
        return carry

    lax.fori_loop(0, 16 // SENDS, send, 0)


def fine_kernel(
    place_ref, got_ref, rho_ref, vel_ref, p_ref, out_ref, message_ref,
    mid_ref, tip_ref, ghost_ref, bound_ref,
):
    gz = place_ref[1]
    parent_ref = Table(place_ref, 2)
    lane, sub = iota(1), iota(0)
    part = lane % 16
    yc, xc = lane // 32, sub // 2
    parents = [parent_ref[2 * gz + box] for box in range(2)]

    for box in range(2):
        tiles = [
            jnp.concatenate([got_ref[parents[box], 2 * t], got_ref[parents[box], 2 * t + 1]])
            for t in range(TILES - 1)
        ]
        short = got_ref[parents[box], 2 * TILES - 2]
        tiles.append(jnp.concatenate([short, roll(short, -60, 1)]))
        for k in range(OLD + 10):
            j = k % PER_ROW
            tile = tiles[k // PER_ROW]
            at = GROUP * j + 1 + part // 2
            mid_ref[box, 8 * k : 8 * k + 8] = jnp.take_along_axis(tile, at, axis=1)
            at = GROUP * j + jnp.where(part < 8, 0, 9)
            tip_ref[box, 8 * k : 8 * k + 8] = jnp.take_along_axis(tile, at, axis=1)

    def every(ref, box, k, row, step=1):
        return ref[box, pl.ds(8 * k + row, 8, stride=8 * step)]

    def by_y(items):
        return jnp.where(
            yc < 2,
            jnp.where(yc == 0, items[0], items[1]),
            jnp.where(yc == 2, items[2], items[3]),
        )

    def spread(value, rows):
        return jnp.take_along_axis(value, rows, axis=0)

    side, low_y = (sub >= 4).astype(jnp.int32), lane < 64
    outer_x = (xc == 0) | (xc == 3)
    half_x = (xc >= 2).astype(jnp.int32)

    def old_parts(box):
        inside, along_x, along_y, along_z = [], [], [], []
        for f in range(5):
            if f % 2 == 0:
                middle = by_y([every(mid_ref, box, 4 * f, 2 + y) for y in range(4)])
                sides = jnp.where(low_y, every(mid_ref, box, 4 * f, 1), every(mid_ref, box, 4 * f, 6))
                tips = by_y([every(tip_ref, box, 4 * f, 2 + y) for y in range(4)])
            if f % 4 == 0:
                faces = by_y(
                    [every(mid_ref, box, 4 * f + y // 2, 7 * (y % 2), 2) for y in range(4)]
                )
            at = 4 * (f % 2) + xc
            inside.append(spread(middle, at))
            along_y.append(spread(sides, at))
            along_z.append(spread(tips, at))
            along_x.append(spread(faces, 2 * (f % 4) + side))
        return inside, [along_x, along_y, along_z]

    def new_parts(box):
        along_x, along_y, along_z = [], [], []
        for f in range(5):
            if f % 4 == 0:
                k = OLD + 2 * f
                faces = by_y([every(mid_ref, box, k, 2 + y) for y in range(4)])
                sides_near = jnp.where(low_y, every(mid_ref, box, k, 1), every(mid_ref, box, k, 6))
                sides_far = jnp.where(low_y, every(mid_ref, box, k, 0), every(mid_ref, box, k, 7))
                tips_near = by_y([every(tip_ref, box, k, 2 + y) for y in range(4)])
                tips_far = by_y([every(tip_ref, box, k, row) for row in (0, 1, 6, 7)])
            at = 2 * (f % 4) + half_x
            along_x.append(spread(faces, 2 * (f % 4) + side))
            along_y.append(jnp.where(outer_x, spread(sides_near, at), spread(sides_far, at)))
            along_z.append(jnp.where(outer_x, spread(tips_near, at), spread(tips_far, at)))
        return [along_x, along_y, along_z]

    directions = (
        (0, 1, sub == 0, sub == 7, 4, sub >= 4),
        (1, 16, lane < 16, lane >= 112, 64, lane >= 64),
        (1, 1, part == 0, part == 15, 8, part >= 8),
    )

    def changes(fields, step_index):
        total = None
        for normal, (axis, step, first, last, park, parked) in enumerate(directions):
            high, low, up = [[], []], [[], []], [[], []]
            for box in range(2):
                for f in range(5):
                    here, ghost = fields[box][f], ghost_ref[step_index, box, normal, f]
                    after = jnp.where(last, ghost, roll(here, -step, axis))
                    before = jnp.where(first, ghost, roll(here, step, axis))
                    one, other = edges(before, here, after)
                    high[box].append(one)
                    low[box].append(other)
                    up[box].append(jnp.where(last, ghost, roll(other, -step, axis)))
            right = [jnp.where(parked, roll(b, park, axis), a) for a, b in zip(low[0], low[1])]
            bottom = hllc([bound_ref[step_index, normal, f] for f in range(5)], right, normal)
            found = []
            for box in range(2):
                flux = hllc(high[box], up[box], normal)
                under = bottom if box == 0 else [roll(item, -park, axis) for item in bottom]
                found.append(
                    [a - jnp.where(first, b, roll(a, step, axis)) for a, b in zip(flux, under)]
                )
            total = (
                found
                if total is None
                else [[a + b for a, b in zip(t, g)] for t, g in zip(total, found)]
            )
        return total

    def keep(step_index, ghosts):
        for normal, (axis, _, _, _, park, parked) in enumerate(directions):
            for f in range(5):
                for box in range(2):
                    ghost_ref[step_index, box, normal, f] = ghosts[box][normal][f]
                bound_ref[step_index, normal, f] = jnp.where(
                    parked, roll(ghosts[1][normal][f], park, axis), ghosts[0][normal][f]
                )

    ghosts, states, later = [], [], []
    for box in range(2):
        inside, found = old_parts(box)
        ghosts.append(found)
        details = [rho_ref[box], vel_ref[0, box], vel_ref[1, box], vel_ref[2, box], p_ref[box]]
        states.append(conserved([a + b for a, b in zip(inside, details)]))
        later.append(
            [
                primitive([0.5 * (a + b) for a, b in zip(conserved(old), new)])
                for old, new in zip(found, new_parts(box))
            ]
        )
    keep(0, ghosts)
    keep(1, later)

    def stage(i, carry):
        start, state = carry
        again = lax.rem(i, 2) == 1
        weight = jnp.where(again, 0.5, 1.0).astype(F32)
        start = jax.tree.map(lambda a, b: jnp.where(again, a, b), start, state)
        moved = changes([primitive(item) for item in state], i // 2)
        state = jax.tree.map(
            lambda s, t, m: (1.0 - weight) * s + weight * (t - 0.05 * m), start, state, moved
        )
        return start, state

    _, states = lax.fori_loop(0, 4, stage, (states, states), unroll=4)
    for box in range(2):
        packed = None
        for f in range(5):
            value = states[box][f]
            out_ref[f, box] = value
            value = value + roll(value, -1, 0)
            value = value + roll(value, -1, 1)
            value = (value + roll(value, -16, 1)) * 0.125
            inside_lane = lane % 32
            at = (inside_lane // 8) * 32 + (inside_lane % 8) * 2
            value = jnp.take_along_axis(value, at, axis=1)
            if f == 0:
                packed = value
            elif f < 4:
                packed = jnp.where(lane // 32 == f, value, packed)
            else:
                packed = jnp.where((sub % 2 == 1) & (lane < 32), roll(value, 1, 0), packed)
        message_ref[parents[box]] = packed


def final_kernel(place_ref, new_ref, got_ref, out_ref, sum_ref):
    gz = place_ref[1]
    parent_ref, shift_ref = Table(place_ref, 2), Table(place_ref, 34)
    lane = iota(1)

    def add(turn, carry):
        count, sums = carry
        for k_owner in range(ADDS):
            owner = ADDS * turn + k_owner
            hit = parent_ref[2 * owner] == gz
            other = parent_ref[2 * owner + 1] == gz
            shift = jnp.where(hit, shift_ref[2 * owner], shift_ref[2 * owner + 1])
            shift = jnp.where(hit | other, shift, 256)
            count = count + jnp.where((lane >= shift) & (lane < shift + 8), 1.0, 0.0)
            value = pltpu.roll(got_ref[owner], lax.rem(shift, 128), 1)
            group = jnp.where(shift < 256, ((lane + (256 - shift)) & 127) >> 3, 16)
            sums = [item + jnp.where(group == k, value, 0.0) for k, item in enumerate(sums)]
        return count, sums

    zero = jnp.zeros((8, 128), F32)
    count, sums = lax.fori_loop(0, 16 // ADDS, add, (zero, [zero] * 16))
    share = inverse(jnp.maximum(count, 1.0))
    for k in range(16):
        sum_ref[8 * k : 8 * k + 8] = roll(sums[k], -8 * k, 1) * share
    for f in range(5):
        for x in range(4):
            start = (0 if f == 4 else 32 * f) + 2 * x + (1 if f == 4 else 0)
            value = sum_ref[pl.ds(start, 4, stride=8)]
            out_ref[f, x] = jnp.where(count[0:4] > 0.0, value, new_ref[f, x])


FINE_SCRATCH = ((2, 352, 128), (2, 352, 128), (2, 2, 3, 5, 8, 128), (2, 3, 5, 8, 128))


def shape(*dims):
    return jax.ShapeDtypeStruct(dims, F32)


def call(kernel, outs, scalars, arrays, scratch=()):
    return pl.pallas_call(
        kernel,
        out_shape=outs,
        in_specs=[pl.BlockSpec(memory_space=pltpu.SMEM)] * scalars
        + [pl.BlockSpec(memory_space=pltpu.VMEM)] * arrays,
        out_specs=jax.tree.map(lambda _: pl.BlockSpec(memory_space=pltpu.VMEM), outs),
        scratch_shapes=[pltpu.VMEM(dims, F32) for dims in scratch],
        compiler_params=pltpu.CompilerParams(vmem_limit_bytes=32 * 1024 * 1024),
    )


def shifted(value, axis, step):
    size = lax.axis_size(axis)
    return lax.ppermute(value, axis, [(i, (i + step) % size) for i in range(size)])


def on_device(
    density, velocity, pressure, fine_density, fine_velocity, fine_pressure, box_parent, box_shift
):
    assert density.shape == (4, 4, 128) and fine_density.shape == (1, 1, 2, 8, 128)
    place = jnp.stack([lax.axis_index("gy"), lax.axis_index("gz")]).astype(jnp.int32)
    place = jnp.concatenate([place, box_parent.reshape(32), box_shift.reshape(32)])
    prim = jnp.concatenate([density[None], velocity, pressure[None]])
    ends = call(ends_kernel, shape(5, 4, 128), 0, 1)(prim)
    before, after = shifted(ends, "gz", 1), shifted(ends, "gz", -1)
    block, for_up, for_down = call(
        block_kernel, (shape(4, 25, 4, 128), shape(10, 4, 128), shape(10, 4, 128)), 1, 4
    )(place, ends, before, after, prim)
    own = lax.all_to_all(block, "gy", 0, 0, tiled=True)
    far_prior, far_next = shifted(for_up, "gx", 2), shifted(for_down, "gx", -2)
    for_up, for_down = call(near_kernel, (shape(60, 4, 128), shape(60, 4, 128)), 1, 3)(
        place, own, far_prior, far_next
    )
    prior, following = shifted(for_up, "gx", 1), shifted(for_down, "gx", -1)
    updated, message = call(
        coarse_kernel,
        (shape(5, 4, 4, 128), shape(16, 2 * TILES - 1, 4, 128)),
        1,
        5,
        (
            (70, 16, 128),
            (25, 16, 128),
            (50, 16, 128),
            (15, 16, 128),
            (30, 8, 128),
            (15, 8, 128),
            (3, 20, 8, 128),
            (10, 8, 128),
            (3, 10, 8, 128),
        ),
    )(place, own, prior, following, far_prior, far_next)
    got = lax.all_to_all(message, "gz", 0, 0, tiled=True)
    fine, means = call(
        fine_kernel,
        (shape(5, 2, 8, 128), shape(16, 8, 128)),
        1,
        4,
        FINE_SCRATCH,
    )(
        place,
        got,
        fine_density.reshape(2, 8, 128),
        fine_velocity.reshape(3, 2, 8, 128),
        fine_pressure.reshape(2, 8, 128),
    )
    incoming = lax.all_to_all(means, "gz", 0, 0, tiled=True)
    coarse = call(final_kernel, shape(5, 4, 4, 128), 1, 2, ((128, 128),))(place, updated, incoming)
    return coarse, fine.reshape(5, 1, 1, 2, 8, 128)


def solution(mesh):
    in_specs = (
        P("gx", "gy", "gz"),
        P(None, "gx", "gy", "gz"),
        P("gx", "gy", "gz"),
        P("gx", "gy", "gz", None, None),
        P(None, "gx", "gy", "gz", None, None),
        P("gx", "gy", "gz", None, None),
        P("gx", "gy", None, None),
        P("gx", "gy", None),
    )
    out_specs = (P(None, "gx", "gy", "gz"), P(None, "gx", "gy", "gz", None, None))
    return jax.shard_map(
        on_device, mesh=mesh, in_specs=in_specs, out_specs=out_specs, check_vma=False
    )
```

```python
import jax
import jax.numpy as jnp
from jax import lax
from jax.experimental import pallas as pl
from jax.experimental.pallas import tpu as pltpu
from jax.sharding import PartitionSpec as P

F32 = jnp.float32
GROUP = 10
PER_ROW = 12
OLD = 20
TILES = 3
FIRST, SECOND = 2, 3
SENDS, ADDS = 8, 16


def iota(dim, shape=(8, 128)):
    return lax.broadcasted_iota(jnp.int32, shape, dim)


class Table:
    def __init__(self, ref, base):
        self.ref, self.base = ref, base

    def __getitem__(self, k):
        return self.ref[self.base + k]


def roll(value, shift, axis):
    size = value.shape[axis]
    shift = shift % size
    return value if shift == 0 else pltpu.roll(value, shift, axis)


def inverse(value):
    guess = pl.reciprocal(value, approx=True)
    return guess * (2.0 - value * guess)


def root(value):
    return value * lax.rsqrt(jnp.maximum(value, 1e-30))


def conserved(prim):
    rho, u, v, w, p = prim
    return [rho, rho * u, rho * v, rho * w, 2.5 * p + 0.5 * rho * (u * u + v * v + w * w)]


def primitive(cons):
    inv = inverse(cons[0])
    u, v, w = cons[1] * inv, cons[2] * inv, cons[3] * inv
    p = 0.4 * (cons[4] - 0.5 * (cons[1] * u + cons[2] * v + cons[3] * w))
    return [cons[0], u, v, w, p]


def edges(before, here, after):
    down, up = here - before, after - here
    half = 0.5 * (
        jnp.maximum(jnp.minimum(down, up), 0.0) + jnp.minimum(jnp.maximum(down, up), 0.0)
    )
    return here + half, here - half


def hllc(left, right, normal):
    order = [0, 1 + normal] + [1 + d for d in range(3) if d != normal] + [4]
    rho_l, un_l, ut_l, us_l, p_l = [left[k] for k in order]
    rho_r, un_r, ut_r, us_r, p_r = [right[k] for k in order]
    a_l, a_r = p_l * inverse(rho_l), p_r * inverse(rho_r)
    c_l, c_r = root(1.4 * a_l), root(1.4 * a_r)
    s_l = jnp.minimum(un_l - c_l, un_r - c_r)
    s_r = jnp.maximum(un_l + c_l, un_r + c_r)
    m_l, m_r = rho_l * (s_l - un_l), rho_r * (s_r - un_r)
    star = (p_r - p_l + m_l * un_l - m_r * un_r) * inverse(m_l - m_r)
    side = (s_l >= 0.0) | (star >= 0.0)
    pick = lambda one, other: jnp.where(side, one, other)
    rho, un, ut, us, p = (
        pick(rho_l, rho_r),
        pick(un_l, un_r),
        pick(ut_l, ut_r),
        pick(us_l, us_r),
        pick(p_l, p_r),
    )
    a, m, s = pick(a_l, a_r), pick(m_l, m_r), pick(s_l, s_r)
    limited = pick(jnp.minimum(s_l, 0.0), jnp.maximum(s_r, 0.0))
    e = 2.5 * a + 0.5 * (un * un + ut * ut + us * us)
    energy = rho * e
    r = inverse(s - star)
    factor = m * r
    momentum = rho * un
    mass = momentum + limited * (factor - rho)
    force = momentum * un + p + limited * (factor * star - momentum)
    power = (energy + p) * un + limited * (
        factor * e + (star - un) * (factor * star + p * r) - energy
    )
    result = [None] * 5
    for k, part in zip(order, [mass, force, ut * mass, us * mass, power]):
        result[k] = part
    return result


def line_change(fields, axis, normal, wide=None):
    high, low = [], []
    for k in range(5):
        here = fields[k]
        if wide is None:
            after, before = roll(here, -1, axis), roll(here, 1, axis)
        else:
            after, before = roll(wide[k], -1, axis)[0:8], roll(wide[k], 1, axis)[0:8]
        one, other = edges(before, here, after)
        high.append(one)
        low.append(roll(other, -1, axis))
    flux = hllc(high, low, normal)
    return [part - roll(part, 1, axis) for part in flux]


def next_group(tiles, j):
    lane = iota(1, tiles[j][0].shape)
    other = tiles[j + 1] if j + 1 < len(tiles) and tiles[j + 1] is not None else tiles[j]
    return [jnp.where(lane < 96, roll(a, -32, 1), roll(b, -32, 1)) for a, b in zip(tiles[j], other)]


def prior_group(tiles, j):
    lane = iota(1, tiles[j][0].shape)
    other = tiles[j - 1] if j > 0 and tiles[j - 1] is not None else tiles[j]
    return [jnp.where(lane >= 32, roll(a, 32, 1), roll(b, 32, 1)) for a, b in zip(tiles[j], other)]


def group_changes(tiles, wanted):
    high, low, flux = [None] * len(tiles), [None] * len(tiles), [None] * len(tiles)
    for j in wanted:
        pairs = [
            edges(before, here, after)
            for before, here, after in zip(prior_group(tiles, j), tiles[j], next_group(tiles, j))
        ]
        high[j] = [pair[0] for pair in pairs]
        low[j] = [pair[1] for pair in pairs]
    for j in wanted:
        flux[j] = hllc(high[j], next_group(low, j), 0)
    return {
        j: [a - b for a, b in zip(flux[j], prior_group(flux, j))] for j in wanted
    }


def ends_kernel(prim_ref, out_ref):
    lane = iota(1, (4, 128))
    for f in range(5):
        total = None
        for x in range(4):
            row = prim_ref[f, x]
            part = lane - 32 * x
            first = roll(row, 32 * x + 8, 1)
            last = roll(row, 32 * x + 24, 1)
            piece = jnp.where(part < 16, first, last)
            total = piece if total is None else jnp.where(part < 0, total, piece)
        out_ref[f] = total


def block_kernel(_, ends_ref, before_ref, after_ref, prim_ref, out_ref, up_ref, down_ref):
    lane = iota(1, (4, 128)) % 32
    for f in range(5):
        edge = jnp.where(
            lane < 8,
            roll(before_ref[f], -16, 1),
            jnp.where(lane >= 24, roll(after_ref[f], 16, 1), ends_ref[f]),
        )
        for copy in range(4):
            out_ref[copy, 20 + f] = edge
            for x in range(4):
                out_ref[copy, 5 * x + f] = prim_ref[f, x]
        for ref, x in ((up_ref, 3), (down_ref, 0)):
            ref[f] = prim_ref[f, x]
            ref[5 + f] = edge


def near_kernel(own_ref, _, __, up_ref, down_ref):
    gy = lax.axis_index("gy")
    over, under = lax.rem(gy + 1, 4), lax.rem(gy + 3, 4)
    for ref, xs in ((up_ref, (3, 2, 1, 0)), (down_ref, (0, 1, 2, 3))):

        def take(block, distance):
            start = 5 * xs[distance - 1] if distance else 20
            return own_ref[block, start : start + 5]

        for k, distance in ((0, 1), (9, 0)):
            for j, block in enumerate((gy, over, under)):
                ref[5 * (k + j) : 5 * (k + j) + 5] = take(block, distance)
        for k, distance in ((3, 3), (5, 2), (6, 4)):
            ref[5 * k : 5 * k + 5] = take(gy, distance)
        ref[20:25, 0:2] = take(under, 3)[:, 2:4]
        ref[20:25, 2:4] = take(over, 3)[:, 0:2]
        ref[35:40, 0:3] = take(under, 2)[:, 1:4]
        ref[35:40, 3:4] = take(under, 4)[:, 3:4]
        ref[40:45, 0:3] = take(over, 2)[:, 0:3]
        ref[40:45, 3:4] = take(over, 4)[:, 0:1]


def coarse_kernel(
    table_ref, own_ref, prior_ref, next_ref, far_prior_ref, far_next_ref,
    new_ref, message_ref,
    prim_ref, edge_ref, section_ref, section_edge_ref, made_ref, made_edge_ref,
    old_pack_ref, body_ref, tips_ref, place_ref, done,
):
    gy, gz = lax.axis_index("gy"), lax.axis_index("gz")
    fetch = pltpu.make_async_copy(table_ref, place_ref, done)
    fetch.start()
    parent_ref, shift_ref = Table(place_ref, 2), Table(place_ref, 34)
    for k in range(4):
        source = lax.rem(gy + k, 4)
        rows, tips = own_ref[source, 0:20], own_ref[source, 20:25]
        for ref, base, count, value in ((prim_ref, 25, 20, rows), (edge_ref, 10, 5, tips)):
            if k < 3:
                ref[base : base + count, 2 + 4 * k : 6 + 4 * k] = value
            else:
                ref[base : base + count, 14:16] = value[:, 0:2]
                ref[base : base + count, 0:2] = value[:, 2:4]
    for got_ref, tile, bases in (
        (prior_ref, 5, (20, 15, 10, 5)),
        (next_ref, 15, (45, 50, 55, 60)),
    ):
        got = [got_ref[5 * k : 5 * k + 5] for k in range(12)]
        for ref, base, first in ((prim_ref, bases[0], 0), (edge_ref, tile, 9)):
            ref[base : base + 5, 2:6] = got[first]
            ref[base : base + 5, 6:10] = got[first + 1]
            ref[base : base + 5, 14:16] = got[first + 2][:, 0:2]
            ref[base : base + 5, 0:2] = got[first + 2][:, 2:4]
        for base, first in ((bases[2], 3), (bases[1], 5), (bases[3], 6)):
            prim_ref[base : base + 5, 2:6] = got[first]
        prim_ref[bases[2] : bases[2] + 5, 0:2] = got[4][:, 0:2]
        prim_ref[bases[2] : bases[2] + 5, 6:8] = got[4][:, 2:4]
        prim_ref[bases[1] : bases[1] + 5, 15:16] = got[7][:, 0:1]
        prim_ref[bases[1] : bases[1] + 5, 0:2] = got[7][:, 1:3]
        prim_ref[bases[1] : bases[1] + 5, 6:9] = got[8][:, 0:3]
        prim_ref[bases[3] : bases[3] + 5, 1:2] = got[7][:, 3:4]
        prim_ref[bases[3] : bases[3] + 5, 6:7] = got[8][:, 3:4]
    prim_ref[0:5, 2:6] = far_prior_ref[0:5]
    edge_ref[0:5, 2:6] = far_prior_ref[5:10]
    prim_ref[65:70, 2:6] = far_next_ref[0:5]
    edge_ref[20:25, 2:6] = far_next_ref[5:10]

    def prim_row(x):
        return [prim_ref[5 * (x + 5) + f] for f in range(5)]

    def section_row(x, rows=16):
        return [section_ref[5 * (x + 3) + f, 0:rows] for f in range(5)]

    def sweep(row, start, rows, at_once, emit):
        def pairs_of(x):
            found = [edges(b, h, a) for b, h, a in zip(row(x - 1), row(x), row(x + 1))]
            return [pair[0] for pair in found], [pair[1] for pair in found]

        def step(i, carry):
            high, flux = carry
            for k in range(at_once):
                x = start + i * at_once + k
                high_next, low = pairs_of(x + 1)
                flux_next = hllc(high, low, 0)
                emit(x, [after - before for before, after in zip(flux, flux_next)])
                high, flux = high_next, flux_next
            return high, flux

        high_before, _ = pairs_of(start - 1)
        high, low = pairs_of(start)
        lax.fori_loop(0, rows // at_once, step, (high, hllc(high_before, low, 0)))

    def section_of(x, by_x):
        middle = prim_row(x)
        by_y = line_change(middle, 0, 1)
        by_z = line_change(middle, 1, 2)
        state = conserved(middle)
        section = [state[f] - 0.05 * (by_x[f] + by_y[f] + by_z[f]) for f in range(5)]
        for f, value in enumerate(primitive(section)):
            section_ref[5 * (x + 3) + f] = value

    sweep(prim_row, -3, 10, FIRST, section_of)
    tiles = [[edge_ref[5 * t + f] for f in range(5)] for t in range(5)]
    by_x = group_changes(tiles, (1, 2, 3))
    for t in (1, 2, 3):
        by_y = line_change(tiles[t], 0, 1)
        by_z = line_change(tiles[t], 1, 2)
        state = conserved(tiles[t])
        section = [state[f] - 0.05 * (by_x[t][f] + by_y[f] + by_z[f]) for f in range(5)]
        for f, value in enumerate(primitive(section)):
            section_edge_ref[5 * (t - 1) + f] = value

    def advance(old, here, changes):
        start, state = conserved(old), conserved(here)
        return [
            0.5 * start[f] + 0.5 * (state[f] - 0.05 * (changes[0][f] + changes[1][f] + changes[2][f]))
            for f in range(5)
        ]

    def updated_of(x, by_x):
        middle = section_row(x, 8)
        by_y = line_change(middle, 0, 1, section_row(x))
        by_z = line_change(middle, 1, 2)
        old = [part[0:8] for part in prim_row(x)]
        for f, value in enumerate(advance(old, middle, (by_x, by_y, by_z))):
            made_ref[5 * (x + 1) + f] = value

    sweep(lambda x: section_row(x, 8), -1, 6, SECOND, updated_of)
    wide = [[section_edge_ref[5 * t + f] for f in range(5)] for t in range(3)]
    tiles = [[part[0:8] for part in tile] for tile in wide]
    by_x = group_changes(tiles, (0, 1, 2))
    for t in range(3):
        by_y = line_change(tiles[t], 0, 1, wide[t])
        by_z = line_change(tiles[t], 1, 2)
        old = [edge_ref[5 * (t + 1) + f, 0:8] for f in range(5)]
        for f, value in enumerate(advance(old, tiles[t], (by_x[t], by_y, by_z))):
            made_edge_ref[5 * t + f] = value

    lane, sub = iota(1), iota(0)

    def spot(x):
        return (0, 3) if x < 0 else ((2, 0) if x > 3 else (1, x))

    for f in range(5):
        olds, news = {}, {}
        for x in range(-1, 5):
            tile, group = spot(x)
            main = prim_ref[5 * (x + 5) + f, 0:8]
            tips = edge_ref[5 * (tile + 1) + f, 0:8]
            under, over = roll(tips, -32 * group - 8, 1), roll(tips, 104 - 32 * group, 1)
            olds[x] = (main, jnp.where(lane == 127, under, main), jnp.where(lane == 0, over, main))
            main, tips = made_ref[5 * (x + 1) + f], made_edge_ref[5 * tile + f]
            under, over = roll(tips, -32 * group - 8, 1), roll(tips, 104 - 32 * group, 1)
            main = jnp.where(lane < 4, under, jnp.where(lane >= 124, over, main))
            news[x] = (main, jnp.where(lane == 127, under, main), jnp.where(lane == 0, over, main))
            if 0 <= x < 4:
                new_ref[f, x] = main[2:6]
        inner = (sub >= 2) & (sub < 6)
        for x in range(4):
            face = olds[-1 if x < 2 else 4][0]
            top, bottom = (-2, 4) if x % 2 == 0 else (-4, 2)
            for kind in range(3):
                old_pack_ref[kind, 4 * f + x] = roll(jnp.where(
                    sub == 0,
                    roll(face, top, 0),
                    jnp.where(sub == 7, roll(face, bottom, 0), olds[x][kind]),
                ), GROUP * ((4 * f + x) % PER_ROW), 1)
        for half, (out, near, far) in enumerate(((-1, 0, 1), (4, 3, 2))):
            body_ref[2 * f + half] = roll(jnp.where(
                inner,
                news[out][0],
                jnp.where(
                    sub == 0,
                    roll(news[far][0], -1, 0),
                    jnp.where(sub == 7, roll(news[far][0], 1, 0), news[near][0]),
                ),
            ), GROUP * ((OLD + 2 * f + half) % PER_ROW), 1)
            for kind in range(3):
                tips_ref[kind, 2 * f + half] = roll(jnp.where(
                    inner,
                    news[near][kind],
                    jnp.where(sub < 2, roll(news[far][kind], -2, 0), roll(news[far][kind], 2, 0)),
                ), GROUP * ((OLD + 2 * f + half) % PER_ROW), 1)

    def send(turn, carry):
        for k_owner in range(SENDS):
            owner = SENDS * turn + k_owner
            hit = parent_ref[2 * owner] == gz
            shift = jnp.where(hit, shift_ref[2 * owner], shift_ref[2 * owner + 1])
            kind = jnp.where(shift == 0, 1, jnp.where(shift == 120, 2, 0))
            place = (lane + (129 - shift)) & 127
            group = (place * 205) >> 11
            within = place - GROUP * group
            ends = (within == 0) | (within == GROUP - 1)
            for tile in range(TILES):
                total = None
                for j in range(PER_ROW):
                    k = tile * PER_ROW + j
                    if k >= OLD + 10:
                        break
                    if k < OLD:
                        piece = old_pack_ref[kind, k]
                    else:
                        piece = jnp.where(ends, tips_ref[kind, k - OLD], body_ref[k - OLD])
                    total = piece if total is None else jnp.where(group == j, piece, total)
                total = pltpu.roll(total, lax.rem(129 - shift, 128), 1)
                if tile < TILES - 1:
                    message_ref[owner, 2 * tile] = total[0:4]
                    message_ref[owner, 2 * tile + 1] = total[4:8]
                else:
                    message_ref[owner, 2 * tile] = jnp.where(
                        iota(1, (4, 128)) < 60, total[0:4], roll(total, 60, 1)[4:8]
                    )
        return carry

    fetch.wait()
    lax.fori_loop(0, 16 // SENDS, send, 0)


def fine_kernel(
    place_ref, got_ref, rho_ref, vel_ref, p_ref, out_ref, message_ref,
    mid_ref, tip_ref, ghost_ref, bound_ref,
):
    gz = place_ref[1]
    parent_ref = Table(place_ref, 2)
    lane, sub = iota(1), iota(0)
    part = lane % 16
    yc, xc = lane // 32, sub // 2
    parents = [parent_ref[2 * gz + box] for box in range(2)]

    for box in range(2):
        tiles = [
            jnp.concatenate([got_ref[parents[box], 2 * t], got_ref[parents[box], 2 * t + 1]])
            for t in range(TILES - 1)
        ]
        short = got_ref[parents[box], 2 * TILES - 2]
        tiles.append(jnp.concatenate([short, roll(short, -60, 1)]))
        for k in range(OLD + 10):
            j = k % PER_ROW
            tile = tiles[k // PER_ROW]
            at = GROUP * j + 1 + part // 2
            mid_ref[box, 8 * k : 8 * k + 8] = jnp.take_along_axis(tile, at, axis=1)
            at = GROUP * j + jnp.where(part < 8, 0, 9)
            tip_ref[box, 8 * k : 8 * k + 8] = jnp.take_along_axis(tile, at, axis=1)

    def every(ref, box, k, row, step=1):
        return ref[box, pl.ds(8 * k + row, 8, stride=8 * step)]

    def by_y(items):
        return jnp.where(
            yc < 2,
            jnp.where(yc == 0, items[0], items[1]),
            jnp.where(yc == 2, items[2], items[3]),
        )

    def spread(value, rows):
        return jnp.take_along_axis(value, rows, axis=0)

    side, low_y = (sub >= 4).astype(jnp.int32), lane < 64
    outer_x = (xc == 0) | (xc == 3)
    half_x = (xc >= 2).astype(jnp.int32)

    def old_parts(box):
        inside, along_x, along_y, along_z = [], [], [], []
        for f in range(5):
            if f % 2 == 0:
                middle = by_y([every(mid_ref, box, 4 * f, 2 + y) for y in range(4)])
                sides = jnp.where(low_y, every(mid_ref, box, 4 * f, 1), every(mid_ref, box, 4 * f, 6))
                tips = by_y([every(tip_ref, box, 4 * f, 2 + y) for y in range(4)])
            if f % 4 == 0:
                faces = by_y(
                    [every(mid_ref, box, 4 * f + y // 2, 7 * (y % 2), 2) for y in range(4)]
                )
            at = 4 * (f % 2) + xc
            inside.append(spread(middle, at))
            along_y.append(spread(sides, at))
            along_z.append(spread(tips, at))
            along_x.append(spread(faces, 2 * (f % 4) + side))
        return inside, [along_x, along_y, along_z]

    def new_parts(box):
        along_x, along_y, along_z = [], [], []
        for f in range(5):
            if f % 4 == 0:
                k = OLD + 2 * f
                faces = by_y([every(mid_ref, box, k, 2 + y) for y in range(4)])
                sides_near = jnp.where(low_y, every(mid_ref, box, k, 1), every(mid_ref, box, k, 6))
                sides_far = jnp.where(low_y, every(mid_ref, box, k, 0), every(mid_ref, box, k, 7))
                tips_near = by_y([every(tip_ref, box, k, 2 + y) for y in range(4)])
                tips_far = by_y([every(tip_ref, box, k, row) for row in (0, 1, 6, 7)])
            at = 2 * (f % 4) + half_x
            along_x.append(spread(faces, 2 * (f % 4) + side))
            along_y.append(jnp.where(outer_x, spread(sides_near, at), spread(sides_far, at)))
            along_z.append(jnp.where(outer_x, spread(tips_near, at), spread(tips_far, at)))
        return [along_x, along_y, along_z]

    directions = (
        (0, 1, sub == 0, sub == 7, 4, sub >= 4),
        (1, 16, lane < 16, lane >= 112, 64, lane >= 64),
        (1, 1, part == 0, part == 15, 8, part >= 8),
    )

    def changes(fields, step_index):
        total = None
        for normal, (axis, step, first, last, park, parked) in enumerate(directions):
            high, low, up = [[], []], [[], []], [[], []]
            for box in range(2):
                for f in range(5):
                    here, ghost = fields[box][f], ghost_ref[step_index, box, normal, f]
                    after = jnp.where(last, ghost, roll(here, -step, axis))
                    before = jnp.where(first, ghost, roll(here, step, axis))
                    one, other = edges(before, here, after)
                    high[box].append(one)
                    low[box].append(other)
                    up[box].append(jnp.where(last, ghost, roll(other, -step, axis)))
            right = [jnp.where(parked, roll(b, park, axis), a) for a, b in zip(low[0], low[1])]
            bottom = hllc([bound_ref[step_index, normal, f] for f in range(5)], right, normal)
            found = []
            for box in range(2):
                flux = hllc(high[box], up[box], normal)
                under = bottom if box == 0 else [roll(item, -park, axis) for item in bottom]
                found.append(
                    [a - jnp.where(first, b, roll(a, step, axis)) for a, b in zip(flux, under)]
                )
            total = (
                found
                if total is None
                else [[a + b for a, b in zip(t, g)] for t, g in zip(total, found)]
            )
        return total

    def keep(step_index, ghosts):
        for normal, (axis, _, _, _, park, parked) in enumerate(directions):
            for f in range(5):
                for box in range(2):
                    ghost_ref[step_index, box, normal, f] = ghosts[box][normal][f]
                bound_ref[step_index, normal, f] = jnp.where(
                    parked, roll(ghosts[1][normal][f], park, axis), ghosts[0][normal][f]
                )

    ghosts, states, later = [], [], []
    for box in range(2):
        inside, found = old_parts(box)
        ghosts.append(found)
        details = [rho_ref[box], vel_ref[0, box], vel_ref[1, box], vel_ref[2, box], p_ref[box]]
        states.append(conserved([a + b for a, b in zip(inside, details)]))
        later.append(
            [
                primitive([0.5 * (a + b) for a, b in zip(conserved(old), new)])
                for old, new in zip(found, new_parts(box))
            ]
        )
    keep(0, ghosts)
    keep(1, later)

    def stage(i, carry):
        start, state = carry
        again = lax.rem(i, 2) == 1
        weight = jnp.where(again, 0.5, 1.0).astype(F32)
        start = jax.tree.map(lambda a, b: jnp.where(again, a, b), start, state)
        moved = changes([primitive(item) for item in state], i // 2)
        state = jax.tree.map(
            lambda s, t, m: (1.0 - weight) * s + weight * (t - 0.05 * m), start, state, moved
        )
        return start, state

    _, states = lax.fori_loop(0, 4, stage, (states, states), unroll=4)
    for box in range(2):
        packed = None
        for f in range(5):
            value = states[box][f]
            out_ref[f, box] = value
            value = value + roll(value, -1, 0)
            value = value + roll(value, -1, 1)
            value = (value + roll(value, -16, 1)) * 0.125
            inside_lane = lane % 32
            at = (inside_lane // 8) * 32 + (inside_lane % 8) * 2
            value = jnp.take_along_axis(value, at, axis=1)
            if f == 0:
                packed = value
            elif f < 4:
                packed = jnp.where(lane // 32 == f, value, packed)
            else:
                packed = jnp.where((sub % 2 == 1) & (lane < 32), roll(value, 1, 0), packed)
        message_ref[parents[box]] = packed


def final_kernel(place_ref, new_ref, got_ref, out_ref, sum_ref):
    gz = place_ref[1]
    parent_ref, shift_ref = Table(place_ref, 2), Table(place_ref, 34)
    lane = iota(1)

    def add(turn, carry):
        count, sums = carry
        for k_owner in range(ADDS):
            owner = ADDS * turn + k_owner
            hit = parent_ref[2 * owner] == gz
            other = parent_ref[2 * owner + 1] == gz
            shift = jnp.where(hit, shift_ref[2 * owner], shift_ref[2 * owner + 1])
            shift = jnp.where(hit | other, shift, 256)
            count = count + jnp.where((lane >= shift) & (lane < shift + 8), 1.0, 0.0)
            value = pltpu.roll(got_ref[owner], lax.rem(shift, 128), 1)
            group = jnp.where(shift < 256, ((lane + (256 - shift)) & 127) >> 3, 16)
            sums = [item + jnp.where(group == k, value, 0.0) for k, item in enumerate(sums)]
        return count, sums

    zero = jnp.zeros((8, 128), F32)
    count, sums = lax.fori_loop(0, 16 // ADDS, add, (zero, [zero] * 16))
    share = inverse(jnp.maximum(count, 1.0))
    for k in range(16):
        sum_ref[8 * k : 8 * k + 8] = roll(sums[k], -8 * k, 1) * share
    for f in range(5):
        for x in range(4):
            start = (0 if f == 4 else 32 * f) + 2 * x + (1 if f == 4 else 0)
            value = sum_ref[pl.ds(start, 4, stride=8)]
            out_ref[f, x] = jnp.where(count[0:4] > 0.0, value, new_ref[f, x])


FINE_SCRATCH = ((2, 352, 128), (2, 352, 128), (2, 2, 3, 5, 8, 128), (2, 3, 5, 8, 128))


def shape(*dims):
    return jax.ShapeDtypeStruct(dims, F32)


def call(kernel, outs, scalars, arrays, scratch=()):
    return pl.pallas_call(
        kernel,
        out_shape=outs,
        in_specs=[pl.BlockSpec(memory_space=pltpu.SMEM)] * scalars
        + [pl.BlockSpec(memory_space=pltpu.VMEM)] * arrays,
        out_specs=jax.tree.map(lambda _: pl.BlockSpec(memory_space=pltpu.VMEM), outs),
        scratch_shapes=[pltpu.VMEM(k, F32) if isinstance(k, tuple) else k for k in scratch],
        compiler_params=pltpu.CompilerParams(vmem_limit_bytes=32 * 1024 * 1024),
    )


def shifted(value, axis, step):
    size = lax.axis_size(axis)
    return lax.ppermute(value, axis, [(i, (i + step) % size) for i in range(size)])


def on_device(
    density, velocity, pressure, fine_density, fine_velocity, fine_pressure, box_parent, box_shift
):
    assert density.shape == (4, 4, 128) and fine_density.shape == (1, 1, 2, 8, 128)
    place = jnp.stack([lax.axis_index("gy"), lax.axis_index("gz")]).astype(jnp.int32)
    place = jnp.concatenate([place, box_parent.reshape(32), box_shift.reshape(32)])
    prim = jnp.concatenate([density[None], velocity, pressure[None]])
    ends = call(ends_kernel, shape(5, 4, 128), 0, 1)(prim)
    before, after = shifted(ends, "gz", 1), shifted(ends, "gz", -1)
    block, for_up, for_down = call(
        block_kernel, (shape(4, 25, 4, 128), shape(10, 4, 128), shape(10, 4, 128)), 0, 5
    )(place, ends, before, after, prim)
    own = lax.all_to_all(block, "gy", 0, 0, tiled=True)
    far_prior, far_next = shifted(for_up, "gx", 2), shifted(for_down, "gx", -2)
    for_up, for_down = call(near_kernel, (shape(60, 4, 128), shape(60, 4, 128)), 0, 3)(
        own, far_prior, far_next
    )
    prior, following = shifted(for_up, "gx", 1), shifted(for_down, "gx", -1)
    updated, message = call(
        coarse_kernel,
        (shape(5, 4, 4, 128), shape(16, 2 * TILES - 1, 4, 128)),
        0,
        6,
        (
            (70, 16, 128),
            (25, 16, 128),
            (50, 16, 128),
            (15, 16, 128),
            (30, 8, 128),
            (15, 8, 128),
            (3, 20, 8, 128),
            (10, 8, 128),
            (3, 10, 8, 128),
            pltpu.SMEM((66,), jnp.int32),
            pltpu.SemaphoreType.DMA,
        ),
    )(place, own, prior, following, far_prior, far_next)
    got = lax.all_to_all(message, "gz", 0, 0, tiled=True)
    fine, means = call(
        fine_kernel,
        (shape(5, 2, 8, 128), shape(16, 8, 128)),
        1,
        4,
        FINE_SCRATCH,
    )(
        place,
        got,
        fine_density.reshape(2, 8, 128),
        fine_velocity.reshape(3, 2, 8, 128),
        fine_pressure.reshape(2, 8, 128),
    )
    incoming = lax.all_to_all(means, "gz", 0, 0, tiled=True)
    coarse = call(final_kernel, shape(5, 4, 4, 128), 1, 2, ((128, 128),))(place, updated, incoming)
    return coarse, fine.reshape(5, 1, 1, 2, 8, 128)


def solution(mesh):
    in_specs = (
        P("gx", "gy", "gz"),
        P(None, "gx", "gy", "gz"),
        P("gx", "gy", "gz"),
        P("gx", "gy", "gz", None, None),
        P(None, "gx", "gy", "gz", None, None),
        P("gx", "gy", "gz", None, None),
        P("gx", "gy", None, None),
        P("gx", "gy", None),
    )
    out_specs = (P(None, "gx", "gy", "gz"), P(None, "gx", "gy", "gz", None, None))
    return jax.shard_map(
        on_device, mesh=mesh, in_specs=in_specs, out_specs=out_specs, check_vma=False
    )
```

```python
import jax
import jax.numpy as jnp
from jax import lax
from jax.experimental import pallas as pl
from jax.experimental.pallas import tpu as pltpu
from jax.sharding import PartitionSpec as P

F32 = jnp.float32
GROUP = 10
PER_ROW = 12
OLD = 20
TILES = 3
FIRST, SECOND = 2, 3
SENDS, ADDS = 8, 16


def iota(dim, shape=(8, 128)):
    return lax.broadcasted_iota(jnp.int32, shape, dim)


class Table:
    def __init__(self, ref, base):
        self.ref, self.base = ref, base

    def __getitem__(self, k):
        return self.ref[self.base + k]


def roll(value, shift, axis):
    size = value.shape[axis]
    shift = shift % size
    return value if shift == 0 else pltpu.roll(value, shift, axis)


def inverse(value):
    guess = pl.reciprocal(value, approx=True)
    return guess * (2.0 - value * guess)


def root(value):
    return value * lax.rsqrt(jnp.maximum(value, 1e-30))


def conserved(prim):
    rho, u, v, w, p = prim
    return [rho, rho * u, rho * v, rho * w, 2.5 * p + 0.5 * rho * (u * u + v * v + w * w)]


def primitive(cons):
    inv = inverse(cons[0])
    u, v, w = cons[1] * inv, cons[2] * inv, cons[3] * inv
    p = 0.4 * (cons[4] - 0.5 * (cons[1] * u + cons[2] * v + cons[3] * w))
    return [cons[0], u, v, w, p]


def edges(before, here, after):
    down, up = here - before, after - here
    half = 0.5 * (
        jnp.maximum(jnp.minimum(down, up), 0.0) + jnp.minimum(jnp.maximum(down, up), 0.0)
    )
    return here + half, here - half


def hllc(left, right, normal):
    order = [0, 1 + normal] + [1 + d for d in range(3) if d != normal] + [4]
    rho_l, un_l, ut_l, us_l, p_l = [left[k] for k in order]
    rho_r, un_r, ut_r, us_r, p_r = [right[k] for k in order]
    a_l, a_r = p_l * inverse(rho_l), p_r * inverse(rho_r)
    c_l, c_r = root(1.4 * a_l), root(1.4 * a_r)
    s_l = jnp.minimum(un_l - c_l, un_r - c_r)
    s_r = jnp.maximum(un_l + c_l, un_r + c_r)
    m_l, m_r = rho_l * (s_l - un_l), rho_r * (s_r - un_r)
    star = (p_r - p_l + m_l * un_l - m_r * un_r) * inverse(m_l - m_r)
    side = (s_l >= 0.0) | (star >= 0.0)
    pick = lambda one, other: jnp.where(side, one, other)
    rho, un, ut, us, p = (
        pick(rho_l, rho_r),
        pick(un_l, un_r),
        pick(ut_l, ut_r),
        pick(us_l, us_r),
        pick(p_l, p_r),
    )
    a, m, s = pick(a_l, a_r), pick(m_l, m_r), pick(s_l, s_r)
    limited = pick(jnp.minimum(s_l, 0.0), jnp.maximum(s_r, 0.0))
    e = 2.5 * a + 0.5 * (un * un + ut * ut + us * us)
    energy = rho * e
    r = inverse(s - star)
    factor = m * r
    momentum = rho * un
    mass = momentum + limited * (factor - rho)
    force = momentum * un + p + limited * (factor * star - momentum)
    power = (energy + p) * un + limited * (
        factor * e + (star - un) * (factor * star + p * r) - energy
    )
    result = [None] * 5
    for k, part in zip(order, [mass, force, ut * mass, us * mass, power]):
        result[k] = part
    return result


def line_change(fields, axis, normal, wide=None):
    high, low = [], []
    for k in range(5):
        here = fields[k]
        if wide is None:
            after, before = roll(here, -1, axis), roll(here, 1, axis)
        else:
            after, before = roll(wide[k], -1, axis)[0:8], roll(wide[k], 1, axis)[0:8]
        one, other = edges(before, here, after)
        high.append(one)
        low.append(roll(other, -1, axis))
    flux = hllc(high, low, normal)
    return [part - roll(part, 1, axis) for part in flux]


def next_group(tiles, j):
    lane = iota(1, tiles[j][0].shape)
    other = tiles[j + 1] if j + 1 < len(tiles) and tiles[j + 1] is not None else tiles[j]
    return [jnp.where(lane < 96, roll(a, -32, 1), roll(b, -32, 1)) for a, b in zip(tiles[j], other)]


def prior_group(tiles, j):
    lane = iota(1, tiles[j][0].shape)
    other = tiles[j - 1] if j > 0 and tiles[j - 1] is not None else tiles[j]
    return [jnp.where(lane >= 32, roll(a, 32, 1), roll(b, 32, 1)) for a, b in zip(tiles[j], other)]


def group_changes(tiles, wanted):
    high, low, flux = [None] * len(tiles), [None] * len(tiles), [None] * len(tiles)
    for j in wanted:
        pairs = [
            edges(before, here, after)
            for before, here, after in zip(prior_group(tiles, j), tiles[j], next_group(tiles, j))
        ]
        high[j] = [pair[0] for pair in pairs]
        low[j] = [pair[1] for pair in pairs]
    for j in wanted:
        flux[j] = hllc(high[j], next_group(low, j), 0)
    return {
        j: [a - b for a, b in zip(flux[j], prior_group(flux, j))] for j in wanted
    }


def ends_kernel(prim_ref, out_ref):
    lane = iota(1, (4, 128))
    for f in range(5):
        total = None
        for x in range(4):
            row = prim_ref[f, x]
            part = lane - 32 * x
            first = roll(row, 32 * x + 8, 1)
            last = roll(row, 32 * x + 24, 1)
            piece = jnp.where(part < 16, first, last)
            total = piece if total is None else jnp.where(part < 0, total, piece)
        out_ref[f] = total


def block_kernel(_, ends_ref, before_ref, after_ref, prim_ref, out_ref, up_ref, down_ref):
    lane = iota(1, (4, 128)) % 32
    for f in range(5):
        edge = jnp.where(
            lane < 8,
            roll(before_ref[f], -16, 1),
            jnp.where(lane >= 24, roll(after_ref[f], 16, 1), ends_ref[f]),
        )
        for copy in range(4):
            out_ref[copy, 20 + f] = edge
            for x in range(4):
                out_ref[copy, 5 * x + f] = prim_ref[f, x]
        for ref, x in ((up_ref, 3), (down_ref, 0)):
            ref[f] = prim_ref[f, x]
            ref[5 + f] = edge


def near_kernel(own_ref, _, __, up_ref, down_ref):
    gy = lax.axis_index("gy")
    over, under = lax.rem(gy + 1, 4), lax.rem(gy + 3, 4)
    for ref, xs in ((up_ref, (3, 2, 1, 0)), (down_ref, (0, 1, 2, 3))):

        def take(block, distance):
            start = 5 * xs[distance - 1] if distance else 20
            return own_ref[block, start : start + 5]

        for k, distance in ((0, 1), (9, 0)):
            for j, block in enumerate((gy, over, under)):
                ref[5 * (k + j) : 5 * (k + j) + 5] = take(block, distance)
        for k, distance in ((3, 3), (5, 2), (6, 4)):
            ref[5 * k : 5 * k + 5] = take(gy, distance)
        ref[20:25, 0:2] = take(under, 3)[:, 2:4]
        ref[20:25, 2:4] = take(over, 3)[:, 0:2]
        ref[35:40, 0:3] = take(under, 2)[:, 1:4]
        ref[35:40, 3:4] = take(under, 4)[:, 3:4]
        ref[40:45, 0:3] = take(over, 2)[:, 0:3]
        ref[40:45, 3:4] = take(over, 4)[:, 0:1]


def coarse_kernel(
    table_ref, own_ref, prior_ref, next_ref, far_prior_ref, far_next_ref,
    new_ref, message_ref, owned_ref, spots_ref,
    prim_ref, edge_ref, section_ref, section_edge_ref, made_ref, made_edge_ref,
    old_pack_ref, body_ref, tips_ref, place_ref, done,
):
    gy, gz = lax.axis_index("gy"), lax.axis_index("gz")
    fetch = pltpu.make_async_copy(table_ref, place_ref, done)
    fetch.start()
    parent_ref, shift_ref = Table(place_ref, 2), Table(place_ref, 34)
    for k in range(4):
        source = lax.rem(gy + k, 4)
        rows, tips = own_ref[source, 0:20], own_ref[source, 20:25]
        for ref, base, count, value in ((prim_ref, 25, 20, rows), (edge_ref, 10, 5, tips)):
            if k < 3:
                ref[base : base + count, 2 + 4 * k : 6 + 4 * k] = value
            else:
                ref[base : base + count, 14:16] = value[:, 0:2]
                ref[base : base + count, 0:2] = value[:, 2:4]
    for got_ref, tile, bases in (
        (prior_ref, 5, (20, 15, 10, 5)),
        (next_ref, 15, (45, 50, 55, 60)),
    ):
        got = [got_ref[5 * k : 5 * k + 5] for k in range(12)]
        for ref, base, first in ((prim_ref, bases[0], 0), (edge_ref, tile, 9)):
            ref[base : base + 5, 2:6] = got[first]
            ref[base : base + 5, 6:10] = got[first + 1]
            ref[base : base + 5, 14:16] = got[first + 2][:, 0:2]
            ref[base : base + 5, 0:2] = got[first + 2][:, 2:4]
        for base, first in ((bases[2], 3), (bases[1], 5), (bases[3], 6)):
            prim_ref[base : base + 5, 2:6] = got[first]
        prim_ref[bases[2] : bases[2] + 5, 0:2] = got[4][:, 0:2]
        prim_ref[bases[2] : bases[2] + 5, 6:8] = got[4][:, 2:4]
        prim_ref[bases[1] : bases[1] + 5, 15:16] = got[7][:, 0:1]
        prim_ref[bases[1] : bases[1] + 5, 0:2] = got[7][:, 1:3]
        prim_ref[bases[1] : bases[1] + 5, 6:9] = got[8][:, 0:3]
        prim_ref[bases[3] : bases[3] + 5, 1:2] = got[7][:, 3:4]
        prim_ref[bases[3] : bases[3] + 5, 6:7] = got[8][:, 3:4]
    prim_ref[0:5, 2:6] = far_prior_ref[0:5]
    edge_ref[0:5, 2:6] = far_prior_ref[5:10]
    prim_ref[65:70, 2:6] = far_next_ref[0:5]
    edge_ref[20:25, 2:6] = far_next_ref[5:10]

    def prim_row(x):
        return [prim_ref[5 * (x + 5) + f] for f in range(5)]

    def section_row(x, rows=16):
        return [section_ref[5 * (x + 3) + f, 0:rows] for f in range(5)]

    def sweep(row, start, rows, at_once, emit):
        def pairs_of(x):
            found = [edges(b, h, a) for b, h, a in zip(row(x - 1), row(x), row(x + 1))]
            return [pair[0] for pair in found], [pair[1] for pair in found]

        def step(i, carry):
            high, flux = carry
            for k in range(at_once):
                x = start + i * at_once + k
                high_next, low = pairs_of(x + 1)
                flux_next = hllc(high, low, 0)
                emit(x, [after - before for before, after in zip(flux, flux_next)])
                high, flux = high_next, flux_next
            return high, flux

        high_before, _ = pairs_of(start - 1)
        high, low = pairs_of(start)
        lax.fori_loop(0, rows // at_once, step, (high, hllc(high_before, low, 0)))

    def section_of(x, by_x):
        middle = prim_row(x)
        by_y = line_change(middle, 0, 1)
        by_z = line_change(middle, 1, 2)
        state = conserved(middle)
        section = [state[f] - 0.05 * (by_x[f] + by_y[f] + by_z[f]) for f in range(5)]
        for f, value in enumerate(primitive(section)):
            section_ref[5 * (x + 3) + f] = value

    sweep(prim_row, -3, 10, FIRST, section_of)
    tiles = [[edge_ref[5 * t + f] for f in range(5)] for t in range(5)]
    by_x = group_changes(tiles, (1, 2, 3))
    for t in (1, 2, 3):
        by_y = line_change(tiles[t], 0, 1)
        by_z = line_change(tiles[t], 1, 2)
        state = conserved(tiles[t])
        section = [state[f] - 0.05 * (by_x[t][f] + by_y[f] + by_z[f]) for f in range(5)]
        for f, value in enumerate(primitive(section)):
            section_edge_ref[5 * (t - 1) + f] = value

    def advance(old, here, changes):
        start, state = conserved(old), conserved(here)
        return [
            0.5 * start[f] + 0.5 * (state[f] - 0.05 * (changes[0][f] + changes[1][f] + changes[2][f]))
            for f in range(5)
        ]

    def updated_of(x, by_x):
        middle = section_row(x, 8)
        by_y = line_change(middle, 0, 1, section_row(x))
        by_z = line_change(middle, 1, 2)
        old = [part[0:8] for part in prim_row(x)]
        for f, value in enumerate(advance(old, middle, (by_x, by_y, by_z))):
            made_ref[5 * (x + 1) + f] = value

    sweep(lambda x: section_row(x, 8), -1, 6, SECOND, updated_of)
    wide = [[section_edge_ref[5 * t + f] for f in range(5)] for t in range(3)]
    tiles = [[part[0:8] for part in tile] for tile in wide]
    by_x = group_changes(tiles, (0, 1, 2))
    for t in range(3):
        by_y = line_change(tiles[t], 0, 1, wide[t])
        by_z = line_change(tiles[t], 1, 2)
        old = [edge_ref[5 * (t + 1) + f, 0:8] for f in range(5)]
        for f, value in enumerate(advance(old, tiles[t], (by_x[t], by_y, by_z))):
            made_edge_ref[5 * t + f] = value

    lane, sub = iota(1), iota(0)

    def spot(x):
        return (0, 3) if x < 0 else ((2, 0) if x > 3 else (1, x))

    for f in range(5):
        olds, news = {}, {}
        for x in range(-1, 5):
            tile, group = spot(x)
            main = prim_ref[5 * (x + 5) + f, 0:8]
            tips = edge_ref[5 * (tile + 1) + f, 0:8]
            under, over = roll(tips, -32 * group - 8, 1), roll(tips, 104 - 32 * group, 1)
            olds[x] = (main, jnp.where(lane == 127, under, main), jnp.where(lane == 0, over, main))
            main, tips = made_ref[5 * (x + 1) + f], made_edge_ref[5 * tile + f]
            under, over = roll(tips, -32 * group - 8, 1), roll(tips, 104 - 32 * group, 1)
            main = jnp.where(lane < 4, under, jnp.where(lane >= 124, over, main))
            news[x] = (main, jnp.where(lane == 127, under, main), jnp.where(lane == 0, over, main))
            if 0 <= x < 4:
                new_ref[f, x] = main[2:6]
        inner = (sub >= 2) & (sub < 6)
        for x in range(4):
            face = olds[-1 if x < 2 else 4][0]
            top, bottom = (-2, 4) if x % 2 == 0 else (-4, 2)
            for kind in range(3):
                old_pack_ref[kind, 4 * f + x] = roll(jnp.where(
                    sub == 0,
                    roll(face, top, 0),
                    jnp.where(sub == 7, roll(face, bottom, 0), olds[x][kind]),
                ), GROUP * ((4 * f + x) % PER_ROW), 1)
        for half, (out, near, far) in enumerate(((-1, 0, 1), (4, 3, 2))):
            body_ref[2 * f + half] = roll(jnp.where(
                inner,
                news[out][0],
                jnp.where(
                    sub == 0,
                    roll(news[far][0], -1, 0),
                    jnp.where(sub == 7, roll(news[far][0], 1, 0), news[near][0]),
                ),
            ), GROUP * ((OLD + 2 * f + half) % PER_ROW), 1)
            for kind in range(3):
                tips_ref[kind, 2 * f + half] = roll(jnp.where(
                    inner,
                    news[near][kind],
                    jnp.where(sub < 2, roll(news[far][kind], -2, 0), roll(news[far][kind], 2, 0)),
                ), GROUP * ((OLD + 2 * f + half) % PER_ROW), 1)

    def send(turn, carry):
        for k_owner in range(SENDS):
            owner = SENDS * turn + k_owner
            hit = parent_ref[2 * owner] == gz
            shift = jnp.where(hit, shift_ref[2 * owner], shift_ref[2 * owner + 1])
            kind = jnp.where(shift == 0, 1, jnp.where(shift == 120, 2, 0))
            place = (lane + (129 - shift)) & 127
            group = (place * 205) >> 11
            within = place - GROUP * group
            ends = (within == 0) | (within == GROUP - 1)
            for tile in range(TILES):
                total = None
                for j in range(PER_ROW):
                    k = tile * PER_ROW + j
                    if k >= OLD + 10:
                        break
                    if k < OLD:
                        piece = old_pack_ref[kind, k]
                    else:
                        piece = jnp.where(ends, tips_ref[kind, k - OLD], body_ref[k - OLD])
                    total = piece if total is None else jnp.where(group == j, piece, total)
                total = pltpu.roll(total, lax.rem(129 - shift, 128), 1)
                if tile < TILES - 1:
                    message_ref[owner, 2 * tile] = total[0:4]
                    message_ref[owner, 2 * tile + 1] = total[4:8]
                else:
                    message_ref[owner, 2 * tile] = jnp.where(
                        iota(1, (4, 128)) < 60, total[0:4], roll(total, 60, 1)[4:8]
                    )
        return carry

    fetch.wait()
    for box in range(2):
        owned_ref[box] = jnp.full((8, 128), parent_ref[2 * gz + box], jnp.int32)
    for owner in range(16):
        hit, other = parent_ref[2 * owner] == gz, parent_ref[2 * owner + 1] == gz
        shift = jnp.where(hit, shift_ref[2 * owner], shift_ref[2 * owner + 1])
        spots_ref[owner] = jnp.full((8, 128), jnp.where(hit | other, shift, 256), jnp.int32)
    lax.fori_loop(0, 16 // SENDS, send, 0)


def fine_kernel(
    owned_ref, got_ref, rho_ref, vel_ref, p_ref, out_ref, message_ref,
    mid_ref, tip_ref, ghost_ref, bound_ref,
):
    lane, sub = iota(1), iota(0)
    part = lane % 16
    yc, xc = lane // 32, sub // 2

    def slot(box, tile):
        named = owned_ref[box, 0:4]
        found = got_ref[0, tile]
        for parent in range(1, 16):
            found = jnp.where(named == parent, got_ref[parent, tile], found)
        return found


    for box in range(2):
        tiles = [
            jnp.concatenate([slot(box, 2 * t), slot(box, 2 * t + 1)])
            for t in range(TILES - 1)
        ]
        short = slot(box, 2 * TILES - 2)
        tiles.append(jnp.concatenate([short, roll(short, -60, 1)]))
        for k in range(OLD + 10):
            j = k % PER_ROW
            tile = tiles[k // PER_ROW]
            at = GROUP * j + 1 + part // 2
            mid_ref[box, 8 * k : 8 * k + 8] = jnp.take_along_axis(tile, at, axis=1)
            at = GROUP * j + jnp.where(part < 8, 0, 9)
            tip_ref[box, 8 * k : 8 * k + 8] = jnp.take_along_axis(tile, at, axis=1)

    def every(ref, box, k, row, step=1):
        return ref[box, pl.ds(8 * k + row, 8, stride=8 * step)]

    def by_y(items):
        return jnp.where(
            yc < 2,
            jnp.where(yc == 0, items[0], items[1]),
            jnp.where(yc == 2, items[2], items[3]),
        )

    def spread(value, rows):
        return jnp.take_along_axis(value, rows, axis=0)

    side, low_y = (sub >= 4).astype(jnp.int32), lane < 64
    outer_x = (xc == 0) | (xc == 3)
    half_x = (xc >= 2).astype(jnp.int32)

    def old_parts(box):
        inside, along_x, along_y, along_z = [], [], [], []
        for f in range(5):
            if f % 2 == 0:
                middle = by_y([every(mid_ref, box, 4 * f, 2 + y) for y in range(4)])
                sides = jnp.where(low_y, every(mid_ref, box, 4 * f, 1), every(mid_ref, box, 4 * f, 6))
                tips = by_y([every(tip_ref, box, 4 * f, 2 + y) for y in range(4)])
            if f % 4 == 0:
                faces = by_y(
                    [every(mid_ref, box, 4 * f + y // 2, 7 * (y % 2), 2) for y in range(4)]
                )
            at = 4 * (f % 2) + xc
            inside.append(spread(middle, at))
            along_y.append(spread(sides, at))
            along_z.append(spread(tips, at))
            along_x.append(spread(faces, 2 * (f % 4) + side))
        return inside, [along_x, along_y, along_z]

    def new_parts(box):
        along_x, along_y, along_z = [], [], []
        for f in range(5):
            if f % 4 == 0:
                k = OLD + 2 * f
                faces = by_y([every(mid_ref, box, k, 2 + y) for y in range(4)])
                sides_near = jnp.where(low_y, every(mid_ref, box, k, 1), every(mid_ref, box, k, 6))
                sides_far = jnp.where(low_y, every(mid_ref, box, k, 0), every(mid_ref, box, k, 7))
                tips_near = by_y([every(tip_ref, box, k, 2 + y) for y in range(4)])
                tips_far = by_y([every(tip_ref, box, k, row) for row in (0, 1, 6, 7)])
            at = 2 * (f % 4) + half_x
            along_x.append(spread(faces, 2 * (f % 4) + side))
            along_y.append(jnp.where(outer_x, spread(sides_near, at), spread(sides_far, at)))
            along_z.append(jnp.where(outer_x, spread(tips_near, at), spread(tips_far, at)))
        return [along_x, along_y, along_z]

    directions = (
        (0, 1, sub == 0, sub == 7, 4, sub >= 4),
        (1, 16, lane < 16, lane >= 112, 64, lane >= 64),
        (1, 1, part == 0, part == 15, 8, part >= 8),
    )

    def changes(fields, step_index):
        total = None
        for normal, (axis, step, first, last, park, parked) in enumerate(directions):
            high, low, up = [[], []], [[], []], [[], []]
            for box in range(2):
                for f in range(5):
                    here, ghost = fields[box][f], ghost_ref[step_index, box, normal, f]
                    after = jnp.where(last, ghost, roll(here, -step, axis))
                    before = jnp.where(first, ghost, roll(here, step, axis))
                    one, other = edges(before, here, after)
                    high[box].append(one)
                    low[box].append(other)
                    up[box].append(jnp.where(last, ghost, roll(other, -step, axis)))
            right = [jnp.where(parked, roll(b, park, axis), a) for a, b in zip(low[0], low[1])]
            bottom = hllc([bound_ref[step_index, normal, f] for f in range(5)], right, normal)
            found = []
            for box in range(2):
                flux = hllc(high[box], up[box], normal)
                under = bottom if box == 0 else [roll(item, -park, axis) for item in bottom]
                found.append(
                    [a - jnp.where(first, b, roll(a, step, axis)) for a, b in zip(flux, under)]
                )
            total = (
                found
                if total is None
                else [[a + b for a, b in zip(t, g)] for t, g in zip(total, found)]
            )
        return total

    def keep(step_index, ghosts):
        for normal, (axis, _, _, _, park, parked) in enumerate(directions):
            for f in range(5):
                for box in range(2):
                    ghost_ref[step_index, box, normal, f] = ghosts[box][normal][f]
                bound_ref[step_index, normal, f] = jnp.where(
                    parked, roll(ghosts[1][normal][f], park, axis), ghosts[0][normal][f]
                )

    ghosts, states, later = [], [], []
    for box in range(2):
        inside, found = old_parts(box)
        ghosts.append(found)
        details = [rho_ref[box], vel_ref[0, box], vel_ref[1, box], vel_ref[2, box], p_ref[box]]
        states.append(conserved([a + b for a, b in zip(inside, details)]))
        later.append(
            [
                primitive([0.5 * (a + b) for a, b in zip(conserved(old), new)])
                for old, new in zip(found, new_parts(box))
            ]
        )
    keep(0, ghosts)
    keep(1, later)

    def stage(i, carry):
        start, state = carry
        again = lax.rem(i, 2) == 1
        weight = jnp.where(again, 0.5, 1.0).astype(F32)
        start = jax.tree.map(lambda a, b: jnp.where(again, a, b), start, state)
        moved = changes([primitive(item) for item in state], i // 2)
        state = jax.tree.map(
            lambda s, t, m: (1.0 - weight) * s + weight * (t - 0.05 * m), start, state, moved
        )
        return start, state

    _, states = lax.fori_loop(0, 4, stage, (states, states), unroll=4)
    means = []
    for box in range(2):
        packed = None
        for f in range(5):
            value = states[box][f]
            out_ref[f, box] = value
            value = value + roll(value, -1, 0)
            value = value + roll(value, -1, 1)
            value = (value + roll(value, -16, 1)) * 0.125
            inside_lane = lane % 32
            at = (inside_lane // 8) * 32 + (inside_lane % 8) * 2
            value = jnp.take_along_axis(value, at, axis=1)
            if f == 0:
                packed = value
            elif f < 4:
                packed = jnp.where(lane // 32 == f, value, packed)
            else:
                packed = jnp.where((sub % 2 == 1) & (lane < 32), roll(value, 1, 0), packed)
        means.append(packed)
    for parent in range(16):
        message_ref[parent] = jnp.where(owned_ref[0] == parent, means[0], means[1])


def final_kernel(spots_ref, new_ref, got_ref, out_ref, sum_ref):
    lane = iota(1)

    def add(turn, carry):
        count, sums = carry
        for k_owner in range(ADDS):
            owner = ADDS * turn + k_owner
            shift = spots_ref[owner]
            count = count + jnp.where((lane >= shift) & (lane < shift + 8), 1.0, 0.0)
            away = (lane + (256 - shift)) & 127
            value = jnp.take_along_axis(got_ref[owner], away, axis=1)
            group = jnp.where(shift < 256, away >> 3, 16)
            sums = [item + jnp.where(group == k, value, 0.0) for k, item in enumerate(sums)]
        return count, sums

    zero = jnp.zeros((8, 128), F32)
    count, sums = lax.fori_loop(0, 16 // ADDS, add, (zero, [zero] * 16))
    share = inverse(jnp.maximum(count, 1.0))
    for k in range(16):
        sum_ref[8 * k : 8 * k + 8] = roll(sums[k], -8 * k, 1) * share
    for f in range(5):
        for x in range(4):
            start = (0 if f == 4 else 32 * f) + 2 * x + (1 if f == 4 else 0)
            value = sum_ref[pl.ds(start, 4, stride=8)]
            out_ref[f, x] = jnp.where(count[0:4] > 0.0, value, new_ref[f, x])


FINE_SCRATCH = ((2, 352, 128), (2, 352, 128), (2, 2, 3, 5, 8, 128), (2, 3, 5, 8, 128))


def shape(*dims):
    return jax.ShapeDtypeStruct(dims, F32)


def call(kernel, outs, scalars, arrays, scratch=()):
    return pl.pallas_call(
        kernel,
        out_shape=outs,
        in_specs=[pl.BlockSpec(memory_space=pltpu.SMEM)] * scalars
        + [pl.BlockSpec(memory_space=pltpu.VMEM)] * arrays,
        out_specs=jax.tree.map(lambda _: pl.BlockSpec(memory_space=pltpu.VMEM), outs),
        scratch_shapes=[pltpu.VMEM(k, F32) if isinstance(k, tuple) else k for k in scratch],
        compiler_params=pltpu.CompilerParams(vmem_limit_bytes=32 * 1024 * 1024),
    )


def shifted(value, axis, step):
    size = lax.axis_size(axis)
    return lax.ppermute(value, axis, [(i, (i + step) % size) for i in range(size)])


def on_device(
    density, velocity, pressure, fine_density, fine_velocity, fine_pressure, box_parent, box_shift
):
    assert density.shape == (4, 4, 128) and fine_density.shape == (1, 1, 2, 8, 128)
    place = jnp.stack([lax.axis_index("gy"), lax.axis_index("gz")]).astype(jnp.int32)
    place = jnp.concatenate([place, box_parent.reshape(32), box_shift.reshape(32)])
    prim = jnp.concatenate([density[None], velocity, pressure[None]])
    ends = call(ends_kernel, shape(5, 4, 128), 0, 1)(prim)
    before, after = shifted(ends, "gz", 1), shifted(ends, "gz", -1)
    block, for_up, for_down = call(
        block_kernel, (shape(4, 25, 4, 128), shape(10, 4, 128), shape(10, 4, 128)), 0, 5
    )(place, ends, before, after, prim)
    own = lax.all_to_all(block, "gy", 0, 0, tiled=True)
    far_prior, far_next = shifted(for_up, "gx", 2), shifted(for_down, "gx", -2)
    for_up, for_down = call(near_kernel, (shape(60, 4, 128), shape(60, 4, 128)), 0, 3)(
        own, far_prior, far_next
    )
    prior, following = shifted(for_up, "gx", 1), shifted(for_down, "gx", -1)
    updated, message, owned, spots = call(
        coarse_kernel,
        (
            shape(5, 4, 4, 128),
            shape(16, 2 * TILES - 1, 4, 128),
            jax.ShapeDtypeStruct((2, 8, 128), jnp.int32),
            jax.ShapeDtypeStruct((16, 8, 128), jnp.int32),
        ),
        0,
        6,
        (
            (70, 16, 128),
            (25, 16, 128),
            (50, 16, 128),
            (15, 16, 128),
            (30, 8, 128),
            (15, 8, 128),
            (3, 20, 8, 128),
            (10, 8, 128),
            (3, 10, 8, 128),
            pltpu.SMEM((66,), jnp.int32),
            pltpu.SemaphoreType.DMA,
        ),
    )(place, own, prior, following, far_prior, far_next)
    got = lax.all_to_all(message, "gz", 0, 0, tiled=True)
    fine, means = call(
        fine_kernel,
        (shape(5, 2, 8, 128), shape(16, 8, 128)),
        0,
        5,
        FINE_SCRATCH,
    )(
        owned,
        got,
        fine_density.reshape(2, 8, 128),
        fine_velocity.reshape(3, 2, 8, 128),
        fine_pressure.reshape(2, 8, 128),
    )
    incoming = lax.all_to_all(means, "gz", 0, 0, tiled=True)
    coarse = call(final_kernel, shape(5, 4, 4, 128), 0, 3, ((128, 128),))(spots, updated, incoming)
    return coarse, fine.reshape(5, 1, 1, 2, 8, 128)


def solution(mesh):
    in_specs = (
        P("gx", "gy", "gz"),
        P(None, "gx", "gy", "gz"),
        P("gx", "gy", "gz"),
        P("gx", "gy", "gz", None, None),
        P(None, "gx", "gy", "gz", None, None),
        P("gx", "gy", "gz", None, None),
        P("gx", "gy", None, None),
        P("gx", "gy", None),
    )
    out_specs = (P(None, "gx", "gy", "gz"), P(None, "gx", "gy", "gz", None, None))
    return jax.shard_map(
        on_device, mesh=mesh, in_specs=in_specs, out_specs=out_specs, check_vma=False
    )
```
